512 devices in a mesh: gx: 32 (over y, z_lo, core), gy: 16 (over z_hi, x).
Axes of the slice: x: 4, y: 8, z: 8 (z_hi: 4, z_lo: 2; z = z_hi * 2 + z_lo), core: 2. Of those that a mesh axis runs over, the one named last changes fastest.
Arguments:
- density: float32 [128, 256, 256], P('gx', 'gy'), may hold values from 0.05 to 1
- modes: bfloat16 [12, 128, 256, 256], P(None, 'gx', 'gy'), may hold values from -12 to 12
Outputs:
- sensitivity: float32 [4, 128, 256, 256], P(None, 'gx', 'gy')
The draws below stay inside these ranges and needn't reach their ends.
All inputs are finite; a program needn't handle non-finite values.
Results may differ from the reference program's by a relative error of at most 0.0014.
Values may be sent and summed in bfloat16 or wider, within the bound.
A program may use at most 64 MiB of HBM per device.

```python
import jax
import jax.numpy as jnp
import numpy as np
from jax import lax

NZ = 256
MODES = 4
RADIUS = 3
NX = 128
NY = 256
ELEMENTS = 8388608


def draw_modes(key, part):
    key = jax.random.fold_in(key, 7)
    first_key = jax.random.fold_in(key, 0)
    shape = (3 * MODES, NX, NY, NZ)
    ramp = 1.0 + 0.75 * jnp.arange(NX, dtype=jnp.float32) / NX
    values = jnp.clip(jax.random.normal(first_key, shape, jnp.float32), -4.0, 4.0)
    return (values * ramp[None, :, None, None]).astype(jnp.bfloat16)


def level_of(own_key, dims, cuts, smallest, high):
    gain = 1.0
    for dim, blocks in cuts:
        steps = jax.random.uniform(jax.random.fold_in(jax.random.fold_in(own_key, 6), dim), (blocks,), jnp.float32, smallest / len(cuts), high / len(cuts))
        gain = gain * jnp.repeat(jnp.exp(steps), dims[dim] // blocks).reshape((-1,) + (1,) * (len(dims) - 1 - dim))
    return gain


def setup_inputs(seed: int = 0) -> dict:
    seeds = jax.random.split(jax.random.key(seed), 3)
    return {
        "density": jnp.clip(0.05 + 0.95 * jax.random.uniform(seeds[0], (NX, NY, NZ), jnp.float32) ** level_of(seeds[0], (NX, NY, NZ), ((0, 32), (1, 16)), -0.2, 0.2), 0.05, 1.0),
        "modes": draw_modes(jax.random.fold_in(seeds[2], 71), 0),
    }


BETA_SHARP = 16.0
ETA_MID = 0.5
YOUNG_MIN = 0.001
PENALTY = 3.0

def element_tables():
    gauss_point = 1.0 / np.sqrt(3.0)
    poisson = 0.3
    lame_first = poisson / ((1.0 + poisson) * (1.0 - 2.0 * poisson))
    lame_shear = 1.0 / (2.0 * (1.0 + poisson))
    elastic = np.zeros((6, 6))
    elastic[:3, :3] = lame_first
    for i in range(3):
        elastic[i, i] += 2.0 * lame_shear
        elastic[3 + i, 3 + i] = lame_shear
    stiffness = np.zeros((24, 24))
    mass_table = np.zeros((24, 24))
    corners = []
    for a in (0, 1):
        for b in (0, 1):
            for d in (0, 1):
                corners.append((2.0 * a - 1.0, 2.0 * b - 1.0, 2.0 * d - 1.0))
    for xi in (-gauss_point, gauss_point):
        for eta in (-gauss_point, gauss_point):
            for zeta in (-gauss_point, gauss_point):
                strain = np.zeros((6, 24))
                shape_rows = np.zeros((3, 24))
                for q in range(8):
                    cx, cy, cz = corners[q]
                    value = (1 + cx * xi) * (1 + cy * eta) * (1 + cz * zeta) / 8.0
                    grad_x = 2.0 * cx * (1 + cy * eta) * (1 + cz * zeta) / 8.0
                    grad_y = 2.0 * cy * (1 + cx * xi) * (1 + cz * zeta) / 8.0
                    grad_z = 2.0 * cz * (1 + cx * xi) * (1 + cy * eta) / 8.0
                    strain[0, 3 * q] = grad_x
                    strain[1, 3 * q + 1] = grad_y
                    strain[2, 3 * q + 2] = grad_z
                    strain[3, 3 * q] = grad_y
                    strain[3, 3 * q + 1] = grad_x
                    strain[4, 3 * q + 1] = grad_z
                    strain[4, 3 * q + 2] = grad_y
                    strain[5, 3 * q] = grad_z
                    strain[5, 3 * q + 2] = grad_x
                    for c in range(3):
                        shape_rows[c, 3 * q + c] = value
                stiffness += strain.T @ elastic @ strain / 8.0
                mass_table += shape_rows.T @ shape_rows / 8.0
    return (stiffness.astype(np.float32), mass_table.astype(np.float32))

def filter_taps(radius):
    reach = radius - 1
    tap_list = []
    for a in range(-reach, reach + 1):
        for b in range(-reach, reach + 1):
            for c in range(-reach, reach + 1):
                weight = radius - float(np.sqrt(a * a + b * b + c * c))
                if weight > 0:
                    tap_list.append((a, b, c, weight))
    return tap_list

def cone_sum(padded, tap_list, reach, size_x, size_y, size_z):
    total = jnp.zeros(padded.shape[:-3] + (size_x, size_y, size_z), jnp.float32)
    for a, b, c, weight in tap_list:
        total = total + weight * padded[..., reach + a:reach + a + size_x, reach + b:reach + b + size_y, reach + c:reach + c + size_z]
    return total

def element_forms(node_slab, stiffness, mass_table, size_y, size_z):
    pieces = []
    for a in (0, 1):
        for b in (0, 1):
            for d in (0, 1):
                pieces.append(node_slab[:, a, b:b + size_y, d:d + size_z])
    stacked = jnp.stack(pieces, 0)
    count = node_slab.shape[0] // 3
    vectors = stacked.reshape(8, count, 3, size_y * size_z).transpose(1, 0, 2, 3).reshape(count, 24, size_y * size_z)
    stiff_vec = jnp.einsum('pq,mqe->mpe', stiffness, vectors, precision=lax.Precision.HIGHEST)
    mass_vec = jnp.einsum('pq,mqe->mpe', mass_table, vectors, precision=lax.Precision.HIGHEST)
    return jnp.stack([lax.optimization_barrier(jnp.sum(vectors * stiff_vec, axis=1)), lax.optimization_barrier(jnp.sum(vectors * mass_vec, axis=1))], 0)

def reference(density, modes):
    reach = RADIUS - 1
    tap_list = filter_taps(RADIUS)
    stiff_np, mass_np = element_tables()
    stiffness = jnp.asarray(stiff_np, jnp.float32)
    mass_table = jnp.asarray(mass_np, jnp.float32)
    widths = ((reach, reach), (reach, reach), (reach, reach))
    inside = jnp.pad(jnp.ones((NX, NY, NZ), jnp.float32), widths)
    weight_sum = cone_sum(inside, tap_list, reach, NX, NY, NZ)
    filtered = cone_sum(jnp.pad(density, widths), tap_list, reach, NX, NY, NZ) / weight_sum
    denom = jnp.tanh(BETA_SHARP * ETA_MID) + jnp.tanh(BETA_SHARP * (1.0 - ETA_MID))
    sharp = jnp.tanh(BETA_SHARP * (filtered - ETA_MID))
    projected = (jnp.tanh(BETA_SHARP * ETA_MID) + sharp) / denom
    slope = BETA_SHARP * (1.0 - sharp * sharp) / denom
    young = YOUNG_MIN + projected ** PENALTY * (1.0 - YOUNG_MIN)
    young_slope = PENALTY * projected ** 2 * (1.0 - YOUNG_MIN)
    extended = jnp.pad(modes, ((0, 0), (0, 1), (0, 1), (0, 1)))
    count = modes.shape[0] // 3

    def row_forms(index):
        node_slab = lax.dynamic_slice_in_dim(extended, index, 2, 1).astype(jnp.float32)
        return element_forms(node_slab, stiffness, mass_table, NY, NZ)
    forms = lax.map(row_forms, jnp.arange(NX, dtype=jnp.int32))
    forms = forms.reshape(NX, 2, count, NY, NZ).transpose(1, 2, 0, 3, 4)
    stiff_form, mass_form = (forms[0], forms[1])
    stiff_norm = lax.optimization_barrier(jnp.sum(young * stiff_form, axis=(1, 2, 3)))
    mass_norm = lax.optimization_barrier(jnp.sum(projected * mass_form, axis=(1, 2, 3)))
    eigen_value = stiff_norm / mass_norm
    gradient = ELEMENTS * slope * (young_slope * stiff_form - eigen_value[:, None, None, None] * mass_form) / mass_norm[:, None, None, None]
    scaled = gradient / weight_sum
    padded = jnp.pad(scaled, ((0, 0),) + widths)
    return cone_sum(padded, tap_list, reach, NX, NY, NZ)
```

```python
import functools
import math

import jax
import jax.numpy as jnp
import numpy as np
from jax import lax
from jax.experimental import pallas as pl
from jax.experimental.pallas import tpu as pltpu
from jax.sharding import PartitionSpec as P

RADIUS = 3
BETA_SHARP = 16.0
ETA_MID = 0.5
YOUNG_MIN = 0.001
POISSON = 0.3
MESH = pl.DeviceIdType.MESH

NX, NY = 32, 16
X, Y, Z = 4, 16, 256
L = 128
MODES = 4
CH = 3 * MODES
ZROWS = 24
F32 = jnp.float32
BF16 = jnp.bfloat16

NEIGHBOURS = [(a, b) for a in (-1, 0, 1) for b in (-1, 0, 1) if (a, b) != (0, 0)]


def weight(n):
    return max(0.0, RADIUS - math.sqrt(n))


def position():
    gx, gy = lax.axis_index("gx"), lax.axis_index("gy")
    return gx, gy


def neighbour(gx, gy, a, b):
    return (lax.rem(gx + a + NX, NX), lax.rem(gy + b + NY, NY))


def far_first(offsets, sizes):
    hops = lambda o: sum(min(v, n - v) for v, n in zip(o, sizes))
    return sorted((o for o in offsets if any(o)), key=lambda o: -hops(o))


GROUP_A = far_first([(i, j) for i in range(8) for j in range(4)], (8, 4))
GROUP_B = far_first([(i, j) for i in range(4) for j in range(4)], (4, 4))


def member_a(gx, gy, o):
    i, low = gx // 4, lax.rem(gx, 4)
    high, j = gy // 4, lax.rem(gy, 4)
    return (lax.rem(i + o[0], 8) * 4 + low, high * 4 + lax.rem(j + o[1], 4))


def member_b(gx, gy, o):
    i, low = gx // 4, lax.rem(gx, 4)
    high, j = gy // 4, lax.rem(gy, 4)
    return (i * 4 + lax.rem(low + o[0], 4), lax.rem(high + o[1], 4) * 4 + j)


def fold_depth(g0, g1, g2, lane):
    lo, hi = g0
    for k, (p, q) in ((1, g1), (2, g2)):
        p_up, q_up = pltpu.roll(p, k, 1), pltpu.roll(q, k, 1)
        p_dn, q_dn = pltpu.roll(p, L - k, 1), pltpu.roll(q, L - k, 1)
        first, last = lane < k, lane >= L - k
        lo = lo + (jnp.where(first, 0.0, p_up) + jnp.where(last, q_dn, p_dn))
        hi = hi + (jnp.where(first, p_up, q_up) + jnp.where(last, 0.0, q_dn))
    return lo, hi


def plane_sums(f, x1, x2):
    s0 = f[2]
    s1 = x1[2] + (f[1] + f[3])
    s2 = x1[1] + x1[3]
    s4 = x2[2] + (f[0] + f[4])
    s5 = (x1[0] + x1[4]) + (x2[1] + x2[3])
    s8 = x2[0] + x2[4]
    sums = ((0, s0), (1, s1), (2, s2), (4, s4), (5, s5), (8, s8))
    out = []
    for c in (0, 1, 4):
        total = None
        for n, s in sums:
            w = weight(n + c)
            if w > 0:
                total = w * s if total is None else total + w * s
        out.append(total)
    return out


def filter_density(ext, x, g, lane):
    planes = []
    for h in (0, 1):
        rows = lambda a, b: ext[h, x + 2 + a, 8 + 8 * g + b : 16 + 8 * g + b, :]
        f = [rows(0, b) for b in range(-2, 3)]
        x1 = [rows(-1, b) + rows(1, b) for b in range(-2, 3)]
        x2 = [rows(-2, b) + rows(2, b) for b in range(-2, 3)]
        planes.append(plane_sums(f, x1, x2))
    g0, g1, g2 = zip(*planes)
    return fold_depth(g0, g1, g2, lane)


def energies(t):
    lame = POISSON / ((1.0 + POISSON) * (1.0 - 2.0 * POISSON))
    shear = 1.0 / (2.0 * (1.0 + POISSON))
    sq = lambda v: v * v
    u, v, w = t
    total = lambda terms: functools.reduce(lambda p, q: p + q, terms)
    rigid = total([sq(c[0][0][0]) for c in t])
    diag = sq(u[1][0][0]) + sq(v[0][1][0]) + sq(w[0][0][1])
    first = total([sq(u[0][1][0]), sq(u[0][0][1]), sq(v[1][0][0]), sq(v[0][0][1]), sq(w[1][0][0]), sq(w[0][1][0])])
    second = total([sq(u[1][1][0]), sq(u[1][0][1]), sq(v[1][1][0]), sq(v[0][1][1]), sq(w[1][0][1]), sq(w[0][1][1])])
    other = total([sq(u[0][1][1]), sq(v[1][0][1]), sq(w[1][1][0])])
    third = total([sq(c[1][1][1]) for c in t])
    mass = rigid * (1 / 64) + (diag + first) * (1 / 192) + (second + other) * (1 / 576) + third * (1 / 1728)
    div = sq(u[1][0][0] + v[0][1][0] + w[0][0][1])
    div1 = total([sq(v[1][1][0] + w[1][0][1]), sq(u[1][1][0] + w[0][1][1]), sq(u[1][0][1] + v[0][1][1])])
    slide = total([sq(u[0][1][0] + v[1][0][0]), sq(u[0][0][1] + w[1][0][0]), sq(v[0][0][1] + w[0][1][0])])
    slide1 = total([sq(u[0][1][1] + v[1][0][1]), sq(u[0][1][1] + w[1][1][0]), sq(v[1][0][1] + w[1][1][0])])
    stiff = (
        (lame / 16) * div
        + (lame / 48) * div1
        + (shear / 8) * diag
        + (shear / 16) * slide
        + (shear / 48) * slide1
        + (shear / 16) * second
        + ((lame + 4 * shear) / 144) * third
    )
    return stiff, mass


def across(low, high):
    return [
        [
            [[low[c][j][k] + high[c][j][k] for k in (0, 1)] for j in (0, 1)],
            [[high[c][j][k] - low[c][j][k] for k in (0, 1)] for j in (0, 1)],
        ]
        for c in range(3)
    ]


def layer_of(zs, m, h, x, g):
    out = []
    for c in range(3):
        both = []
        for k in (0, 1):
            at = x * ZROWS + 8 * g
            here = zs[3 * m + c, 2 * k + h, at : at + 8, :]
            there = zs[3 * m + c, 2 * k + h, at + 1 : at + 9, :]
            both.append((here + there, there - here))
        out.append([[both[k][j] for k in (0, 1)] for j in (0, 1)])
    return out


def last_row_of(zs, yz, m, h, x):
    out = []
    for c in range(3):
        both = []
        for k in (0, 1):
            here = zs[3 * m + c, 2 * k + h, pl.ds(x * ZROWS + Y - 1, 8, stride=ZROWS), :]
            there = yz[2 * k + h, pl.ds(x * 16 + 3 * m + c, 8, stride=16), :]
            both.append((here + there, there - here))
        out.append([[both[k][j] for k in (0, 1)] for j in (0, 1)])
    return out


def kernel(
    dens_ref,
    modes_ref,
    out_ref,
    dext,
    wext,
    nodes,
    row0,
    first_row,
    next_row,
    zmat,
    zs,
    yz,
    forms,
    coef,
    ext,
    cone,
    slots_a,
    slots_b,
    in_sem,
    halo_send,
    halo_recv,
    field_send,
    field_recv,
    sum_send,
    sum_recv,
):
    gx, gy = position()
    lane = lax.broadcasted_iota(jnp.int32, (8, L), 1)

    loads = [
        pltpu.make_async_copy(dens_ref.at[:, :, L * h : L * (h + 1)], dext.at[h, 2:6, 8:24, :], in_sem.at[h])
        for h in (0, 1)
    ] + [pltpu.make_async_copy(modes_ref.at[:, x], nodes.at[x], in_sem.at[2 + x]) for x in range(X)]
    for load in loads:
        load.start()

    barrier = pltpu.get_barrier_semaphore()
    for a, b in NEIGHBOURS:
        pl.semaphore_signal(barrier, inc=1, device_id=neighbour(gx, gy, a, b), device_id_type=MESH)
    for o in GROUP_B:
        pl.semaphore_signal(barrier, inc=1, device_id=member_b(gx, gy, o), device_id_type=MESH)
    for o in GROUP_A:
        pl.semaphore_signal(barrier, inc=1, device_id=member_a(gx, gy, o), device_id_type=MESH)

    for load in loads:
        load.wait()

    def pack(c, _):
        for x in range(X):
            row0[pl.ds(x * 16 + c, 1), :] = nodes[x, c].astype(F32)[0:1, :]
        return 0

    lax.fori_loop(0, CH, pack, 0)
    first_row[...] = row0[...].astype(BF16)

    pl.semaphore_wait(barrier, len(NEIGHBOURS) + len(GROUP_A) + len(GROUP_B))

    def remote(src, dst, send, recv, a, b):
        return pltpu.make_async_remote_copy(
            src_ref=src,
            dst_ref=dst,
            send_sem=send,
            recv_sem=recv,
            device_id=neighbour(gx, gy, a, b),
            device_id_type=MESH,
        )

    src_x, dst_x = {-1: (2, 2), 0: (2, 4), 1: (4, 2)}, {-1: 6, 0: 2, 1: 0}
    halos = []
    far = sorted(NEIGHBOURS, key=lambda o: -abs(o[0]) - abs(o[1]))
    halos.append(remote(first_row.at[0:16], next_row.at[64:80], halo_send.at[8], halo_recv.at[8], -1, -1))
    for i, (a, b) in enumerate(far):
        x0, xn = src_x[a]
        y0, yn = {-1: (8, 8), 0: (8, 16), 1: (16, 8)}[b]
        y1 = {-1: 24, 0: 8, 1: 0}[b]
        halos.append(
            remote(
                dext.at[:, x0 : x0 + xn, y0 : y0 + yn, :],
                dext.at[:, dst_x[a] : dst_x[a] + xn, y1 : y1 + yn, :],
                halo_send.at[i],
                halo_recv.at[i],
                a,
                b,
            )
        )
    halos.append(remote(first_row, next_row.at[0:64], halo_send.at[9], halo_recv.at[9], 0, -1))
    halos.append(remote(nodes.at[0], nodes.at[4], halo_send.at[10], halo_recv.at[10], -1, 0))
    for halo in halos:
        halo.start()

    for h in (0, 1):
        for x in range(X + 4):
            ix = gx * X + (x - 2)
            inside_x = jnp.where((ix >= 0) & (ix < NX * X), 1.0, 0.0)
            iy = gy * Y - 8 + lax.broadcasted_iota(jnp.int32, (32, L), 0)
            wext[h, x] = jnp.where((iy >= 0) & (iy < NY * Y), inside_x, 0.0)

    def weights(x, _):
        for g in (0, 1):
            at = pl.ds(pl.multiple_of(x * Y + 8 * g, 8), 8)
            for h, s in enumerate(filter_density(wext, x, g, lane)):
                coef[0, h, at, :] = 1.0 / s
        return 0

    lax.fori_loop(0, X, weights, 0)

    row = lax.broadcasted_iota(jnp.int32, (Z, Z), 0)
    col = lax.broadcasted_iota(jnp.int32, (Z, Z), 1)
    here = jnp.where(row == col, 1.0, 0.0)
    there = jnp.where(row == col + 1, 1.0, 0.0)
    zmat[:, 0:Z] = (here + there).astype(BF16)
    zmat[:, Z : 2 * Z] = (there - here).astype(BF16)

    def depth(x, _):
        t = jnp.dot(nodes[x].reshape(CH * Y, Z), zmat[...], preferred_element_type=F32)
        at = pl.ds(pl.multiple_of(x * ZROWS, 8), Y)
        for c in range(CH):
            for q in range(4):
                zs[c, q, at, :] = t[c * Y : (c + 1) * Y, q * L : (q + 1) * L]
        return 0

    lax.fori_loop(0, X, depth, 0)

    def elements(x0, x1):
        def body(i, _):
            m, h = i // 2, lax.rem(i, 2)
            for g in (0, 1):
                low = layer_of(zs, m, h, x0, g)
                for x in range(x0, x1):
                    high = layer_of(zs, m, h, x + 1, g)
                    kq, mq = energies(across(low, high))
                    at = slice(x * Y + 8 * g, x * Y + 8 * g + 8)
                    forms[m, h, at, :] = kq
                    forms[MODES + m, h, at, :] = mq
                    low = high
            return 0

        lax.fori_loop(0, 2 * MODES, body, 0)

    elements(0, X - 1)

    for halo in halos:
        halo.wait_recv()

    @pl.when(gx == NX - 1)
    def _():
        nodes[4] = jnp.zeros((CH, Y, Z), BF16)
        next_row[64:80, :] = jnp.zeros((16, Z), BF16)
        dext[:, 6:8] = jnp.zeros((2, 2, 32, L), F32)

    @pl.when(gx == 0)
    def _():
        dext[:, 0:2] = jnp.zeros((2, 2, 32, L), F32)

    @pl.when(gy == NY - 1)
    def _():
        next_row[...] = jnp.zeros((80, Z), BF16)
        dext[:, :, 24:32] = jnp.zeros((2, 8, 8, L), F32)

    @pl.when(gy == 0)
    def _():
        dext[:, :, 0:8] = jnp.zeros((2, 8, 8, L), F32)

    depth(X, 0)
    t = jnp.dot(next_row[...], zmat[...], preferred_element_type=F32)
    for q in range(4):
        yz[q, 0:80, :] = t[:, q * L : (q + 1) * L]

    elements(X - 1, X)

    def last_row(i, _):
        m, h = i // 2, lax.rem(i, 2)
        kq, mq = energies(across(last_row_of(zs, yz, m, h, 0), last_row_of(zs, yz, m, h, 1)))
        forms[m, h, pl.ds(Y - 1, X, stride=Y), :] = kq[0:X]
        forms[MODES + m, h, pl.ds(Y - 1, X, stride=Y), :] = mq[0:X]
        return 0

    lax.fori_loop(0, 2 * MODES, last_row, 0)

    top = math.tanh(BETA_SHARP * ETA_MID)
    denom = top + math.tanh(BETA_SHARP * (1.0 - ETA_MID))

    def project(x, _):
        for g in (0, 1):
            at = pl.ds(pl.multiple_of(x * Y + 8 * g, 8), 8)
            for h, s in enumerate(filter_density(dext, x, g, lane)):
                share = coef[0, h, at, :]
                sharp = jnp.tanh(BETA_SHARP * (s * share - ETA_MID))
                projected = (top + sharp) * (1.0 / denom)
                slope = (BETA_SHARP / denom) * (1.0 - sharp * sharp) * share
                square = projected * projected
                coef[1, h, at, :] = YOUNG_MIN + square * projected * (1.0 - YOUNG_MIN)
                coef[2, h, at, :] = projected
                coef[3, h, at, :] = slope * (square * (3.0 * (1.0 - YOUNG_MIN)))
                coef[4, h, at, :] = slope
        return 0

    lax.fori_loop(0, X, project, 0)

    def scale(i, sums):
        h, x = i // X, lax.rem(i, X)
        sums = list(sums)
        for g in (0, 1):
            at = pl.ds(pl.multiple_of(x * Y + 8 * g, 8), 8)
            young, projected, a, b = (coef[n, h, at, :] for n in range(1, 5))
            for f in range(2 * MODES):
                q = forms[f, h, at, :]
                sums[f] = sums[f] + q * (young if f < MODES else projected)
                ext[h, x + 2, pl.ds((2 + 8 * g) * 8 + f, 8, stride=8), :] = q * (a if f < MODES else b)
        return tuple(sums)

    sums = lax.fori_loop(0, 2 * X, scale, tuple(jnp.zeros((8, L), F32) for _ in range(2 * MODES)))

    part = jnp.concatenate([jnp.sum(s, axis=0, keepdims=True) for s in sums], axis=0)
    for k in (64, 32, 16):
        part = part + pltpu.roll(part, k, 1)
    own = lane // 16 == lax.broadcasted_iota(jnp.int32, (8, L), 0)
    part = jnp.sum(jnp.where(own, part, 0.0), axis=0, keepdims=True)

    def group(slots, offsets, member, n, value):
        slots[0] = value
        for k, o in enumerate(offsets):
            pltpu.make_async_remote_copy(
                src_ref=slots.at[0],
                dst_ref=slots.at[k + 1],
                send_sem=sum_send.at[n],
                recv_sem=sum_recv.at[n],
                device_id=member(gx, gy, o),
                device_id_type=MESH,
            ).start()

    def group_wait(slots, sem):
        others = slots.at[pl.ds(1, slots.shape[0] - 1)]
        pltpu.make_async_copy(others, others, sem).wait()

    def group_sum(slots, n):
        group_wait(slots, sum_recv.at[n])
        return jnp.sum(slots[...], axis=0)

    group(slots_a, GROUP_A, member_a, 0, part)

    fields = []
    for i, (a, b) in enumerate(far):
        x0, xn = src_x[a]
        y0, yn = {-1: (2, 2), 0: (2, 16), 1: (16, 2)}[b]
        y1 = {-1: 18, 0: 2, 1: 0}[b]
        fields.append(
            remote(
                ext.at[:, x0 : x0 + xn, 8 * y0 : 8 * (y0 + yn), :],
                ext.at[:, dst_x[a] : dst_x[a] + xn, 8 * y1 : 8 * (y1 + yn), :],
                field_send.at[i],
                field_recv.at[i],
                a,
                b,
            )
        )
    for field in fields:
        field.start()

    group(slots_b, GROUP_B, member_b, 1, group_sum(slots_a, 0))

    for field in fields:
        field.wait_recv()

    @pl.when(gx == NX - 1)
    def _():
        ext[:, 6:8] = jnp.zeros((2, 2, 160, L), F32)

    @pl.when(gx == 0)
    def _():
        ext[:, 0:2] = jnp.zeros((2, 2, 160, L), F32)

    @pl.when(gy == NY - 1)
    def _():
        ext[:, :, 144:160] = jnp.zeros((2, 8, 16, L), F32)

    @pl.when(gy == 0)
    def _():
        ext[:, :, 0:16] = jnp.zeros((2, 8, 16, L), F32)

    def filter_fields(x, _):
        f, x1, x2 = [[], []], [[], []], [[], []]
        for y in range(Y + 4):
            for h in (0, 1):
                at = lambda a: ext[h, x + 2 + a, 8 * y : 8 * y + 8, :]
                f[h].append(at(0))
                x1[h].append(at(-1) + at(1))
                x2[h].append(at(-2) + at(2))
        for y in range(Y):
            planes = [plane_sums(f[h][y : y + 5], x1[h][y : y + 5], x2[h][y : y + 5]) for h in (0, 1)]
            g0, g1, g2 = zip(*planes)
            for h, s in enumerate(fold_depth(g0, g1, g2, lane)):
                cone[h, x, 8 * y : 8 * y + 8, :] = s
        return 0

    lax.fori_loop(0, X, filter_fields, 0)

    total = jnp.broadcast_to(group_sum(slots_b, 1), (8, L))
    total = jnp.sum(jnp.where(own, total, 0.0), axis=1, keepdims=True)
    elements_total = float(NX * X * NY * Y * Z)
    first, second = [], []
    for m in range(MODES):
        stiff_norm = jnp.broadcast_to(total[m : m + 1, :], (8, L))
        mass_norm = jnp.broadcast_to(total[MODES + m : MODES + m + 1, :], (8, L))
        first.append(elements_total / mass_norm)
        second.append(first[m] * (stiff_norm / mass_norm))

    def combine(x, _):
        for m in range(MODES):
            for g in (0, 1):
                for h in (0, 1):
                    stiff = cone[h, x, pl.ds(64 * g + m, 8, stride=8), :]
                    mass = cone[h, x, pl.ds(64 * g + MODES + m, 8, stride=8), :]
                    out_ref[m, x, 8 * g : 8 * g + 8, L * h : L * (h + 1)] = first[m] * stiff - second[m] * mass
        return 0

    lax.fori_loop(0, X, combine, 0)

    for copy in halos + fields:
        copy.wait_send()
    group_wait(slots_a, sum_send.at[0])
    group_wait(slots_b, sum_send.at[1])


def local(density, modes):
    return pl.pallas_call(
        kernel,
        out_shape=jax.ShapeDtypeStruct((MODES, X, Y, Z), F32),
        in_specs=[pl.BlockSpec(memory_space=pl.ANY)] * 2,
        out_specs=pl.BlockSpec(memory_space=pltpu.VMEM),
        scratch_shapes=[
            pltpu.VMEM((2, X + 4, 32, L), F32),
            pltpu.VMEM((2, X + 4, 32, L), F32),
            pltpu.VMEM((X + 1, CH, Y, Z), BF16),
            pltpu.VMEM((16 * X, Z), F32),
            pltpu.VMEM((16 * X, Z), BF16),
            pltpu.VMEM((16 * (X + 1), Z), BF16),
            pltpu.VMEM((Z, 2 * Z), BF16),
            pltpu.VMEM((CH, 4, 9 * ZROWS, L), F32),
            pltpu.VMEM((4, 9 * 16, L), F32),
            pltpu.VMEM((2 * MODES, 2, X * Y, L), F32),
            pltpu.VMEM((5, 2, X * Y, L), F32),
            pltpu.VMEM((2, X + 4, 8 * (Y + 4), L), F32),
            pltpu.VMEM((2, X, 8 * Y, L), F32),
            pltpu.VMEM((len(GROUP_A) + 1, 1, L), F32),
            pltpu.VMEM((len(GROUP_B) + 1, 1, L), F32),
            pltpu.SemaphoreType.DMA((2 + X,)),
            pltpu.SemaphoreType.DMA((11,)),
            pltpu.SemaphoreType.DMA((11,)),
            pltpu.SemaphoreType.DMA((8,)),
            pltpu.SemaphoreType.DMA((8,)),
            pltpu.SemaphoreType.DMA((2,)),
            pltpu.SemaphoreType.DMA((2,)),
        ],
        compiler_params=pltpu.CompilerParams(
            collective_id=0, has_side_effects=True, vmem_limit_bytes=40 * 1024 * 1024
        ),
    )(density, modes)


def solution(mesh):
    return jax.shard_map(
        local,
        mesh=mesh,
        in_specs=(P("gx", "gy", None), P(None, "gx", "gy", None)),
        out_specs=P(None, "gx", "gy", None),
        check_vma=False,
    )
```

```python
import functools
import math

import jax
import jax.numpy as jnp
import numpy as np
from jax import lax
from jax.experimental import pallas as pl
from jax.experimental.pallas import tpu as pltpu
from jax.sharding import PartitionSpec as P

RADIUS = 3
BETA_SHARP = 16.0
ETA_MID = 0.5
YOUNG_MIN = 0.001
POISSON = 0.3
MESH = pl.DeviceIdType.MESH

NX, NY = 32, 16
X, Y, Z = 4, 16, 256
L = 128
MODES = 4
CH = 3 * MODES
ZROWS = 24
F32 = jnp.float32
BF16 = jnp.bfloat16

NEIGHBOURS = [(a, b) for a in (-1, 0, 1) for b in (-1, 0, 1) if (a, b) != (0, 0)]


def weight(n):
    return max(0.0, RADIUS - math.sqrt(n))


def position():
    gx, gy = lax.axis_index("gx"), lax.axis_index("gy")
    return gx, gy


def neighbour(gx, gy, a, b):
    return (lax.rem(gx + a + NX, NX), lax.rem(gy + b + NY, NY))


def far_first(offsets, sizes):
    hops = lambda o: sum(min(v, n - v) for v, n in zip(o, sizes))
    return sorted((o for o in offsets if any(o)), key=lambda o: -hops(o))


GROUP_A = far_first([(i, j) for i in range(8) for j in range(4)], (8, 4))
GROUP_B = far_first([(i, j) for i in range(4) for j in range(4)], (4, 4))


def member_a(gx, gy, o):
    i, low = gx // 4, lax.rem(gx, 4)
    high, j = gy // 4, lax.rem(gy, 4)
    return (lax.rem(i + o[0], 8) * 4 + low, high * 4 + lax.rem(j + o[1], 4))


def member_b(gx, gy, o):
    i, low = gx // 4, lax.rem(gx, 4)
    high, j = gy // 4, lax.rem(gy, 4)
    return (i * 4 + lax.rem(low + o[0], 4), lax.rem(high + o[1], 4) * 4 + j)


def fold_depth(g0, g1, g2, lane):
    lo, hi = g0
    for k, (p, q) in ((1, g1), (2, g2)):
        p_up, q_up = pltpu.roll(p, k, 1), pltpu.roll(q, k, 1)
        p_dn, q_dn = pltpu.roll(p, L - k, 1), pltpu.roll(q, L - k, 1)
        first, last = lane < k, lane >= L - k
        lo = lo + (jnp.where(first, 0.0, p_up) + jnp.where(last, q_dn, p_dn))
        hi = hi + (jnp.where(first, p_up, q_up) + jnp.where(last, 0.0, q_dn))
    return lo, hi


def plane_sums(f, x1, x2):
    s0 = f[2]
    s1 = x1[2] + (f[1] + f[3])
    s2 = x1[1] + x1[3]
    s4 = x2[2] + (f[0] + f[4])
    s5 = (x1[0] + x1[4]) + (x2[1] + x2[3])
    s8 = x2[0] + x2[4]
    sums = ((0, s0), (1, s1), (2, s2), (4, s4), (5, s5), (8, s8))
    out = []
    for c in (0, 1, 4):
        total = None
        for n, s in sums:
            w = weight(n + c)
            if w > 0:
                total = w * s if total is None else total + w * s
        out.append(total)
    return out


def filter_density(ext, x, g, lane):
    planes = []
    for h in (0, 1):
        rows = lambda a, b: ext[h, x + 2 + a, 8 + 8 * g + b : 16 + 8 * g + b, :]
        f = [rows(0, b) for b in range(-2, 3)]
        x1 = [rows(-1, b) + rows(1, b) for b in range(-2, 3)]
        x2 = [rows(-2, b) + rows(2, b) for b in range(-2, 3)]
        planes.append(plane_sums(f, x1, x2))
    g0, g1, g2 = zip(*planes)
    return fold_depth(g0, g1, g2, lane)


def energies(t):
    lame = POISSON / ((1.0 + POISSON) * (1.0 - 2.0 * POISSON))
    shear = 1.0 / (2.0 * (1.0 + POISSON))
    sq = lambda v: v * v
    u, v, w = t
    total = lambda terms: functools.reduce(lambda p, q: p + q, terms)
    rigid = total([sq(c[0][0][0]) for c in t])
    diag = sq(u[1][0][0]) + sq(v[0][1][0]) + sq(w[0][0][1])
    first = total([sq(u[0][1][0]), sq(u[0][0][1]), sq(v[1][0][0]), sq(v[0][0][1]), sq(w[1][0][0]), sq(w[0][1][0])])
    second = total([sq(u[1][1][0]), sq(u[1][0][1]), sq(v[1][1][0]), sq(v[0][1][1]), sq(w[1][0][1]), sq(w[0][1][1])])
    other = total([sq(u[0][1][1]), sq(v[1][0][1]), sq(w[1][1][0])])
    third = total([sq(c[1][1][1]) for c in t])
    mass = rigid * (1 / 64) + (diag + first) * (1 / 192) + (second + other) * (1 / 576) + third * (1 / 1728)
    div = sq(u[1][0][0] + v[0][1][0] + w[0][0][1])
    div1 = total([sq(v[1][1][0] + w[1][0][1]), sq(u[1][1][0] + w[0][1][1]), sq(u[1][0][1] + v[0][1][1])])
    slide = total([sq(u[0][1][0] + v[1][0][0]), sq(u[0][0][1] + w[1][0][0]), sq(v[0][0][1] + w[0][1][0])])
    slide1 = total([sq(u[0][1][1] + v[1][0][1]), sq(u[0][1][1] + w[1][1][0]), sq(v[1][0][1] + w[1][1][0])])
    stiff = (
        (lame / 16) * div
        + (lame / 48) * div1
        + (shear / 8) * diag
        + (shear / 16) * slide
        + (shear / 48) * slide1
        + (shear / 16) * second
        + ((lame + 4 * shear) / 144) * third
    )
    return stiff, mass


def across(low, high):
    return [
        [
            [[low[c][j][k] + high[c][j][k] for k in (0, 1)] for j in (0, 1)],
            [[high[c][j][k] - low[c][j][k] for k in (0, 1)] for j in (0, 1)],
        ]
        for c in range(3)
    ]


def layer_of(zs, m, h, x, g):
    out = []
    for c in range(3):
        both = []
        for k in (0, 1):
            at = x * ZROWS + 8 * g
            here = zs[3 * m + c, 2 * k + h, at : at + 8, :]
            there = zs[3 * m + c, 2 * k + h, at + 1 : at + 9, :]
            both.append((here + there, there - here))
        out.append([[both[k][j] for k in (0, 1)] for j in (0, 1)])
    return out


def last_row_of(zs, yz, m, h, x):
    out = []
    for c in range(3):
        both = []
        for k in (0, 1):
            here = zs[3 * m + c, 2 * k + h, pl.ds(x * ZROWS + Y - 1, 8, stride=ZROWS), :]
            there = yz[2 * k + h, pl.ds(x * 16 + 3 * m + c, 8, stride=16), :]
            both.append((here + there, there - here))
        out.append([[both[k][j] for k in (0, 1)] for j in (0, 1)])
    return out


def kernel(
    dens_ref,
    modes_ref,
    out_ref,
    dext,
    wext,
    nodes,
    row0,
    first_row,
    next_row,
    zmat,
    zs,
    yz,
    forms,
    coef,
    ext,
    sent,
    received,
    cone,
    slots_a,
    slots_b,
    in_sem,
    halo_send,
    halo_recv,
    field_send,
    field_recv,
    sum_send,
    sum_recv,
):
    gx, gy = position()
    lane = lax.broadcasted_iota(jnp.int32, (8, L), 1)

    barrier = pltpu.get_barrier_semaphore()
    for a, b in NEIGHBOURS:
        pl.semaphore_signal(barrier, inc=1, device_id=neighbour(gx, gy, a, b), device_id_type=MESH)
    loads = [
        pltpu.make_async_copy(dens_ref.at[:, :, L * h : L * (h + 1)], dext.at[h, 2:6, 8:24, :], in_sem.at[h])
        for h in (0, 1)
    ] + [pltpu.make_async_copy(modes_ref.at[:, x], nodes.at[x], in_sem.at[2 + x]) for x in range(X)]
    for load in loads:
        load.start()

    for o in GROUP_B:
        pl.semaphore_signal(barrier, inc=1, device_id=member_b(gx, gy, o), device_id_type=MESH)
    for o in GROUP_A:
        pl.semaphore_signal(barrier, inc=1, device_id=member_a(gx, gy, o), device_id_type=MESH)

    for load in loads:
        load.wait()

    def pack(c, _):
        for x in range(X):
            row0[pl.ds(x * 16 + c, 1), :] = nodes[x, c].astype(F32)[0:1, :]
        return 0

    lax.fori_loop(0, CH, pack, 0)
    first_row[...] = row0[...].astype(BF16)

    pl.semaphore_wait(barrier, len(NEIGHBOURS) + len(GROUP_A) + len(GROUP_B))

    def remote(src, dst, send, recv, a, b):
        return pltpu.make_async_remote_copy(
            src_ref=src,
            dst_ref=dst,
            send_sem=send,
            recv_sem=recv,
            device_id=neighbour(gx, gy, a, b),
            device_id_type=MESH,
        )

    src_x, dst_x = {-1: (2, 2), 0: (2, 4), 1: (4, 2)}, {-1: 6, 0: 2, 1: 0}
    halos = []
    far = sorted(NEIGHBOURS, key=lambda o: -abs(o[0]) - abs(o[1]))
    halos.append(remote(first_row.at[0:16], next_row.at[64:80], halo_send.at[8], halo_recv.at[8], -1, -1))
    for i, (a, b) in enumerate(far):
        x0, xn = src_x[a]
        y0, yn = {-1: (8, 8), 0: (8, 16), 1: (16, 8)}[b]
        y1 = {-1: 24, 0: 8, 1: 0}[b]
        halos.append(
            remote(
                dext.at[:, x0 : x0 + xn, y0 : y0 + yn, :],
                dext.at[:, dst_x[a] : dst_x[a] + xn, y1 : y1 + yn, :],
                halo_send.at[i],
                halo_recv.at[i],
                a,
                b,
            )
        )
    halos.append(remote(first_row, next_row.at[0:64], halo_send.at[9], halo_recv.at[9], 0, -1))
    halos.append(remote(nodes.at[0], nodes.at[4], halo_send.at[10], halo_recv.at[10], -1, 0))
    for halo in halos:
        halo.start()

    for h in (0, 1):
        for x in range(X + 4):
            ix = gx * X + (x - 2)
            inside_x = jnp.where((ix >= 0) & (ix < NX * X), 1.0, 0.0)
            iy = gy * Y - 8 + lax.broadcasted_iota(jnp.int32, (32, L), 0)
            wext[h, x] = jnp.where((iy >= 0) & (iy < NY * Y), inside_x, 0.0)

    def weights(x, _):
        for g in (0, 1):
            at = pl.ds(pl.multiple_of(x * Y + 8 * g, 8), 8)
            for h, s in enumerate(filter_density(wext, x, g, lane)):
                coef[0, h, at, :] = 1.0 / s
        return 0

    lax.fori_loop(0, X, weights, 0)

    row = lax.broadcasted_iota(jnp.int32, (Z, Z), 0)
    col = lax.broadcasted_iota(jnp.int32, (Z, Z), 1)
    here = jnp.where(row == col, 1.0, 0.0)
    there = jnp.where(row == col + 1, 1.0, 0.0)
    zmat[:, 0:Z] = (here + there).astype(BF16)
    zmat[:, Z : 2 * Z] = (there - here).astype(BF16)

    def depth(x, _):
        t = jnp.dot(nodes[x].reshape(CH * Y, Z), zmat[...], preferred_element_type=F32)
        at = pl.ds(pl.multiple_of(x * ZROWS, 8), Y)
        for c in range(CH):
            for q in range(4):
                zs[c, q, at, :] = t[c * Y : (c + 1) * Y, q * L : (q + 1) * L]
        return 0

    lax.fori_loop(0, X, depth, 0)

    def elements(x0, x1):
        def body(i, _):
            m, h = i // 2, lax.rem(i, 2)
            for g in (0, 1):
                low = layer_of(zs, m, h, x0, g)
                for x in range(x0, x1):
                    high = layer_of(zs, m, h, x + 1, g)
                    kq, mq = energies(across(low, high))
                    at = slice(x * Y + 8 * g, x * Y + 8 * g + 8)
                    forms[m, h, at, :] = kq
                    forms[MODES + m, h, at, :] = mq
                    low = high
            return 0

        lax.fori_loop(0, 2 * MODES, body, 0)

    elements(0, X - 1)

    for halo in halos:
        halo.wait_recv()

    @pl.when(gx == NX - 1)
    def _():
        nodes[4] = jnp.zeros((CH, Y, Z), BF16)
        next_row[64:80, :] = jnp.zeros((16, Z), BF16)
        dext[:, 6:8] = jnp.zeros((2, 2, 32, L), F32)

    @pl.when(gx == 0)
    def _():
        dext[:, 0:2] = jnp.zeros((2, 2, 32, L), F32)

    @pl.when(gy == NY - 1)
    def _():
        next_row[...] = jnp.zeros((80, Z), BF16)
        dext[:, :, 24:32] = jnp.zeros((2, 8, 8, L), F32)

    @pl.when(gy == 0)
    def _():
        dext[:, :, 0:8] = jnp.zeros((2, 8, 8, L), F32)

    depth(X, 0)
    t = jnp.dot(next_row[...], zmat[...], preferred_element_type=F32)
    for q in range(4):
        yz[q, 0:80, :] = t[:, q * L : (q + 1) * L]

    elements(X - 1, X)

    def last_row(i, _):
        m, h = i // 2, lax.rem(i, 2)
        kq, mq = energies(across(last_row_of(zs, yz, m, h, 0), last_row_of(zs, yz, m, h, 1)))
        forms[m, h, pl.ds(Y - 1, X, stride=Y), :] = kq[0:X]
        forms[MODES + m, h, pl.ds(Y - 1, X, stride=Y), :] = mq[0:X]
        return 0

    lax.fori_loop(0, 2 * MODES, last_row, 0)

    top = math.tanh(BETA_SHARP * ETA_MID)
    denom = top + math.tanh(BETA_SHARP * (1.0 - ETA_MID))

    def project(x, _):
        for g in (0, 1):
            at = pl.ds(pl.multiple_of(x * Y + 8 * g, 8), 8)
            for h, s in enumerate(filter_density(dext, x, g, lane)):
                share = coef[0, h, at, :]
                sharp = jnp.tanh(BETA_SHARP * (s * share - ETA_MID))
                projected = (top + sharp) * (1.0 / denom)
                slope = (BETA_SHARP / denom) * (1.0 - sharp * sharp) * share
                square = projected * projected
                coef[1, h, at, :] = YOUNG_MIN + square * projected * (1.0 - YOUNG_MIN)
                coef[2, h, at, :] = projected
                coef[3, h, at, :] = slope * (square * (3.0 * (1.0 - YOUNG_MIN)))
                coef[4, h, at, :] = slope
        return 0

    lax.fori_loop(0, X, project, 0)

    def scale(i, sums):
        h, x = i // X, lax.rem(i, X)
        sums = list(sums)
        for g in (0, 1):
            at = pl.ds(pl.multiple_of(x * Y + 8 * g, 8), 8)
            young, projected, a, b = (coef[n, h, at, :] for n in range(1, 5))
            for f in range(2 * MODES):
                q = forms[f, h, at, :]
                sums[f] = sums[f] + q * (young if f < MODES else projected)
                ext[h, x + 2, pl.ds((2 + 8 * g) * 8 + f, 8, stride=8), :] = q * (a if f < MODES else b)
        return tuple(sums)

    sums = lax.fori_loop(0, 2 * X, scale, tuple(jnp.zeros((8, L), F32) for _ in range(2 * MODES)))

    part = jnp.concatenate([jnp.sum(s, axis=0, keepdims=True) for s in sums], axis=0)
    for k in (64, 32, 16):
        part = part + pltpu.roll(part, k, 1)
    own = lane // 16 == lax.broadcasted_iota(jnp.int32, (8, L), 0)
    part = jnp.sum(jnp.where(own, part, 0.0), axis=0, keepdims=True)

    def group(slots, offsets, member, n, value):
        slots[0] = value
        for k, o in enumerate(offsets):
            pltpu.make_async_remote_copy(
                src_ref=slots.at[0],
                dst_ref=slots.at[k + 1],
                send_sem=sum_send.at[n],
                recv_sem=sum_recv.at[n],
                device_id=member(gx, gy, o),
                device_id_type=MESH,
            ).start()

    def group_wait(slots, sem):
        others = slots.at[pl.ds(1, slots.shape[0] - 1)]
        pltpu.make_async_copy(others, others, sem).wait()

    def group_sum(slots, n):
        group_wait(slots, sum_recv.at[n])
        return jnp.sum(slots[...], axis=0)

    group(slots_a, GROUP_A, member_a, 0, part)

    def shorten(x, _):
        for h in (0, 1):
            sent[h, x] = ext[h, x + 2, 16:144, :].astype(BF16)
        return 0

    lax.fori_loop(0, X, shorten, 0)
    fields = []
    for i, (a, b) in enumerate(far):
        x0, xn = src_x[a]
        y0, yn = {-1: (0, 2), 0: (0, 16), 1: (14, 2)}[b]
        y1 = {-1: 18, 0: 2, 1: 0}[b]
        fields.append(
            remote(
                sent.at[:, x0 - 2 : x0 - 2 + xn, 8 * y0 : 8 * (y0 + yn), :],
                received.at[:, dst_x[a] : dst_x[a] + xn, 8 * y1 : 8 * (y1 + yn), :],
                field_send.at[i],
                field_recv.at[i],
                a,
                b,
            )
        )
    for field in fields:
        field.start()

    group(slots_b, GROUP_B, member_b, 1, group_sum(slots_a, 0))

    for field in fields:
        field.wait_recv()

    @pl.when(gx == NX - 1)
    def _():
        received[:, 6:8] = jnp.zeros((2, 2, 160, L), BF16)

    @pl.when(gx == 0)
    def _():
        received[:, 0:2] = jnp.zeros((2, 2, 160, L), BF16)

    @pl.when(gy == NY - 1)
    def _():
        received[:, :, 144:160] = jnp.zeros((2, 8, 16, L), BF16)

    @pl.when(gy == 0)
    def _():
        received[:, :, 0:16] = jnp.zeros((2, 8, 16, L), BF16)

    for h in (0, 1):
        for x in range(X + 4):
            if 2 <= x < X + 2:
                for at in (slice(0, 16), slice(144, 160)):
                    ext[h, x, at, :] = received[h, x, at, :].astype(F32)
            else:
                ext[h, x] = received[h, x].astype(F32)

    def filter_fields(x, _):
        f, x1, x2 = [[], []], [[], []], [[], []]
        for y in range(Y + 4):
            for h in (0, 1):
                at = lambda a: ext[h, x + 2 + a, 8 * y : 8 * y + 8, :]
                f[h].append(at(0))
                x1[h].append(at(-1) + at(1))
                x2[h].append(at(-2) + at(2))
        for y in range(Y):
            planes = [plane_sums(f[h][y : y + 5], x1[h][y : y + 5], x2[h][y : y + 5]) for h in (0, 1)]
            g0, g1, g2 = zip(*planes)
            for h, s in enumerate(fold_depth(g0, g1, g2, lane)):
                cone[h, x, 8 * y : 8 * y + 8, :] = s
        return 0

    lax.fori_loop(0, X, filter_fields, 0)

    total = jnp.broadcast_to(group_sum(slots_b, 1), (8, L))
    total = jnp.sum(jnp.where(own, total, 0.0), axis=1, keepdims=True)
    elements_total = float(NX * X * NY * Y * Z)
    first, second = [], []
    for m in range(MODES):
        stiff_norm = jnp.broadcast_to(total[m : m + 1, :], (8, L))
        mass_norm = jnp.broadcast_to(total[MODES + m : MODES + m + 1, :], (8, L))
        first.append(elements_total / mass_norm)
        second.append(first[m] * (stiff_norm / mass_norm))

    def combine(x, _):
        for m in range(MODES):
            for g in (0, 1):
                for h in (0, 1):
                    stiff = cone[h, x, pl.ds(64 * g + m, 8, stride=8), :]
                    mass = cone[h, x, pl.ds(64 * g + MODES + m, 8, stride=8), :]
                    out_ref[m, x, 8 * g : 8 * g + 8, L * h : L * (h + 1)] = first[m] * stiff - second[m] * mass
        return 0

    lax.fori_loop(0, X, combine, 0)

    for copy in halos + fields:
        copy.wait_send()
    group_wait(slots_a, sum_send.at[0])
    group_wait(slots_b, sum_send.at[1])


def local(density, modes):
    return pl.pallas_call(
        kernel,
        out_shape=jax.ShapeDtypeStruct((MODES, X, Y, Z), F32),
        in_specs=[pl.BlockSpec(memory_space=pl.ANY)] * 2,
        out_specs=pl.BlockSpec(memory_space=pltpu.VMEM),
        scratch_shapes=[
            pltpu.VMEM((2, X + 4, 32, L), F32),
            pltpu.VMEM((2, X + 4, 32, L), F32),
            pltpu.VMEM((X + 1, CH, Y, Z), BF16),
            pltpu.VMEM((16 * X, Z), F32),
            pltpu.VMEM((16 * X, Z), BF16),
            pltpu.VMEM((16 * (X + 1), Z), BF16),
            pltpu.VMEM((Z, 2 * Z), BF16),
            pltpu.VMEM((CH, 4, 9 * ZROWS, L), F32),
            pltpu.VMEM((4, 9 * 16, L), F32),
            pltpu.VMEM((2 * MODES, 2, X * Y, L), F32),
            pltpu.VMEM((5, 2, X * Y, L), F32),
            pltpu.VMEM((2, X + 4, 8 * (Y + 4), L), F32),
            pltpu.VMEM((2, X, 8 * Y, L), BF16),
            pltpu.VMEM((2, X + 4, 8 * (Y + 4), L), BF16),
            pltpu.VMEM((2, X, 8 * Y, L), F32),
            pltpu.VMEM((len(GROUP_A) + 1, 1, L), F32),
            pltpu.VMEM((len(GROUP_B) + 1, 1, L), F32),
            pltpu.SemaphoreType.DMA((2 + X,)),
            pltpu.SemaphoreType.DMA((11,)),
            pltpu.SemaphoreType.DMA((11,)),
            pltpu.SemaphoreType.DMA((8,)),
            pltpu.SemaphoreType.DMA((8,)),
            pltpu.SemaphoreType.DMA((2,)),
            pltpu.SemaphoreType.DMA((2,)),
        ],
        compiler_params=pltpu.CompilerParams(
            collective_id=0, has_side_effects=True, vmem_limit_bytes=40 * 1024 * 1024
        ),
    )(*(pltpu.with_memory_space_constraint(a, pltpu.HBM) for a in (density, modes)))


def solution(mesh):
    return jax.shard_map(
        local,
        mesh=mesh,
        in_specs=(P("gx", "gy", None), P(None, "gx", "gy", None)),
        out_specs=P(None, "gx", "gy", None),
        check_vma=False,
    )
```

```python
import functools
import math

import jax
import jax.numpy as jnp
import numpy as np
from jax import lax
from jax.experimental import pallas as pl
from jax.experimental.pallas import tpu as pltpu
from jax.sharding import PartitionSpec as P

RADIUS = 3
BETA_SHARP = 16.0
ETA_MID = 0.5
YOUNG_MIN = 0.001
POISSON = 0.3
MESH = pl.DeviceIdType.MESH

NX, NY = 32, 16
X, Y, Z = 4, 16, 256
L = 128
MODES = 4
CH = 3 * MODES
ZROWS = 24
F32 = jnp.float32
BF16 = jnp.bfloat16

NEIGHBOURS = [(a, b) for a in (-1, 0, 1) for b in (-1, 0, 1) if (a, b) != (0, 0)]


def weight(n):
    return max(0.0, RADIUS - math.sqrt(n))


def position():
    gx, gy = lax.axis_index("gx"), lax.axis_index("gy")
    return gx, gy


def neighbour(gx, gy, a, b):
    return (lax.rem(gx + a + NX, NX), lax.rem(gy + b + NY, NY))


def far_first(offsets, sizes):
    hops = lambda o: sum(min(v, n - v) for v, n in zip(o, sizes))
    return sorted((o for o in offsets if any(o)), key=lambda o: -hops(o))


GROUP_A = far_first([(i, j) for i in range(8) for j in range(4)], (8, 4))
GROUP_B = far_first([(i, j) for i in range(4) for j in range(4)], (4, 4))


def member_a(gx, gy, o):
    i, low = gx // 4, lax.rem(gx, 4)
    high, j = gy // 4, lax.rem(gy, 4)
    return (lax.rem(i + o[0], 8) * 4 + low, high * 4 + lax.rem(j + o[1], 4))


def member_b(gx, gy, o):
    i, low = gx // 4, lax.rem(gx, 4)
    high, j = gy // 4, lax.rem(gy, 4)
    return (i * 4 + lax.rem(low + o[0], 4), lax.rem(high + o[1], 4) * 4 + j)


def fold_depth(g0, g1, g2, lane):
    lo, hi = g0
    for k, (p, q) in ((1, g1), (2, g2)):
        p_up, q_up = pltpu.roll(p, k, 1), pltpu.roll(q, k, 1)
        p_dn, q_dn = pltpu.roll(p, L - k, 1), pltpu.roll(q, L - k, 1)
        first, last = lane < k, lane >= L - k
        lo = lo + (jnp.where(first, 0.0, p_up) + jnp.where(last, q_dn, p_dn))
        hi = hi + (jnp.where(first, p_up, q_up) + jnp.where(last, 0.0, q_dn))
    return lo, hi


def plane_sums(f, x1, x2):
    s0 = f[2]
    s1 = x1[2] + (f[1] + f[3])
    s2 = x1[1] + x1[3]
    s4 = x2[2] + (f[0] + f[4])
    s5 = (x1[0] + x1[4]) + (x2[1] + x2[3])
    s8 = x2[0] + x2[4]
    sums = ((0, s0), (1, s1), (2, s2), (4, s4), (5, s5), (8, s8))
    out = []
    for c in (0, 1, 4):
        total = None
        for n, s in sums:
            w = weight(n + c)
            if w > 0:
                total = w * s if total is None else total + w * s
        out.append(total)
    return out


def filter_density(ext, x, g, lane):
    planes = []
    for h in (0, 1):
        rows = lambda a, b: ext[h, x + 2 + a, 8 + 8 * g + b : 16 + 8 * g + b, :]
        f = [rows(0, b) for b in range(-2, 3)]
        x1 = [rows(-1, b) + rows(1, b) for b in range(-2, 3)]
        x2 = [rows(-2, b) + rows(2, b) for b in range(-2, 3)]
        planes.append(plane_sums(f, x1, x2))
    g0, g1, g2 = zip(*planes)
    return fold_depth(g0, g1, g2, lane)


def energies(t):
    lame = POISSON / ((1.0 + POISSON) * (1.0 - 2.0 * POISSON))
    shear = 1.0 / (2.0 * (1.0 + POISSON))
    sq = lambda v: v * v
    u, v, w = t
    total = lambda terms: functools.reduce(lambda p, q: p + q, terms)
    rigid = total([sq(c[0][0][0]) for c in t])
    diag = sq(u[1][0][0]) + sq(v[0][1][0]) + sq(w[0][0][1])
    first = total([sq(u[0][1][0]), sq(u[0][0][1]), sq(v[1][0][0]), sq(v[0][0][1]), sq(w[1][0][0]), sq(w[0][1][0])])
    second = total([sq(u[1][1][0]), sq(u[1][0][1]), sq(v[1][1][0]), sq(v[0][1][1]), sq(w[1][0][1]), sq(w[0][1][1])])
    other = total([sq(u[0][1][1]), sq(v[1][0][1]), sq(w[1][1][0])])
    third = total([sq(c[1][1][1]) for c in t])
    mass = rigid * (1 / 64) + (diag + first) * (1 / 192) + (second + other) * (1 / 576) + third * (1 / 1728)
    div = sq(u[1][0][0] + v[0][1][0] + w[0][0][1])
    div1 = total([sq(v[1][1][0] + w[1][0][1]), sq(u[1][1][0] + w[0][1][1]), sq(u[1][0][1] + v[0][1][1])])
    slide = total([sq(u[0][1][0] + v[1][0][0]), sq(u[0][0][1] + w[1][0][0]), sq(v[0][0][1] + w[0][1][0])])
    slide1 = total([sq(u[0][1][1] + v[1][0][1]), sq(u[0][1][1] + w[1][1][0]), sq(v[1][0][1] + w[1][1][0])])
    stiff = (
        (lame / 16) * div
        + (lame / 48) * div1
        + (shear / 8) * diag
        + (shear / 16) * slide
        + (shear / 48) * slide1
        + (shear / 16) * second
        + ((lame + 4 * shear) / 144) * third
    )
    return stiff, mass


def across(low, high):
    return [
        [
            [[low[c][j][k] + high[c][j][k] for k in (0, 1)] for j in (0, 1)],
            [[high[c][j][k] - low[c][j][k] for k in (0, 1)] for j in (0, 1)],
        ]
        for c in range(3)
    ]


def layer_of(zs, m, h, x, g):
    out = []
    for c in range(3):
        both = []
        for k in (0, 1):
            at = x * ZROWS + 8 * g
            here = zs[3 * m + c, 2 * k + h, at : at + 8, :]
            there = zs[3 * m + c, 2 * k + h, at + 1 : at + 9, :]
            both.append((here + there, there - here))
        out.append([[both[k][j] for k in (0, 1)] for j in (0, 1)])
    return out


def last_row_of(zs, yz, m, h, x):
    out = []
    for c in range(3):
        both = []
        for k in (0, 1):
            here = zs[3 * m + c, 2 * k + h, pl.ds(x * ZROWS + Y - 1, 8, stride=ZROWS), :]
            there = yz[2 * k + h, pl.ds(x * CH + 3 * m + c, 8, stride=CH), :]
            both.append((here + there, there - here))
        out.append([[both[k][j] for k in (0, 1)] for j in (0, 1)])
    return out


def kernel(
    dens_ref,
    modes_ref,
    out_ref,
    dext,
    wext,
    nodes,
    side_out,
    side_in,
    corner_out,
    corner_in,
    row0,
    first_row,
    next_row,
    zmat,
    zs,
    yz,
    forms,
    coef,
    ext,
    sent,
    received,
    cone,
    slots_a,
    slots_b,
    in_sem,
    halo_send,
    halo_recv,
    field_send,
    field_recv,
    sum_send,
    sum_recv,
):
    gx, gy = position()
    lane = lax.broadcasted_iota(jnp.int32, (8, L), 1)

    barrier = pltpu.get_barrier_semaphore()
    for a, b in NEIGHBOURS:
        pl.semaphore_signal(barrier, inc=1, device_id=neighbour(gx, gy, a, b), device_id_type=MESH)
    loads = [
        pltpu.make_async_copy(dens_ref.at[:, :, L * h : L * (h + 1)], dext.at[h, 2:6, 8:24, :], in_sem.at[h])
        for h in (0, 1)
    ] + [pltpu.make_async_copy(modes_ref.at[:, x], nodes.at[x], in_sem.at[2 + x]) for x in range(X)]
    for load in loads:
        load.start()

    for o in GROUP_B:
        pl.semaphore_signal(barrier, inc=1, device_id=member_b(gx, gy, o), device_id_type=MESH)
    for o in GROUP_A:
        pl.semaphore_signal(barrier, inc=1, device_id=member_a(gx, gy, o), device_id_type=MESH)

    for load in loads:
        load.wait()

    corners = [(a, b) for a in (-1, 1) for b in (-1, 1)]
    rows_from = {-1: slice(8, 10), 1: slice(22, 24)}
    for h in (0, 1):
        for s, b in enumerate((-1, 1)):
            for x in range(X):
                side_out[s, h, 2 * x : 2 * x + 2, :] = dext[h, x + 2, rows_from[b], :]
        for k, (a, b) in enumerate(corners):
            for i in (0, 1):
                x = i if a == -1 else X - 2 + i
                corner_out[k, 4 * h + 2 * i : 4 * h + 2 * i + 2, :] = dext[h, x + 2, rows_from[b], :]

    def pack(c, _):
        for x in range(X):
            row0[pl.ds(x * CH + c, 1), :] = nodes[x, c].astype(F32)[0:1, :]
        return 0

    lax.fori_loop(0, CH, pack, 0)
    first_row[...] = row0[...].astype(BF16)

    pl.semaphore_wait(barrier, len(NEIGHBOURS) + len(GROUP_A) + len(GROUP_B))

    def remote(src, dst, send, recv, a, b):
        return pltpu.make_async_remote_copy(
            src_ref=src,
            dst_ref=dst,
            send_sem=send,
            recv_sem=recv,
            device_id=neighbour(gx, gy, a, b),
            device_id_type=MESH,
        )

    src_x, dst_x = {-1: (2, 2), 0: (2, 4), 1: (4, 2)}, {-1: 6, 0: 2, 1: 0}
    far = sorted(NEIGHBOURS, key=lambda o: -abs(o[0]) - abs(o[1]))
    parts = [(first_row.at[0:16], next_row.at[CH * X : CH * X + 16], -1, -1)]
    parts += [(corner_out.at[k], corner_in.at[k], a, b) for k, (a, b) in enumerate(corners)]
    parts += [(side_out.at[s], side_in.at[s], 0, b) for s, b in enumerate((-1, 1))]
    parts.append((first_row, next_row.at[0 : CH * X], 0, -1))
    for a in (-1, 1):
        x0 = src_x[a][0]
        parts.append((dext.at[:, x0 : x0 + 2, 8:24, :], dext.at[:, dst_x[a] : dst_x[a] + 2, 8:24, :], a, 0))
    parts.append((nodes.at[0], nodes.at[X], -1, 0))
    halos = [remote(src, dst, halo_send.at[i], halo_recv.at[i], a, b) for i, (src, dst, a, b) in enumerate(parts)]
    for halo in halos:
        halo.start()

    for h in (0, 1):
        for x in range(X + 4):
            ix = gx * X + (x - 2)
            inside_x = jnp.where((ix >= 0) & (ix < NX * X), 1.0, 0.0)
            iy = gy * Y - 8 + lax.broadcasted_iota(jnp.int32, (32, L), 0)
            wext[h, x] = jnp.where((iy >= 0) & (iy < NY * Y), inside_x, 0.0)

    def weights(x, _):
        for g in (0, 1):
            at = pl.ds(pl.multiple_of(x * Y + 8 * g, 8), 8)
            for h, s in enumerate(filter_density(wext, x, g, lane)):
                coef[0, h, at, :] = 1.0 / s
        return 0

    lax.fori_loop(0, X, weights, 0)

    row = lax.broadcasted_iota(jnp.int32, (Z, Z), 0)
    col = lax.broadcasted_iota(jnp.int32, (Z, Z), 1)
    here = jnp.where(row == col, 1.0, 0.0)
    there = jnp.where(row == col + 1, 1.0, 0.0)
    zmat[:, 0:Z] = (here + there).astype(BF16)
    zmat[:, Z : 2 * Z] = (there - here).astype(BF16)

    def depth(x, _):
        t = jnp.dot(nodes[x].reshape(CH * Y, Z), zmat[...], preferred_element_type=F32)
        at = pl.ds(pl.multiple_of(x * ZROWS, 8), Y)
        for c in range(CH):
            for q in range(4):
                zs[c, q, at, :] = t[c * Y : (c + 1) * Y, q * L : (q + 1) * L]
        return 0

    lax.fori_loop(0, X, depth, 0)

    def elements(x0, x1):
        def body(i, _):
            m, h = i // 2, lax.rem(i, 2)
            for g in (0, 1):
                low = layer_of(zs, m, h, x0, g)
                for x in range(x0, x1):
                    high = layer_of(zs, m, h, x + 1, g)
                    kq, mq = energies(across(low, high))
                    at = slice(x * Y + 8 * g, x * Y + 8 * g + 8)
                    forms[m, h, at, :] = kq
                    forms[MODES + m, h, at, :] = mq
                    low = high
            return 0

        lax.fori_loop(0, 2 * MODES, body, 0)

    elements(0, X - 1)

    for halo in halos:
        halo.wait_recv()

    @pl.when(gx == NX - 1)
    def _():
        nodes[X] = jnp.zeros((CH, Y, Z), BF16)
        next_row[CH * X : CH * X + 16, :] = jnp.zeros((16, Z), BF16)
        dext[:, 6:8, 8:24] = jnp.zeros((2, 2, Y, L), F32)
        corner_in[0:2] = jnp.zeros((2, 8, L), F32)

    @pl.when(gx == 0)
    def _():
        dext[:, 0:2, 8:24] = jnp.zeros((2, 2, Y, L), F32)
        corner_in[2:4] = jnp.zeros((2, 8, L), F32)

    @pl.when(gy == NY - 1)
    def _():
        next_row[...] = jnp.zeros((CH * X + 16, Z), BF16)
        side_in[0] = jnp.zeros((2, 8, L), F32)
        corner_in[0] = jnp.zeros((8, L), F32)
        corner_in[2] = jnp.zeros((8, L), F32)

    @pl.when(gy == 0)
    def _():
        side_in[1] = jnp.zeros((2, 8, L), F32)
        corner_in[1] = jnp.zeros((8, L), F32)
        corner_in[3] = jnp.zeros((8, L), F32)

    rows_to = {-1: slice(24, 26), 1: slice(6, 8)}
    for h in (0, 1):
        for s, b in enumerate((-1, 1)):
            for x in range(X):
                dext[h, x + 2, rows_to[b], :] = side_in[s, h, 2 * x : 2 * x + 2, :]
        for k, (a, b) in enumerate(corners):
            for i in (0, 1):
                dext[h, dst_x[a] + i, rows_to[b], :] = corner_in[k, 4 * h + 2 * i : 4 * h + 2 * i + 2, :]

    depth(X, 0)
    t = jnp.dot(next_row[...], zmat[...], preferred_element_type=F32)
    for q in range(4):
        yz[q, 0 : CH * X + 16, :] = t[:, q * L : (q + 1) * L]

    elements(X - 1, X)

    def last_row(i, _):
        m, h = i // 2, lax.rem(i, 2)
        kq, mq = energies(across(last_row_of(zs, yz, m, h, 0), last_row_of(zs, yz, m, h, 1)))
        forms[m, h, pl.ds(Y - 1, X, stride=Y), :] = kq[0:X]
        forms[MODES + m, h, pl.ds(Y - 1, X, stride=Y), :] = mq[0:X]
        return 0

    lax.fori_loop(0, 2 * MODES, last_row, 0)

    top = math.tanh(BETA_SHARP * ETA_MID)
    denom = top + math.tanh(BETA_SHARP * (1.0 - ETA_MID))

    def project(x, _):
        for g in (0, 1):
            at = pl.ds(pl.multiple_of(x * Y + 8 * g, 8), 8)
            for h, s in enumerate(filter_density(dext, x, g, lane)):
                share = coef[0, h, at, :]
                sharp = jnp.tanh(BETA_SHARP * (s * share - ETA_MID))
                projected = (top + sharp) * (1.0 / denom)
                slope = (BETA_SHARP / denom) * (1.0 - sharp * sharp) * share
                square = projected * projected
                coef[1, h, at, :] = YOUNG_MIN + square * projected * (1.0 - YOUNG_MIN)
                coef[2, h, at, :] = projected
                coef[3, h, at, :] = slope * (square * (3.0 * (1.0 - YOUNG_MIN)))
                coef[4, h, at, :] = slope
        return 0

    lax.fori_loop(0, X, project, 0)

    def scale(i, sums):
        h, x = i // X, lax.rem(i, X)
        sums = list(sums)
        for g in (0, 1):
            at = pl.ds(pl.multiple_of(x * Y + 8 * g, 8), 8)
            young, projected, a, b = (coef[n, h, at, :] for n in range(1, 5))
            for f in range(2 * MODES):
                q = forms[f, h, at, :]
                sums[f] = sums[f] + q * (young if f < MODES else projected)
                ext[h, x + 2, pl.ds((2 + 8 * g) * 8 + f, 8, stride=8), :] = q * (a if f < MODES else b)
        return tuple(sums)

    sums = lax.fori_loop(0, 2 * X, scale, tuple(jnp.zeros((8, L), F32) for _ in range(2 * MODES)))

    part = jnp.concatenate([jnp.sum(s, axis=0, keepdims=True) for s in sums], axis=0)
    for k in (64, 32, 16):
        part = part + pltpu.roll(part, k, 1)
    own = lane // 16 == lax.broadcasted_iota(jnp.int32, (8, L), 0)
    part = jnp.sum(jnp.where(own, part, 0.0), axis=0, keepdims=True)

    def group(slots, offsets, member, n, value):
        slots[0] = value
        for k, o in enumerate(offsets):
            pltpu.make_async_remote_copy(
                src_ref=slots.at[0],
                dst_ref=slots.at[k + 1],
                send_sem=sum_send.at[n],
                recv_sem=sum_recv.at[n],
                device_id=member(gx, gy, o),
                device_id_type=MESH,
            ).start()

    def group_wait(slots, sem):
        others = slots.at[pl.ds(1, slots.shape[0] - 1)]
        pltpu.make_async_copy(others, others, sem).wait()

    def group_sum(slots, n):
        group_wait(slots, sum_recv.at[n])
        return jnp.sum(slots[...], axis=0)

    group(slots_a, GROUP_A, member_a, 0, part)

    def shorten(x, _):
        for h in (0, 1):
            sent[h, x] = ext[h, x + 2, 16:144, :].astype(BF16)
        return 0

    lax.fori_loop(0, X, shorten, 0)
    fields = []
    for i, (a, b) in enumerate(far):
        x0, xn = src_x[a]
        y0, yn = {-1: (0, 2), 0: (0, 16), 1: (14, 2)}[b]
        y1 = {-1: 18, 0: 2, 1: 0}[b]
        fields.append(
            remote(
                sent.at[:, x0 - 2 : x0 - 2 + xn, 8 * y0 : 8 * (y0 + yn), :],
                received.at[:, dst_x[a] : dst_x[a] + xn, 8 * y1 : 8 * (y1 + yn), :],
                field_send.at[i],
                field_recv.at[i],
                a,
                b,
            )
        )
    for field in fields:
        field.start()

    group(slots_b, GROUP_B, member_b, 1, group_sum(slots_a, 0))

    for field in fields:
        field.wait_recv()

    @pl.when(gx == NX - 1)
    def _():
        received[:, 6:8] = jnp.zeros((2, 2, 160, L), BF16)

    @pl.when(gx == 0)
    def _():
        received[:, 0:2] = jnp.zeros((2, 2, 160, L), BF16)

    @pl.when(gy == NY - 1)
    def _():
        received[:, :, 144:160] = jnp.zeros((2, 8, 16, L), BF16)

    @pl.when(gy == 0)
    def _():
        received[:, :, 0:16] = jnp.zeros((2, 8, 16, L), BF16)

    for h in (0, 1):
        for x in range(X + 4):
            if 2 <= x < X + 2:
                for at in (slice(0, 16), slice(144, 160)):
                    ext[h, x, at, :] = received[h, x, at, :].astype(F32)
            else:
                ext[h, x] = received[h, x].astype(F32)

    def filter_fields(x, _):
        f, x1, x2 = [[], []], [[], []], [[], []]
        for y in range(Y + 4):
            for h in (0, 1):
                at = lambda a: ext[h, x + 2 + a, 8 * y : 8 * y + 8, :]
                f[h].append(at(0))
                x1[h].append(at(-1) + at(1))
                x2[h].append(at(-2) + at(2))
        for y in range(Y):
            planes = [plane_sums(f[h][y : y + 5], x1[h][y : y + 5], x2[h][y : y + 5]) for h in (0, 1)]
            g0, g1, g2 = zip(*planes)
            for h, s in enumerate(fold_depth(g0, g1, g2, lane)):
                cone[h, x, 8 * y : 8 * y + 8, :] = s
        return 0

    lax.fori_loop(0, X, filter_fields, 0)

    total = jnp.broadcast_to(group_sum(slots_b, 1), (8, L))
    total = jnp.sum(jnp.where(own, total, 0.0), axis=1, keepdims=True)
    elements_total = float(NX * X * NY * Y * Z)
    first, second = [], []
    for m in range(MODES):
        stiff_norm = jnp.broadcast_to(total[m : m + 1, :], (8, L))
        mass_norm = jnp.broadcast_to(total[MODES + m : MODES + m + 1, :], (8, L))
        first.append(elements_total / mass_norm)
        second.append(first[m] * (stiff_norm / mass_norm))

    def combine(x, _):
        for m in range(MODES):
            for g in (0, 1):
                for h in (0, 1):
                    stiff = cone[h, x, pl.ds(64 * g + m, 8, stride=8), :]
                    mass = cone[h, x, pl.ds(64 * g + MODES + m, 8, stride=8), :]
                    out_ref[m, x, 8 * g : 8 * g + 8, L * h : L * (h + 1)] = first[m] * stiff - second[m] * mass
        return 0

    lax.fori_loop(0, X, combine, 0)

    for copy in halos + fields:
        copy.wait_send()
    group_wait(slots_a, sum_send.at[0])
    group_wait(slots_b, sum_send.at[1])


def local(density, modes):
    return pl.pallas_call(
        kernel,
        out_shape=jax.ShapeDtypeStruct((MODES, X, Y, Z), F32),
        in_specs=[pl.BlockSpec(memory_space=pl.ANY)] * 2,
        out_specs=pl.BlockSpec(memory_space=pltpu.VMEM),
        scratch_shapes=[
            pltpu.VMEM((2, X + 4, 32, L), F32),
            pltpu.VMEM((2, X + 4, 32, L), F32),
            pltpu.VMEM((X + 1, CH, Y, Z), BF16),
            pltpu.VMEM((2, 2, 8, L), F32),
            pltpu.VMEM((2, 2, 8, L), F32),
            pltpu.VMEM((4, 8, L), F32),
            pltpu.VMEM((4, 8, L), F32),
            pltpu.VMEM((CH * X, Z), F32),
            pltpu.VMEM((CH * X, Z), BF16),
            pltpu.VMEM((CH * X + 16, Z), BF16),
            pltpu.VMEM((Z, 2 * Z), BF16),
            pltpu.VMEM((CH, 4, 9 * ZROWS, L), F32),
            pltpu.VMEM((4, 112, L), F32),
            pltpu.VMEM((2 * MODES, 2, X * Y, L), F32),
            pltpu.VMEM((5, 2, X * Y, L), F32),
            pltpu.VMEM((2, X + 4, 8 * (Y + 4), L), F32),
            pltpu.VMEM((2, X, 8 * Y, L), BF16),
            pltpu.VMEM((2, X + 4, 8 * (Y + 4), L), BF16),
            pltpu.VMEM((2, X, 8 * Y, L), F32),
            pltpu.VMEM((len(GROUP_A) + 1, 1, L), F32),
            pltpu.VMEM((len(GROUP_B) + 1, 1, L), F32),
            pltpu.SemaphoreType.DMA((2 + X,)),
            pltpu.SemaphoreType.DMA((11,)),
            pltpu.SemaphoreType.DMA((11,)),
            pltpu.SemaphoreType.DMA((8,)),
            pltpu.SemaphoreType.DMA((8,)),
            pltpu.SemaphoreType.DMA((2,)),
            pltpu.SemaphoreType.DMA((2,)),
        ],
        compiler_params=pltpu.CompilerParams(
            collective_id=0, has_side_effects=True, vmem_limit_bytes=40 * 1024 * 1024
        ),
    )(*(pltpu.with_memory_space_constraint(a, pltpu.HBM) for a in (density, modes)))


def solution(mesh):
    return jax.shard_map(
        local,
        mesh=mesh,
        in_specs=(P("gx", "gy", None), P(None, "gx", "gy", None)),
        out_specs=P(None, "gx", "gy", None),
        check_vma=False,
    )
```

```python
import functools
import math

import jax
import jax.numpy as jnp
import numpy as np
from jax import lax
from jax.experimental import pallas as pl
from jax.experimental.pallas import tpu as pltpu
from jax.sharding import PartitionSpec as P

RADIUS = 3
BETA_SHARP = 16.0
ETA_MID = 0.5
YOUNG_MIN = 0.001
POISSON = 0.3
MESH = pl.DeviceIdType.MESH

NX, NY = 32, 16
X, Y, Z = 4, 16, 256
L = 128
MODES = 4
CH = 3 * MODES
ZROWS = 24
F32 = jnp.float32
BF16 = jnp.bfloat16

NEIGHBOURS = [(a, b) for a in (-1, 0, 1) for b in (-1, 0, 1) if (a, b) != (0, 0)]


def weight(n):
    return max(0.0, RADIUS - math.sqrt(n))


def position():
    gx, gy = lax.axis_index("gx"), lax.axis_index("gy")
    return gx, gy


def exists(gx, gy, a, b):
    inside = {-1: lambda i, n: [i > 0], 0: lambda i, n: [], 1: lambda i, n: [i < n - 1]}
    return functools.reduce(jnp.logical_and, inside[a](gx, NX) + inside[b](gy, NY))


def neighbour(gx, gy, a, b):
    return (lax.rem(gx + a + NX, NX), lax.rem(gy + b + NY, NY))


def ring(v, n):
    v %= n
    return min(v, n - v)


def hops_a(o):
    return ring(o[0], 8) + ring(o[1], 4)


def hops_b(o):
    return ring(o[0], 8)


GROUP_A = sorted(((y, x) for y in range(8) for x in range(4) if (y, x) != (0, 0)), key=lambda o: -hops_a(o))
GROUP_B = sorted(((z, c) for z in range(8) for c in range(2) if (z, c) != (0, 0)), key=lambda o: -hops_b(o))
NEAR_A = [o for o in GROUP_A if hops_a(o) <= 3]
NEAR_B = [o for o in GROUP_B if hops_b(o) <= 2]
TOKENS_A = [(2, 1), (6, 1), (2, 3)]
TOKENS_B = [(2, 0), (6, 0)]
for group, near, tokens, hops, limit in (
    (GROUP_A, NEAR_A, TOKENS_A, hops_a, 3),
    (GROUP_B, NEAR_B, TOKENS_B, hops_b, 2),
):
    assert all(t in near for t in tokens)
    assert all(o in near or any(hops((o[0] - t[0], o[1] - t[1])) <= limit for t in tokens) for o in group)


def member_a(gx, gy, o):
    y, low = gx // 4, lax.rem(gx, 4)
    high, x = gy // 4, lax.rem(gy, 4)
    return (lax.rem(y + o[0], 8) * 4 + low, high * 4 + lax.rem(x + o[1], 4))


def member_b(gx, gy, o):
    y, core = gx // 4, lax.rem(gx, 2)
    z = lax.rem(2 * (gy // 4) + lax.rem(gx // 2, 2) + o[0], 8)
    return (y * 4 + 2 * lax.rem(z, 2) + lax.rem(core + o[1], 2), (z // 2) * 4 + lax.rem(gy, 4))


def fold_depth(g0, g1, g2, lane):
    lo, hi = g0
    for k, (p, q) in ((1, g1), (2, g2)):
        p_up, q_up = pltpu.roll(p, k, 1), pltpu.roll(q, k, 1)
        p_dn, q_dn = pltpu.roll(p, L - k, 1), pltpu.roll(q, L - k, 1)
        first, last = lane < k, lane >= L - k
        lo = lo + (jnp.where(first, 0.0, p_up) + jnp.where(last, q_dn, p_dn))
        hi = hi + (jnp.where(first, p_up, q_up) + jnp.where(last, 0.0, q_dn))
    return lo, hi


def plane_sums(f, x1, x2):
    s0 = f[2]
    s1 = x1[2] + (f[1] + f[3])
    s2 = x1[1] + x1[3]
    s4 = x2[2] + (f[0] + f[4])
    s5 = (x1[0] + x1[4]) + (x2[1] + x2[3])
    s8 = x2[0] + x2[4]
    sums = ((0, s0), (1, s1), (2, s2), (4, s4), (5, s5), (8, s8))
    out = []
    for c in (0, 1, 4):
        total = None
        for n, s in sums:
            w = weight(n + c)
            if w > 0:
                total = w * s if total is None else total + w * s
        out.append(total)
    return out


def filter_density(ext, x, g, lane):
    planes = []
    for h in (0, 1):
        rows = lambda a, b: ext[h, x + 2 + a, 8 + 8 * g + b : 16 + 8 * g + b, :]
        f = [rows(0, b) for b in range(-2, 3)]
        x1 = [rows(-1, b) + rows(1, b) for b in range(-2, 3)]
        x2 = [rows(-2, b) + rows(2, b) for b in range(-2, 3)]
        planes.append(plane_sums(f, x1, x2))
    g0, g1, g2 = zip(*planes)
    return fold_depth(g0, g1, g2, lane)


def energies(t):
    lame = POISSON / ((1.0 + POISSON) * (1.0 - 2.0 * POISSON))
    shear = 1.0 / (2.0 * (1.0 + POISSON))
    sq = lambda v: v * v
    u, v, w = t
    total = lambda terms: functools.reduce(lambda p, q: p + q, terms)
    rigid = total([sq(c[0][0][0]) for c in t])
    diag = sq(u[1][0][0]) + sq(v[0][1][0]) + sq(w[0][0][1])
    first = total([sq(u[0][1][0]), sq(u[0][0][1]), sq(v[1][0][0]), sq(v[0][0][1]), sq(w[1][0][0]), sq(w[0][1][0])])
    second = total([sq(u[1][1][0]), sq(u[1][0][1]), sq(v[1][1][0]), sq(v[0][1][1]), sq(w[1][0][1]), sq(w[0][1][1])])
    other = total([sq(u[0][1][1]), sq(v[1][0][1]), sq(w[1][1][0])])
    third = total([sq(c[1][1][1]) for c in t])
    mass = rigid * (1 / 64) + (diag + first) * (1 / 192) + (second + other) * (1 / 576) + third * (1 / 1728)
    div = sq(u[1][0][0] + v[0][1][0] + w[0][0][1])
    div1 = total([sq(v[1][1][0] + w[1][0][1]), sq(u[1][1][0] + w[0][1][1]), sq(u[1][0][1] + v[0][1][1])])
    slide = total([sq(u[0][1][0] + v[1][0][0]), sq(u[0][0][1] + w[1][0][0]), sq(v[0][0][1] + w[0][1][0])])
    slide1 = total([sq(u[0][1][1] + v[1][0][1]), sq(u[0][1][1] + w[1][1][0]), sq(v[1][0][1] + w[1][1][0])])
    stiff = (
        (lame / 16) * div
        + (lame / 48) * div1
        + (shear / 8) * diag
        + (shear / 16) * slide
        + (shear / 48) * slide1
        + (shear / 16) * second
        + ((lame + 4 * shear) / 144) * third
    )
    return stiff, mass


def across(low, high):
    return [
        [
            [[low[c][j][k] + high[c][j][k] for k in (0, 1)] for j in (0, 1)],
            [[high[c][j][k] - low[c][j][k] for k in (0, 1)] for j in (0, 1)],
        ]
        for c in range(3)
    ]


def layer_of(zs, m, h, x, g):
    out = []
    for c in range(3):
        both = []
        for k in (0, 1):
            at = x * ZROWS + 8 * g
            here = zs[3 * m + c, 2 * k + h, at : at + 8, :]
            there = zs[3 * m + c, 2 * k + h, at + 1 : at + 9, :]
            both.append((here + there, there - here))
        out.append([[both[k][j] for k in (0, 1)] for j in (0, 1)])
    return out


def last_row_of(zs, yz, m, h, x):
    out = []
    for c in range(3):
        both = []
        for k in (0, 1):
            here = zs[3 * m + c, 2 * k + h, pl.ds(x * ZROWS + Y - 1, 8, stride=ZROWS), :]
            there = yz[2 * k + h, pl.ds(x * CH + 3 * m + c, 8, stride=CH), :]
            both.append((here + there, there - here))
        out.append([[both[k][j] for k in (0, 1)] for j in (0, 1)])
    return out


def kernel(
    dens_ref,
    modes_ref,
    out_ref,
    dext,
    wext,
    nodes,
    side_out,
    side_in,
    corner_out,
    corner_in,
    row0,
    first_row,
    next_row,
    zmat,
    zs,
    yz,
    forms,
    coef,
    ext,
    sent,
    received,
    cone,
    slots_a,
    slots_b,
    in_sem,
    halo_send,
    halo_recv,
    field_send,
    field_recv,
    sum_send,
    sum_recv,
    token,
):
    gx, gy = position()
    lane = lax.broadcasted_iota(jnp.int32, (8, L), 1)

    barrier = pltpu.get_barrier_semaphore()
    for a, b in NEIGHBOURS:

        @pl.when(exists(gx, gy, a, b))
        def _(a=a, b=b):
            pl.semaphore_signal(barrier, inc=1, device_id=neighbour(gx, gy, a, b), device_id_type=MESH)

    loads = [
        pltpu.make_async_copy(dens_ref.at[:, :, L * h : L * (h + 1)], dext.at[h, 2:6, 8:24, :], in_sem.at[h])
        for h in (0, 1)
    ] + [pltpu.make_async_copy(modes_ref.at[:, x], nodes.at[x], in_sem.at[2 + x]) for x in range(X)]
    for load in loads:
        load.start()

    for o in NEAR_A:
        pl.semaphore_signal(barrier, inc=1, device_id=member_a(gx, gy, o), device_id_type=MESH)
    for o in NEAR_B:
        pl.semaphore_signal(barrier, inc=1, device_id=member_b(gx, gy, o), device_id_type=MESH)

    for load in loads:
        load.wait()

    corners = [(a, b) for a in (-1, 1) for b in (-1, 1)]
    rows_from = {-1: slice(8, 10), 1: slice(22, 24)}
    for h in (0, 1):
        for s, b in enumerate((-1, 1)):
            for x in range(X):
                side_out[s, h, 2 * x : 2 * x + 2, :] = dext[h, x + 2, rows_from[b], :]
        for k, (a, b) in enumerate(corners):
            for i in (0, 1):
                x = i if a == -1 else X - 2 + i
                corner_out[k, 4 * h + 2 * i : 4 * h + 2 * i + 2, :] = dext[h, x + 2, rows_from[b], :]

    def remote(src, dst, send, recv, a, b):
        return pltpu.make_async_remote_copy(
            src_ref=src,
            dst_ref=dst,
            send_sem=send,
            recv_sem=recv,
            device_id=neighbour(gx, gy, a, b),
            device_id_type=MESH,
        )

    src_x, dst_x = {-1: (2, 2), 0: (2, 4), 1: (4, 2)}, {-1: 6, 0: 2, 1: 0}
    far = sorted(NEIGHBOURS, key=lambda o: (-abs(o[0]) - abs(o[1]), abs(o[0]), -o[0]))
    parts = [(first_row.at[0:16], next_row.at[CH * X : CH * X + 16], -1, -1)]
    parts += [(corner_out.at[k], corner_in.at[k], a, b) for k, (a, b) in enumerate(corners)]
    parts += [(side_out.at[s], side_in.at[s], 0, b) for s, b in enumerate((-1, 1))]
    parts.append((first_row, next_row.at[0 : CH * X], 0, -1))
    for a in (-1, 1):
        x0 = src_x[a][0]
        parts.append((dext.at[:, x0 : x0 + 2, 8:24, :], dext.at[:, dst_x[a] : dst_x[a] + 2, 8:24, :], a, 0))
    parts.append((nodes.at[0], nodes.at[X], -1, 0))
    halos = [(remote(src, dst, halo_send.at[i], halo_recv.at[i], a, b), a, b) for i, (src, dst, a, b) in enumerate(parts)]
    parts_f = []
    for a, b in far:
        x0, xn = src_x[a]
        y0, yn = {-1: (0, 2), 0: (0, 16), 1: (14, 2)}[b]
        y1 = {-1: 18, 0: 2, 1: 0}[b]
        parts_f.append(
            (
                sent.at[:, x0 - 2 : x0 - 2 + xn, 8 * y0 : 8 * (y0 + yn), :],
                received.at[:, dst_x[a] : dst_x[a] + xn, 8 * y1 : 8 * (y1 + yn), :],
                a,
                b,
            )
        )
    fields = [
        (remote(src, dst, field_send.at[i], field_recv.at[i], a, b), a, b) for i, (src, dst, a, b) in enumerate(parts_f)
    ]

    for _, dst, a, b in parts + parts_f:

        @pl.when(jnp.logical_not(exists(gx, gy, -a, -b)))
        def _(dst=dst):
            dst[...] = jnp.zeros(dst.shape, dst.dtype)

    def each(copies, step, sign):
        for direction in far:
            mine = [copy for copy, a, b in copies if (a, b) == direction]

            @pl.when(exists(gx, gy, sign * direction[0], sign * direction[1]))
            def _(mine=mine):
                for copy in mine:
                    step(copy)

    def start(copies):
        each(copies, lambda copy: copy.start(), 1)

    def arrive(copies):
        each(copies, lambda copy: copy.wait_recv(), -1)

    def leave(copies):
        each(copies, lambda copy: copy.wait_send(), 1)

    def pack(c, _):
        for x in range(X):
            row0[pl.ds(x * CH + c, 1), :] = nodes[x, c].astype(F32)[0:1, :]
        return 0

    lax.fori_loop(0, CH, pack, 0)
    first_row[...] = row0[...].astype(BF16)

    along = lambda i, n: 1 + (i > 0).astype(jnp.int32) + (i < n - 1).astype(jnp.int32)
    pl.semaphore_wait(barrier, along(gx, NX) * along(gy, NY) - 1 + len(NEAR_A) + len(NEAR_B))

    start(halos)
    for tokens, member in ((TOKENS_A, member_a), (TOKENS_B, member_b)):
        for o in tokens:
            back = (8 - o[0], (4 if member is member_a else 2) - o[1])
            pl.semaphore_signal(token, inc=1, device_id=member(gx, gy, back), device_id_type=MESH)

    for h in (0, 1):
        for x in range(X + 4):
            ix = gx * X + (x - 2)
            inside_x = jnp.where((ix >= 0) & (ix < NX * X), 1.0, 0.0)
            iy = gy * Y - 8 + lax.broadcasted_iota(jnp.int32, (32, L), 0)
            wext[h, x] = jnp.where((iy >= 0) & (iy < NY * Y), inside_x, 0.0)

    def weights(x, _):
        for g in (0, 1):
            at = pl.ds(pl.multiple_of(x * Y + 8 * g, 8), 8)
            for h, s in enumerate(filter_density(wext, x, g, lane)):
                coef[0, h, at, :] = 1.0 / s
        return 0

    lax.fori_loop(0, X, weights, 0)

    row = lax.broadcasted_iota(jnp.int32, (Z, Z), 0)
    col = lax.broadcasted_iota(jnp.int32, (Z, Z), 1)
    here = jnp.where(row == col, 1.0, 0.0)
    there = jnp.where(row == col + 1, 1.0, 0.0)
    zmat[:, 0:Z] = (here + there).astype(BF16)
    zmat[:, Z : 2 * Z] = (there - here).astype(BF16)

    def depth(x, _):
        t = jnp.dot(nodes[x].reshape(CH * Y, Z), zmat[...], preferred_element_type=F32)
        at = pl.ds(pl.multiple_of(x * ZROWS, 8), Y)
        for c in range(CH):
            for q in range(4):
                zs[c, q, at, :] = t[c * Y : (c + 1) * Y, q * L : (q + 1) * L]
        return 0

    lax.fori_loop(0, X, depth, 0)

    def elements(x0, x1):
        def body(i, _):
            m, h = i // 2, lax.rem(i, 2)
            for g in (0, 1):
                low = layer_of(zs, m, h, x0, g)
                for x in range(x0, x1):
                    high = layer_of(zs, m, h, x + 1, g)
                    kq, mq = energies(across(low, high))
                    at = slice(x * Y + 8 * g, x * Y + 8 * g + 8)
                    forms[m, h, at, :] = kq
                    forms[MODES + m, h, at, :] = mq
                    low = high
            return 0

        lax.fori_loop(0, 2 * MODES, body, 0)

    elements(0, X - 1)

    arrive(halos[1:7] + halos[8:10])

    rows_to = {-1: slice(24, 26), 1: slice(6, 8)}
    for h in (0, 1):
        for s, b in enumerate((-1, 1)):
            for x in range(X):
                dext[h, x + 2, rows_to[b], :] = side_in[s, h, 2 * x : 2 * x + 2, :]
        for k, (a, b) in enumerate(corners):
            for i in (0, 1):
                dext[h, dst_x[a] + i, rows_to[b], :] = corner_in[k, 4 * h + 2 * i : 4 * h + 2 * i + 2, :]

    top = math.tanh(BETA_SHARP * ETA_MID)
    denom = top + math.tanh(BETA_SHARP * (1.0 - ETA_MID))

    def project(x, _):
        for g in (0, 1):
            at = pl.ds(pl.multiple_of(x * Y + 8 * g, 8), 8)
            for h, s in enumerate(filter_density(dext, x, g, lane)):
                share = coef[0, h, at, :]
                sharp = jnp.tanh(BETA_SHARP * (s * share - ETA_MID))
                projected = (top + sharp) * (1.0 / denom)
                slope = (BETA_SHARP / denom) * (1.0 - sharp * sharp) * share
                square = projected * projected
                coef[1, h, at, :] = YOUNG_MIN + square * projected * (1.0 - YOUNG_MIN)
                coef[2, h, at, :] = projected
                coef[3, h, at, :] = slope * (square * (3.0 * (1.0 - YOUNG_MIN)))
                coef[4, h, at, :] = slope
        return 0

    lax.fori_loop(0, X, project, 0)

    arrive(halos[10:])
    depth(X, 0)
    elements(X - 1, X)

    def scale(g, i, sums):
        h, x = i // X, lax.rem(i, X)
        sums = list(sums)
        at = pl.ds(pl.multiple_of(x * Y + 8 * g, 8), 8)
        young, projected, a, b = (coef[n, h, at, :] for n in range(1, 5))
        for f in range(2 * MODES):
            q = forms[f, h, at, :]
            sums[f] = sums[f] + q * (young if f < MODES else projected)
            ext[h, x + 2, pl.ds((2 + 8 * g) * 8 + f, 8, stride=8), :] = q * (a if f < MODES else b)
        return tuple(sums)

    zeros = tuple(jnp.zeros((8, L), F32) for _ in range(2 * MODES))
    sums = lax.fori_loop(0, 2 * X, functools.partial(scale, 0), zeros)

    arrive(halos[0:1] + halos[7:8])
    t = jnp.dot(next_row[...], zmat[...], preferred_element_type=F32)
    for q in range(4):
        yz[q, 0 : CH * X + 16, :] = t[:, q * L : (q + 1) * L]

    def last_row(i, _):
        m, h = i // 2, lax.rem(i, 2)
        kq, mq = energies(across(last_row_of(zs, yz, m, h, 0), last_row_of(zs, yz, m, h, 1)))
        forms[m, h, pl.ds(Y - 1, X, stride=Y), :] = kq[0:X]
        forms[MODES + m, h, pl.ds(Y - 1, X, stride=Y), :] = mq[0:X]
        return 0

    lax.fori_loop(0, 2 * MODES, last_row, 0)

    sums = lax.fori_loop(0, 2 * X, functools.partial(scale, 1), sums)

    part = list(sums)
    for k in (64, 32, 16):
        half = len(part) // 2
        upper = lane & k != 0
        part = [
            jnp.where(upper, q + pltpu.roll(q, k, 1), p + pltpu.roll(p, L - k, 1))
            for p, q in zip(part[:half], part[half:])
        ]
    part = jnp.sum(part[0], axis=0, keepdims=True)
    own = lane // 16 == lax.broadcasted_iota(jnp.int32, (8, L), 0)

    def group(slots, offsets, member, n, value):
        slots[0] = value
        for k, o in enumerate(offsets):
            pltpu.make_async_remote_copy(
                src_ref=slots.at[0],
                dst_ref=slots.at[k + 1],
                send_sem=sum_send.at[n],
                recv_sem=sum_recv.at[n],
                device_id=member(gx, gy, o),
                device_id_type=MESH,
            ).start()

    def group_wait(slots, sem):
        others = slots.at[pl.ds(1, slots.shape[0] - 1)]
        pltpu.make_async_copy(others, others, sem).wait()

    def group_sum(slots, n):
        group_wait(slots, sum_recv.at[n])
        return jnp.sum(slots[...], axis=0)

    pl.semaphore_wait(token, len(TOKENS_A) + len(TOKENS_B))
    group(slots_a, GROUP_A, member_a, 0, part)

    def shorten(x, _):
        for h in (0, 1):
            sent[h, x] = ext[h, x + 2, 16:144, :].astype(BF16)
        return 0

    lax.fori_loop(0, X, shorten, 0)
    start(fields)

    group(slots_b, GROUP_B, member_b, 1, group_sum(slots_a, 0))

    arrive(fields)

    for h in (0, 1):
        for x in range(X + 4):
            if 2 <= x < X + 2:
                for at in (slice(0, 16), slice(144, 160)):
                    ext[h, x, at, :] = received[h, x, at, :].astype(F32)
            else:
                ext[h, x] = received[h, x].astype(F32)

    def filter_fields(x, _):
        f, x1, x2 = [[], []], [[], []], [[], []]
        for y in range(Y + 4):
            for h in (0, 1):
                at = lambda a: ext[h, x + 2 + a, 8 * y : 8 * y + 8, :]
                f[h].append(at(0))
                x1[h].append(at(-1) + at(1))
                x2[h].append(at(-2) + at(2))
        for y in range(Y):
            planes = [plane_sums(f[h][y : y + 5], x1[h][y : y + 5], x2[h][y : y + 5]) for h in (0, 1)]
            g0, g1, g2 = zip(*planes)
            for h, s in enumerate(fold_depth(g0, g1, g2, lane)):
                cone[h, x, 8 * y : 8 * y + 8, :] = s
        return 0

    lax.fori_loop(0, X, filter_fields, 0)

    leave(halos + fields)
    group_wait(slots_a, sum_send.at[0])
    group_wait(slots_b, sum_send.at[1])
    total = jnp.broadcast_to(group_sum(slots_b, 1), (8, L))
    total = jnp.sum(jnp.where(own, total, 0.0), axis=1, keepdims=True)
    elements_total = float(NX * X * NY * Y * Z)
    first, second = [], []
    for m in range(MODES):
        stiff_norm = jnp.broadcast_to(total[m : m + 1, :], (8, L))
        mass_norm = jnp.broadcast_to(total[MODES + m : MODES + m + 1, :], (8, L))
        first.append(elements_total / mass_norm)
        second.append(first[m] * (stiff_norm / mass_norm))

    def combine(x, _):
        for m in range(MODES):
            for g in (0, 1):
                for h in (0, 1):
                    stiff = cone[h, x, pl.ds(64 * g + m, 8, stride=8), :]
                    mass = cone[h, x, pl.ds(64 * g + MODES + m, 8, stride=8), :]
                    out_ref[m, x, 8 * g : 8 * g + 8, L * h : L * (h + 1)] = first[m] * stiff - second[m] * mass
        return 0

    lax.fori_loop(0, X, combine, 0)


def local(density, modes):
    return pl.pallas_call(
        kernel,
        out_shape=jax.ShapeDtypeStruct((MODES, X, Y, Z), F32),
        in_specs=[pl.BlockSpec(memory_space=pl.ANY)] * 2,
        out_specs=pl.BlockSpec(memory_space=pltpu.VMEM),
        scratch_shapes=[
            pltpu.VMEM((2, X + 4, 32, L), F32),
            pltpu.VMEM((2, X + 4, 32, L), F32),
            pltpu.VMEM((X + 1, CH, Y, Z), BF16),
            pltpu.VMEM((2, 2, 8, L), F32),
            pltpu.VMEM((2, 2, 8, L), F32),
            pltpu.VMEM((4, 8, L), F32),
            pltpu.VMEM((4, 8, L), F32),
            pltpu.VMEM((CH * X, Z), F32),
            pltpu.VMEM((CH * X, Z), BF16),
            pltpu.VMEM((CH * X + 16, Z), BF16),
            pltpu.VMEM((Z, 2 * Z), BF16),
            pltpu.VMEM((CH, 4, 9 * ZROWS, L), F32),
            pltpu.VMEM((4, 112, L), F32),
            pltpu.VMEM((2 * MODES, 2, X * Y, L), F32),
            pltpu.VMEM((5, 2, X * Y, L), F32),
            pltpu.VMEM((2, X + 4, 8 * (Y + 4), L), F32),
            pltpu.VMEM((2, X, 8 * Y, L), BF16),
            pltpu.VMEM((2, X + 4, 8 * (Y + 4), L), BF16),
            pltpu.VMEM((2, X, 8 * Y, L), F32),
            pltpu.VMEM((len(GROUP_A) + 1, 1, L), F32),
            pltpu.VMEM((len(GROUP_B) + 1, 1, L), F32),
            pltpu.SemaphoreType.DMA((2 + X,)),
            pltpu.SemaphoreType.DMA((11,)),
            pltpu.SemaphoreType.DMA((11,)),
            pltpu.SemaphoreType.DMA((8,)),
            pltpu.SemaphoreType.DMA((8,)),
            pltpu.SemaphoreType.DMA((2,)),
            pltpu.SemaphoreType.DMA((2,)),
            pltpu.SemaphoreType.REGULAR,
        ],
        compiler_params=pltpu.CompilerParams(
            collective_id=0, has_side_effects=True, vmem_limit_bytes=40 * 1024 * 1024
        ),
    )(*(pltpu.with_memory_space_constraint(a, pltpu.HBM) for a in (density, modes)))


def solution(mesh):
    return jax.shard_map(
        local,
        mesh=mesh,
        in_specs=(P("gx", "gy", None), P(None, "gx", "gy", None)),
        out_specs=P(None, "gx", "gy", None),
        check_vma=False,
    )
```

```python
import functools
import math

import jax
import jax.numpy as jnp
import numpy as np
from jax import lax
from jax.experimental import pallas as pl
from jax.experimental.pallas import tpu as pltpu
from jax.sharding import PartitionSpec as P

RADIUS = 3
BETA_SHARP = 16.0
ETA_MID = 0.5
YOUNG_MIN = 0.001
POISSON = 0.3
MESH = pl.DeviceIdType.MESH

NX, NY = 32, 16
X, Y, Z = 4, 16, 256
L = 128
MODES = 4
CH = 3 * MODES
ZROWS = 24
F32 = jnp.float32
BF16 = jnp.bfloat16

NEIGHBOURS = [(a, b) for a in (-1, 0, 1) for b in (-1, 0, 1) if (a, b) != (0, 0)]


def weight(n):
    return max(0.0, RADIUS - math.sqrt(n))


def position():
    gx, gy = lax.axis_index("gx"), lax.axis_index("gy")
    return gx, gy


def exists(gx, gy, a, b):
    inside = {-1: lambda i, n: [i > 0], 0: lambda i, n: [], 1: lambda i, n: [i < n - 1]}
    return functools.reduce(jnp.logical_and, inside[a](gx, NX) + inside[b](gy, NY))


def neighbour(gx, gy, a, b):
    return (lax.rem(gx + a + NX, NX), lax.rem(gy + b + NY, NY))


def ring(v, n):
    v %= n
    return min(v, n - v)


def hops_a(o):
    return ring(o[0], 8) + ring(o[1], 4)


def hops_b(o):
    return ring(o[0], 8)


GROUP_A = sorted(((y, x) for y in range(8) for x in range(4) if (y, x) != (0, 0)), key=lambda o: -hops_a(o))
GROUP_B = sorted(((z, c) for z in range(8) for c in range(2) if (z, c) != (0, 0)), key=lambda o: -hops_b(o))
NEAR_A = [o for o in GROUP_A if hops_a(o) <= 3]
NEAR_B = [o for o in GROUP_B if hops_b(o) <= 2]
TOKENS_A = [(2, 1), (6, 1), (2, 3)]
TOKENS_B = [(2, 0), (6, 0)]
for group, near, tokens, hops, limit in (
    (GROUP_A, NEAR_A, TOKENS_A, hops_a, 3),
    (GROUP_B, NEAR_B, TOKENS_B, hops_b, 2),
):
    assert all(t in near for t in tokens)
    assert all(o in near or any(hops((o[0] - t[0], o[1] - t[1])) <= limit for t in tokens) for o in group)


def member_a(gx, gy, o):
    y, low = gx // 4, lax.rem(gx, 4)
    high, x = gy // 4, lax.rem(gy, 4)
    return (lax.rem(y + o[0], 8) * 4 + low, high * 4 + lax.rem(x + o[1], 4))


def member_b(gx, gy, o):
    y, core = gx // 4, lax.rem(gx, 2)
    z = lax.rem(2 * (gy // 4) + lax.rem(gx // 2, 2) + o[0], 8)
    return (y * 4 + 2 * lax.rem(z, 2) + lax.rem(core + o[1], 2), (z // 2) * 4 + lax.rem(gy, 4))


def fold_depth(g0, g1, g2, lane):
    lo, hi = g0
    for k, (p, q) in ((1, g1), (2, g2)):
        p_up, q_up = pltpu.roll(p, k, 1), pltpu.roll(q, k, 1)
        p_dn, q_dn = pltpu.roll(p, L - k, 1), pltpu.roll(q, L - k, 1)
        first, last = lane < k, lane >= L - k
        lo = lo + (jnp.where(first, 0.0, p_up) + jnp.where(last, q_dn, p_dn))
        hi = hi + (jnp.where(first, p_up, q_up) + jnp.where(last, 0.0, q_dn))
    return lo, hi


def plane_sums(f, x1, x2):
    s0 = f[2]
    s1 = x1[2] + (f[1] + f[3])
    s2 = x1[1] + x1[3]
    s4 = x2[2] + (f[0] + f[4])
    s5 = (x1[0] + x1[4]) + (x2[1] + x2[3])
    s8 = x2[0] + x2[4]
    sums = ((0, s0), (1, s1), (2, s2), (4, s4), (5, s5), (8, s8))
    out = []
    for c in (0, 1, 4):
        total = None
        for n, s in sums:
            w = weight(n + c)
            if w > 0:
                total = w * s if total is None else total + w * s
        out.append(total)
    return out


def filter_density(ext, x, g, lane):
    planes = []
    for h in (0, 1):
        rows = lambda a, b: ext[h, x + 2 + a, 8 + 8 * g + b : 16 + 8 * g + b, :]
        f = [rows(0, b) for b in range(-2, 3)]
        x1 = [rows(-1, b) + rows(1, b) for b in range(-2, 3)]
        x2 = [rows(-2, b) + rows(2, b) for b in range(-2, 3)]
        planes.append(plane_sums(f, x1, x2))
    g0, g1, g2 = zip(*planes)
    return fold_depth(g0, g1, g2, lane)


def energies(t):
    lame = POISSON / ((1.0 + POISSON) * (1.0 - 2.0 * POISSON))
    shear = 1.0 / (2.0 * (1.0 + POISSON))
    sq = lambda v: v * v
    u, v, w = t
    total = lambda terms: functools.reduce(lambda p, q: p + q, terms)
    rigid = total([sq(c[0][0][0]) for c in t])
    diag = sq(u[1][0][0]) + sq(v[0][1][0]) + sq(w[0][0][1])
    first = total([sq(u[0][1][0]), sq(u[0][0][1]), sq(v[1][0][0]), sq(v[0][0][1]), sq(w[1][0][0]), sq(w[0][1][0])])
    second = total([sq(u[1][1][0]), sq(u[1][0][1]), sq(v[1][1][0]), sq(v[0][1][1]), sq(w[1][0][1]), sq(w[0][1][1])])
    other = total([sq(u[0][1][1]), sq(v[1][0][1]), sq(w[1][1][0])])
    third = total([sq(c[1][1][1]) for c in t])
    mass = rigid * (1 / 64) + (diag + first) * (1 / 192) + (second + other) * (1 / 576) + third * (1 / 1728)
    div = sq(u[1][0][0] + v[0][1][0] + w[0][0][1])
    div1 = total([sq(v[1][1][0] + w[1][0][1]), sq(u[1][1][0] + w[0][1][1]), sq(u[1][0][1] + v[0][1][1])])
    slide = total([sq(u[0][1][0] + v[1][0][0]), sq(u[0][0][1] + w[1][0][0]), sq(v[0][0][1] + w[0][1][0])])
    slide1 = total([sq(u[0][1][1] + v[1][0][1]), sq(u[0][1][1] + w[1][1][0]), sq(v[1][0][1] + w[1][1][0])])
    stiff = (
        (lame / 16) * div
        + (lame / 48) * div1
        + (shear / 8) * diag
        + (shear / 16) * slide
        + (shear / 48) * slide1
        + (shear / 16) * second
        + ((lame + 4 * shear) / 144) * third
    )
    return stiff, mass


def across(low, high):
    return [
        [
            [[low[c][j][k] + high[c][j][k] for k in (0, 1)] for j in (0, 1)],
            [[high[c][j][k] - low[c][j][k] for k in (0, 1)] for j in (0, 1)],
        ]
        for c in range(3)
    ]


def layer_of(zs, m, h, x, g):
    out = []
    for c in range(3):
        both = []
        for k in (0, 1):
            at = x * ZROWS + 8 * g
            here = zs[3 * m + c, 2 * k + h, at : at + 8, :]
            there = zs[3 * m + c, 2 * k + h, at + 1 : at + 9, :]
            both.append((here + there, there - here))
        out.append([[both[k][j] for k in (0, 1)] for j in (0, 1)])
    return out


def last_row_of(zs, yz, m, h, x):
    out = []
    for c in range(3):
        both = []
        for k in (0, 1):
            here = zs[3 * m + c, 2 * k + h, pl.ds(x * ZROWS + Y - 1, 8, stride=ZROWS), :]
            there = yz[2 * k + h, pl.ds(x * CH + 3 * m + c, 8, stride=CH), :]
            both.append((here + there, there - here))
        out.append([[both[k][j] for k in (0, 1)] for j in (0, 1)])
    return out


def kernel(
    dens_ref,
    modes_ref,
    out_ref,
    dext,
    wext,
    nodes,
    side_out,
    side_in,
    corner_out,
    corner_in,
    row0,
    first_row,
    next_row,
    zmat,
    zs,
    yz,
    forms,
    coef,
    ext,
    sent,
    received,
    cone,
    slots_a,
    slots_b,
    in_sem,
    halo_send,
    halo_recv,
    field_send,
    field_recv,
    sum_send,
    sum_recv,
    token,
):
    gx, gy = position()
    lane = lax.broadcasted_iota(jnp.int32, (8, L), 1)

    barrier = pltpu.get_barrier_semaphore()
    for a, b in NEIGHBOURS:

        @pl.when(exists(gx, gy, a, b))
        def _(a=a, b=b):
            pl.semaphore_signal(barrier, inc=1, device_id=neighbour(gx, gy, a, b), device_id_type=MESH)

    loads = [
        pltpu.make_async_copy(dens_ref.at[:, :, L * h : L * (h + 1)], dext.at[h, 2:6, 8:24, :], in_sem.at[h])
        for h in (0, 1)
    ] + [pltpu.make_async_copy(modes_ref.at[:, x], nodes.at[x], in_sem.at[2 + x]) for x in range(X)]
    for load in loads:
        load.start()

    for o in NEAR_A:
        pl.semaphore_signal(barrier, inc=1, device_id=member_a(gx, gy, o), device_id_type=MESH)
    for o in NEAR_B:
        pl.semaphore_signal(barrier, inc=1, device_id=member_b(gx, gy, o), device_id_type=MESH)

    for load in loads:
        load.wait()

    corners = [(a, b) for a in (-1, 1) for b in (-1, 1)]
    rows_from = {-1: slice(8, 10), 1: slice(22, 24)}
    for h in (0, 1):
        for s, b in enumerate((-1, 1)):
            for x in range(X):
                side_out[s, h, 2 * x : 2 * x + 2, :] = dext[h, x + 2, rows_from[b], :]
        for k, (a, b) in enumerate(corners):
            for i in (0, 1):
                x = i if a == -1 else X - 2 + i
                corner_out[k, 4 * h + 2 * i : 4 * h + 2 * i + 2, :] = dext[h, x + 2, rows_from[b], :]

    def remote(src, dst, send, recv, a, b):
        return pltpu.make_async_remote_copy(
            src_ref=src,
            dst_ref=dst,
            send_sem=send,
            recv_sem=recv,
            device_id=neighbour(gx, gy, a, b),
            device_id_type=MESH,
        )

    src_x, dst_x = {-1: (2, 2), 0: (2, 4), 1: (4, 2)}, {-1: 6, 0: 2, 1: 0}
    far = sorted(NEIGHBOURS, key=lambda o: (-abs(o[0]) - abs(o[1]), abs(o[0]), -o[0]))
    parts = [(first_row.at[0:16], next_row.at[CH * X : CH * X + 16], -1, -1)]
    parts += [(corner_out.at[k], corner_in.at[k], a, b) for k, (a, b) in enumerate(corners)]
    parts += [(side_out.at[s], side_in.at[s], 0, b) for s, b in enumerate((-1, 1))]
    parts.append((first_row, next_row.at[0 : CH * X], 0, -1))
    for a in (-1, 1):
        x0 = src_x[a][0]
        parts.append((dext.at[:, x0 : x0 + 2, 8:24, :], dext.at[:, dst_x[a] : dst_x[a] + 2, 8:24, :], a, 0))
    parts.append((nodes.at[0], nodes.at[X], -1, 0))
    halos = [(remote(src, dst, halo_send.at[i], halo_recv.at[i], a, b), a, b) for i, (src, dst, a, b) in enumerate(parts)]
    parts_f = []
    for a, b in far:
        x0, xn = src_x[a]
        y0, yn = {-1: (0, 2), 0: (0, 16), 1: (14, 2)}[b]
        y1 = {-1: 18, 0: 2, 1: 0}[b]
        parts_f.append(
            (
                sent.at[:, x0 - 2 : x0 - 2 + xn, 8 * y0 : 8 * (y0 + yn), :],
                received.at[:, dst_x[a] : dst_x[a] + xn, 8 * y1 : 8 * (y1 + yn), :],
                a,
                b,
            )
        )
    fields = [
        (remote(src, dst, field_send.at[i], field_recv.at[i], a, b), a, b) for i, (src, dst, a, b) in enumerate(parts_f)
    ]

    for _, dst, a, b in parts + parts_f:

        @pl.when(jnp.logical_not(exists(gx, gy, -a, -b)))
        def _(dst=dst):
            dst[...] = jnp.zeros(dst.shape, dst.dtype)

    def each(copies, step, sign):
        for direction in far:
            mine = [copy for copy, a, b in copies if (a, b) == direction]
            if not mine:
                continue

            @pl.when(exists(gx, gy, sign * direction[0], sign * direction[1]))
            def _(mine=mine):
                for copy in mine:
                    step(copy)

    def start(copies):
        each(copies, lambda copy: copy.start(), 1)

    def arrive(copies):
        each(copies, lambda copy: copy.wait_recv(), -1)

    def leave(copies):
        each(copies, lambda copy: copy.wait_send(), 1)

    def pack(c, _):
        for x in range(X):
            row0[pl.ds(x * CH + c, 1), :] = nodes[x, c].astype(F32)[0:1, :]
        return 0

    lax.fori_loop(0, CH, pack, 0)
    first_row[...] = row0[...].astype(BF16)

    along = lambda i, n: 1 + (i > 0).astype(jnp.int32) + (i < n - 1).astype(jnp.int32)
    pl.semaphore_wait(barrier, along(gx, NX) * along(gy, NY) - 1 + len(NEAR_A) + len(NEAR_B))

    start(halos)
    for tokens, member in ((TOKENS_A, member_a), (TOKENS_B, member_b)):
        for o in tokens:
            back = (8 - o[0], (4 if member is member_a else 2) - o[1])
            pl.semaphore_signal(token, inc=1, device_id=member(gx, gy, back), device_id_type=MESH)

    for h in (0, 1):
        for x in range(X + 4):
            ix = gx * X + (x - 2)
            inside_x = jnp.where((ix >= 0) & (ix < NX * X), 1.0, 0.0)
            iy = gy * Y - 8 + lax.broadcasted_iota(jnp.int32, (32, L), 0)
            wext[h, x] = jnp.where((iy >= 0) & (iy < NY * Y), inside_x, 0.0)

    def weights(x, _):
        for g in (0, 1):
            at = pl.ds(pl.multiple_of(x * Y + 8 * g, 8), 8)
            for h, s in enumerate(filter_density(wext, x, g, lane)):
                coef[0, h, at, :] = 1.0 / s
        return 0

    lax.fori_loop(0, X, weights, 0)

    row = lax.broadcasted_iota(jnp.int32, (Z, Z), 0)
    col = lax.broadcasted_iota(jnp.int32, (Z, Z), 1)
    here = jnp.where(row == col, 1.0, 0.0)
    there = jnp.where(row == col + 1, 1.0, 0.0)
    zmat[:, 0:Z] = (here + there).astype(BF16)
    zmat[:, Z : 2 * Z] = (there - here).astype(BF16)

    def depth(x, _):
        t = jnp.dot(nodes[x].reshape(CH * Y, Z), zmat[...], preferred_element_type=F32)
        at = pl.ds(pl.multiple_of(x * ZROWS, 8), Y)
        for c in range(CH):
            for q in range(4):
                zs[c, q, at, :] = t[c * Y : (c + 1) * Y, q * L : (q + 1) * L]
        return 0

    lax.fori_loop(0, X, depth, 0)

    def elements(x0, x1):
        def body(i, _):
            m, h = i // 2, lax.rem(i, 2)
            for g in (0, 1):
                low = layer_of(zs, m, h, x0, g)
                for x in range(x0, x1):
                    high = layer_of(zs, m, h, x + 1, g)
                    kq, mq = energies(across(low, high))
                    at = slice(x * Y + 8 * g, x * Y + 8 * g + 8)
                    forms[m, h, at, :] = kq
                    forms[MODES + m, h, at, :] = mq
                    low = high
            return 0

        lax.fori_loop(0, 2 * MODES, body, 0)

    elements(0, X - 1)

    arrive(halos[10:])
    depth(X, 0)
    elements(X - 1, X)

    def unpack(b):
        s = (b + 1) // 2
        to = {-1: slice(24, 26), 1: slice(6, 8)}[b]
        for h in (0, 1):
            for x in range(X):
                dext[h, x + 2, to, :] = side_in[s, h, 2 * x : 2 * x + 2, :]
            for k, (a, _) in enumerate(corners):
                if k % 2 == s:
                    for i in (0, 1):
                        dext[h, dst_x[a] + i, to, :] = corner_in[k, 4 * h + 2 * i : 4 * h + 2 * i + 2, :]

    top = math.tanh(BETA_SHARP * ETA_MID)
    denom = top + math.tanh(BETA_SHARP * (1.0 - ETA_MID))

    def project(g, x, _):
        at = pl.ds(pl.multiple_of(x * Y + 8 * g, 8), 8)
        for h, s in enumerate(filter_density(dext, x, g, lane)):
            share = coef[0, h, at, :]
            sharp = jnp.tanh(BETA_SHARP * (s * share - ETA_MID))
            projected = (top + sharp) * (1.0 / denom)
            slope = (BETA_SHARP / denom) * (1.0 - sharp * sharp) * share
            square = projected * projected
            coef[1, h, at, :] = YOUNG_MIN + square * projected * (1.0 - YOUNG_MIN)
            coef[2, h, at, :] = projected
            coef[3, h, at, :] = slope * (square * (3.0 * (1.0 - YOUNG_MIN)))
            coef[4, h, at, :] = slope
        return 0

    arrive(halos[8:10] + halos[6:7] + halos[2:5:2])
    unpack(1)
    lax.fori_loop(0, X, functools.partial(project, 0), 0)

    def scale(g, i, sums):
        h, x = i // X, lax.rem(i, X)
        sums = list(sums)
        at = pl.ds(pl.multiple_of(x * Y + 8 * g, 8), 8)
        young, projected, a, b = (coef[n, h, at, :] for n in range(1, 5))
        for f in range(2 * MODES):
            q = forms[f, h, at, :]
            sums[f] = sums[f] + q * (young if f < MODES else projected)
            ext[h, x + 2, pl.ds((2 + 8 * g) * 8 + f, 8, stride=8), :] = q * (a if f < MODES else b)
        return tuple(sums)

    zeros = tuple(jnp.zeros((8, L), F32) for _ in range(2 * MODES))
    sums = lax.fori_loop(0, 2 * X, functools.partial(scale, 0), zeros)

    arrive(halos[5:6] + halos[1:4:2])
    unpack(-1)
    lax.fori_loop(0, X, functools.partial(project, 1), 0)

    arrive(halos[0:1] + halos[7:8])
    t = jnp.dot(next_row[...], zmat[...], preferred_element_type=F32)
    for q in range(4):
        yz[q, 0 : CH * X + 16, :] = t[:, q * L : (q + 1) * L]

    def last_row(i, _):
        m, h = i // 2, lax.rem(i, 2)
        kq, mq = energies(across(last_row_of(zs, yz, m, h, 0), last_row_of(zs, yz, m, h, 1)))
        forms[m, h, pl.ds(Y - 1, X, stride=Y), :] = kq[0:X]
        forms[MODES + m, h, pl.ds(Y - 1, X, stride=Y), :] = mq[0:X]
        return 0

    lax.fori_loop(0, 2 * MODES, last_row, 0)

    sums = lax.fori_loop(0, 2 * X, functools.partial(scale, 1), sums)

    part = list(sums)
    for k in (64, 32, 16):
        half = len(part) // 2
        upper = lane & k != 0
        part = [
            jnp.where(upper, q + pltpu.roll(q, k, 1), p + pltpu.roll(p, L - k, 1))
            for p, q in zip(part[:half], part[half:])
        ]
    part = jnp.sum(part[0], axis=0, keepdims=True)
    own = lane // 16 == lax.broadcasted_iota(jnp.int32, (8, L), 0)

    def group(slots, offsets, member, n, value):
        slots[0] = value
        for k, o in enumerate(offsets):
            pltpu.make_async_remote_copy(
                src_ref=slots.at[0],
                dst_ref=slots.at[k + 1],
                send_sem=sum_send.at[n],
                recv_sem=sum_recv.at[n],
                device_id=member(gx, gy, o),
                device_id_type=MESH,
            ).start()

    def group_wait(slots, sem):
        others = slots.at[pl.ds(1, slots.shape[0] - 1)]
        pltpu.make_async_copy(others, others, sem).wait()

    def group_sum(slots, n):
        group_wait(slots, sum_recv.at[n])
        return jnp.sum(slots[...], axis=0)

    pl.semaphore_wait(token, len(TOKENS_A) + len(TOKENS_B))
    group(slots_a, GROUP_A, member_a, 0, part)

    def shorten(x, _):
        for h in (0, 1):
            sent[h, x] = ext[h, x + 2, 16:144, :].astype(BF16)
        return 0

    lax.fori_loop(0, X, shorten, 0)
    start(fields)

    group(slots_b, GROUP_B, member_b, 1, group_sum(slots_a, 0))

    arrive(fields)

    for h in (0, 1):
        for x in range(X + 4):
            if 2 <= x < X + 2:
                for at in (slice(0, 16), slice(144, 160)):
                    ext[h, x, at, :] = received[h, x, at, :].astype(F32)
            else:
                ext[h, x] = received[h, x].astype(F32)

    def filter_fields(x, _):
        f, x1, x2 = [[], []], [[], []], [[], []]
        for y in range(Y + 4):
            for h in (0, 1):
                at = lambda a: ext[h, x + 2 + a, 8 * y : 8 * y + 8, :]
                f[h].append(at(0))
                x1[h].append(at(-1) + at(1))
                x2[h].append(at(-2) + at(2))
        for y in range(Y):
            planes = [plane_sums(f[h][y : y + 5], x1[h][y : y + 5], x2[h][y : y + 5]) for h in (0, 1)]
            g0, g1, g2 = zip(*planes)
            for h, s in enumerate(fold_depth(g0, g1, g2, lane)):
                cone[h, x, 8 * y : 8 * y + 8, :] = s
        return 0

    lax.fori_loop(0, X, filter_fields, 0)

    leave(halos + fields)
    group_wait(slots_a, sum_send.at[0])
    group_wait(slots_b, sum_send.at[1])
    total = jnp.broadcast_to(group_sum(slots_b, 1), (8, L))
    total = jnp.sum(jnp.where(own, total, 0.0), axis=1, keepdims=True)
    elements_total = float(NX * X * NY * Y * Z)
    first, second = [], []
    for m in range(MODES):
        stiff_norm = jnp.broadcast_to(total[m : m + 1, :], (8, L))
        mass_norm = jnp.broadcast_to(total[MODES + m : MODES + m + 1, :], (8, L))
        first.append(elements_total / mass_norm)
        second.append(first[m] * (stiff_norm / mass_norm))

    def combine(x, _):
        for m in range(MODES):
            for g in (0, 1):
                for h in (0, 1):
                    stiff = cone[h, x, pl.ds(64 * g + m, 8, stride=8), :]
                    mass = cone[h, x, pl.ds(64 * g + MODES + m, 8, stride=8), :]
                    out_ref[m, x, 8 * g : 8 * g + 8, L * h : L * (h + 1)] = first[m] * stiff - second[m] * mass
        return 0

    lax.fori_loop(0, X, combine, 0)


def local(density, modes):
    return pl.pallas_call(
        kernel,
        out_shape=jax.ShapeDtypeStruct((MODES, X, Y, Z), F32),
        in_specs=[pl.BlockSpec(memory_space=pl.ANY)] * 2,
        out_specs=pl.BlockSpec(memory_space=pltpu.VMEM),
        scratch_shapes=[
            pltpu.VMEM((2, X + 4, 32, L), F32),
            pltpu.VMEM((2, X + 4, 32, L), F32),
            pltpu.VMEM((X + 1, CH, Y, Z), BF16),
            pltpu.VMEM((2, 2, 8, L), F32),
            pltpu.VMEM((2, 2, 8, L), F32),
            pltpu.VMEM((4, 8, L), F32),
            pltpu.VMEM((4, 8, L), F32),
            pltpu.VMEM((CH * X, Z), F32),
            pltpu.VMEM((CH * X, Z), BF16),
            pltpu.VMEM((CH * X + 16, Z), BF16),
            pltpu.VMEM((Z, 2 * Z), BF16),
            pltpu.VMEM((CH, 4, 9 * ZROWS, L), F32),
            pltpu.VMEM((4, 112, L), F32),
            pltpu.VMEM((2 * MODES, 2, X * Y, L), F32),
            pltpu.VMEM((5, 2, X * Y, L), F32),
            pltpu.VMEM((2, X + 4, 8 * (Y + 4), L), F32),
            pltpu.VMEM((2, X, 8 * Y, L), BF16),
            pltpu.VMEM((2, X + 4, 8 * (Y + 4), L), BF16),
            pltpu.VMEM((2, X, 8 * Y, L), F32),
            pltpu.VMEM((len(GROUP_A) + 1, 1, L), F32),
            pltpu.VMEM((len(GROUP_B) + 1, 1, L), F32),
            pltpu.SemaphoreType.DMA((2 + X,)),
            pltpu.SemaphoreType.DMA((11,)),
            pltpu.SemaphoreType.DMA((11,)),
            pltpu.SemaphoreType.DMA((8,)),
            pltpu.SemaphoreType.DMA((8,)),
            pltpu.SemaphoreType.DMA((2,)),
            pltpu.SemaphoreType.DMA((2,)),
            pltpu.SemaphoreType.REGULAR,
        ],
        compiler_params=pltpu.CompilerParams(
            collective_id=0, has_side_effects=True, vmem_limit_bytes=40 * 1024 * 1024
        ),
    )(*(pltpu.with_memory_space_constraint(a, pltpu.HBM) for a in (density, modes)))


def solution(mesh):
    return jax.shard_map(
        local,
        mesh=mesh,
        in_specs=(P("gx", "gy", None), P(None, "gx", "gy", None)),
        out_specs=P(None, "gx", "gy", None),
        check_vma=False,
    )
```

```python
import functools
import math

import jax
import jax.numpy as jnp
import numpy as np
from jax import lax
from jax.experimental import pallas as pl
from jax.experimental.pallas import tpu as pltpu
from jax.sharding import PartitionSpec as P

RADIUS = 3
BETA_SHARP = 16.0
ETA_MID = 0.5
YOUNG_MIN = 0.001
POISSON = 0.3
MESH = pl.DeviceIdType.MESH

NX, NY = 32, 16
X, Y, Z = 4, 16, 256
L = 128
MODES = 4
CH = 3 * MODES
ZROWS = 24
F32 = jnp.float32
BF16 = jnp.bfloat16

NEIGHBOURS = [(a, b) for a in (-1, 0, 1) for b in (-1, 0, 1) if (a, b) != (0, 0)]


def weight(n):
    return max(0.0, RADIUS - math.sqrt(n))


def position():
    gx, gy = lax.axis_index("gx"), lax.axis_index("gy")
    return gx, gy


def exists(gx, gy, a, b):
    inside = {-1: lambda i, n: [i > 0], 0: lambda i, n: [], 1: lambda i, n: [i < n - 1]}
    return functools.reduce(jnp.logical_and, inside[a](gx, NX) + inside[b](gy, NY))


def neighbour(gx, gy, a, b):
    return (lax.rem(gx + a + NX, NX), lax.rem(gy + b + NY, NY))


def ring(v, n):
    v %= n
    return min(v, n - v)


def hops_a(o):
    return ring(o[0], 8) + ring(o[1], 4)


def hops_b(o):
    return ring(o[0], 8)


GROUP_A = sorted(((y, x) for y in range(8) for x in range(4) if (y, x) != (0, 0)), key=lambda o: -hops_a(o))
GROUP_B = sorted(((z, c) for z in range(8) for c in range(2) if (z, c) != (0, 0)), key=lambda o: -hops_b(o))
NEAR_A = [o for o in GROUP_A if hops_a(o) <= 3]
NEAR_B = [o for o in GROUP_B if hops_b(o) <= 2]
TOKENS_A = [(2, 1), (6, 1), (2, 3)]
TOKENS_B = [(2, 0), (6, 0)]
for group, near, tokens, hops, limit in (
    (GROUP_A, NEAR_A, TOKENS_A, hops_a, 3),
    (GROUP_B, NEAR_B, TOKENS_B, hops_b, 2),
):
    assert all(t in near for t in tokens)
    assert all(o in near or any(hops((o[0] - t[0], o[1] - t[1])) <= limit for t in tokens) for o in group)


def member_a(gx, gy, o):
    y, low = gx // 4, lax.rem(gx, 4)
    high, x = gy // 4, lax.rem(gy, 4)
    return (lax.rem(y + o[0], 8) * 4 + low, high * 4 + lax.rem(x + o[1], 4))


def member_b(gx, gy, o):
    y, core = gx // 4, lax.rem(gx, 2)
    z = lax.rem(2 * (gy // 4) + lax.rem(gx // 2, 2) + o[0], 8)
    return (y * 4 + 2 * lax.rem(z, 2) + lax.rem(core + o[1], 2), (z // 2) * 4 + lax.rem(gy, 4))


def fold_depth(g0, g1, g2, lane):
    lo, hi = g0
    for k, (p, q) in ((1, g1), (2, g2)):
        p_up, q_up = pltpu.roll(p, k, 1), pltpu.roll(q, k, 1)
        p_dn, q_dn = pltpu.roll(p, L - k, 1), pltpu.roll(q, L - k, 1)
        first, last = lane < k, lane >= L - k
        lo = lo + (jnp.where(first, 0.0, p_up) + jnp.where(last, q_dn, p_dn))
        hi = hi + (jnp.where(first, p_up, q_up) + jnp.where(last, 0.0, q_dn))
    return lo, hi


def plane_sums(f, x1, x2):
    s0 = f[2]
    s1 = x1[2] + (f[1] + f[3])
    s2 = x1[1] + x1[3]
    s4 = x2[2] + (f[0] + f[4])
    s5 = (x1[0] + x1[4]) + (x2[1] + x2[3])
    s8 = x2[0] + x2[4]
    sums = ((0, s0), (1, s1), (2, s2), (4, s4), (5, s5), (8, s8))
    out = []
    for c in (0, 1, 4):
        total = None
        for n, s in sums:
            w = weight(n + c)
            if w > 0:
                total = w * s if total is None else total + w * s
        out.append(total)
    return out


def filter_density(ext, x, g, lane):
    planes = []
    for h in (0, 1):
        rows = lambda a, b: ext[h, x + 2 + a, 8 + 8 * g + b : 16 + 8 * g + b, :]
        f = [rows(0, b) for b in range(-2, 3)]
        x1 = [rows(-1, b) + rows(1, b) for b in range(-2, 3)]
        x2 = [rows(-2, b) + rows(2, b) for b in range(-2, 3)]
        planes.append(plane_sums(f, x1, x2))
    g0, g1, g2 = zip(*planes)
    return fold_depth(g0, g1, g2, lane)


def energies(t):
    lame = POISSON / ((1.0 + POISSON) * (1.0 - 2.0 * POISSON))
    shear = 1.0 / (2.0 * (1.0 + POISSON))
    sq = lambda v: v * v
    u, v, w = t
    total = lambda terms: functools.reduce(lambda p, q: p + q, terms)
    rigid = total([sq(c[0][0][0]) for c in t])
    diag = sq(u[1][0][0]) + sq(v[0][1][0]) + sq(w[0][0][1])
    first = total([sq(u[0][1][0]), sq(u[0][0][1]), sq(v[1][0][0]), sq(v[0][0][1]), sq(w[1][0][0]), sq(w[0][1][0])])
    second = total([sq(u[1][1][0]), sq(u[1][0][1]), sq(v[1][1][0]), sq(v[0][1][1]), sq(w[1][0][1]), sq(w[0][1][1])])
    other = total([sq(u[0][1][1]), sq(v[1][0][1]), sq(w[1][1][0])])
    third = total([sq(c[1][1][1]) for c in t])
    mass = rigid * (1 / 64) + (diag + first) * (1 / 192) + (second + other) * (1 / 576) + third * (1 / 1728)
    div = sq(u[1][0][0] + v[0][1][0] + w[0][0][1])
    div1 = total([sq(v[1][1][0] + w[1][0][1]), sq(u[1][1][0] + w[0][1][1]), sq(u[1][0][1] + v[0][1][1])])
    slide = total([sq(u[0][1][0] + v[1][0][0]), sq(u[0][0][1] + w[1][0][0]), sq(v[0][0][1] + w[0][1][0])])
    slide1 = total([sq(u[0][1][1] + v[1][0][1]), sq(u[0][1][1] + w[1][1][0]), sq(v[1][0][1] + w[1][1][0])])
    stiff = (
        (lame / 16) * div
        + (lame / 48) * div1
        + (shear / 8) * diag
        + (shear / 16) * slide
        + (shear / 48) * slide1
        + (shear / 16) * second
        + ((lame + 4 * shear) / 144) * third
    )
    return stiff, mass


def across(low, high):
    return [
        [
            [[low[c][j][k] + high[c][j][k] for k in (0, 1)] for j in (0, 1)],
            [[high[c][j][k] - low[c][j][k] for k in (0, 1)] for j in (0, 1)],
        ]
        for c in range(3)
    ]


def layer_of(zs, m, h, x, g):
    out = []
    for c in range(3):
        both = []
        for k in (0, 1):
            at = x * ZROWS + 8 * g
            here = zs[3 * m + c, 2 * k + h, at : at + 8, :]
            there = zs[3 * m + c, 2 * k + h, at + 1 : at + 9, :]
            both.append((here + there, there - here))
        out.append([[both[k][j] for k in (0, 1)] for j in (0, 1)])
    return out


def last_row_of(zs, yz, m, h, x):
    out = []
    for c in range(3):
        both = []
        for k in (0, 1):
            here = zs[3 * m + c, 2 * k + h, pl.ds(x * ZROWS + Y - 1, 8, stride=ZROWS), :]
            there = yz[2 * k + h, pl.ds(x * CH + 3 * m + c, 8, stride=CH), :]
            both.append((here + there, there - here))
        out.append([[both[k][j] for k in (0, 1)] for j in (0, 1)])
    return out


def kernel(
    dens_ref,
    modes_ref,
    out_ref,
    dext,
    wext,
    nodes,
    side_out,
    side_in,
    corner_out,
    corner_in,
    row0,
    first_row,
    next_row,
    zmat,
    zs,
    yz,
    forms,
    coef,
    ext,
    sent,
    received,
    cone,
    slots_a,
    slots_b,
    in_sem,
    halo_send,
    halo_recv,
    field_send,
    field_recv,
    sum_send,
    sum_recv,
    token,
):
    gx, gy = position()
    lane = lax.broadcasted_iota(jnp.int32, (8, L), 1)

    barrier = pltpu.get_barrier_semaphore()
    for a, b in NEIGHBOURS:

        @pl.when(exists(gx, gy, a, b))
        def _(a=a, b=b):
            pl.semaphore_signal(barrier, inc=1, device_id=neighbour(gx, gy, a, b), device_id_type=MESH)

    loads = [
        pltpu.make_async_copy(dens_ref.at[:, :, L * h : L * (h + 1)], dext.at[h, 2:6, 8:24, :], in_sem.at[h])
        for h in (0, 1)
    ] + [pltpu.make_async_copy(modes_ref.at[:, x], nodes.at[x], in_sem.at[2 + x]) for x in range(X)]
    for load in loads:
        load.start()

    for o in NEAR_A:
        pl.semaphore_signal(barrier, inc=1, device_id=member_a(gx, gy, o), device_id_type=MESH)
    for o in NEAR_B:
        pl.semaphore_signal(barrier, inc=1, device_id=member_b(gx, gy, o), device_id_type=MESH)

    for load in loads:
        load.wait()

    corners = [(a, b) for a in (-1, 1) for b in (-1, 1)]
    rows_from = {-1: slice(8, 10), 1: slice(22, 24)}
    for h in (0, 1):
        for s, b in enumerate((-1, 1)):
            for x in range(X):
                side_out[s, h, 2 * x : 2 * x + 2, :] = dext[h, x + 2, rows_from[b], :]
        for k, (a, b) in enumerate(corners):
            for i in (0, 1):
                x = i if a == -1 else X - 2 + i
                corner_out[k, 4 * h + 2 * i : 4 * h + 2 * i + 2, :] = dext[h, x + 2, rows_from[b], :]

    def remote(src, dst, send, recv, a, b):
        return pltpu.make_async_remote_copy(
            src_ref=src,
            dst_ref=dst,
            send_sem=send,
            recv_sem=recv,
            device_id=neighbour(gx, gy, a, b),
            device_id_type=MESH,
        )

    src_x, dst_x = {-1: (2, 2), 0: (2, 4), 1: (4, 2)}, {-1: 6, 0: 2, 1: 0}
    far = sorted(NEIGHBOURS, key=lambda o: (-abs(o[0]) - abs(o[1]), abs(o[0]), -o[0]))
    parts = [(first_row.at[0:16], next_row.at[CH * X : CH * X + 16], -1, -1)]
    parts += [(corner_out.at[k], corner_in.at[k], a, b) for k, (a, b) in enumerate(corners)]
    parts += [(side_out.at[s], side_in.at[s], 0, b) for s, b in enumerate((-1, 1))]
    parts.append((first_row, next_row.at[0 : CH * X], 0, -1))
    for a in (-1, 1):
        x0 = src_x[a][0]
        parts.append((dext.at[:, x0 : x0 + 2, 8:24, :], dext.at[:, dst_x[a] : dst_x[a] + 2, 8:24, :], a, 0))
    parts.append((nodes.at[0], nodes.at[X], -1, 0))
    halos = [(remote(src, dst, halo_send.at[i], halo_recv.at[i], a, b), a, b) for i, (src, dst, a, b) in enumerate(parts)]
    parts_f = []
    for a, b in far:
        x0, xn = src_x[a]
        y0, yn = {-1: (0, 2), 0: (0, 16), 1: (14, 2)}[b]
        y1 = {-1: 18, 0: 2, 1: 0}[b]
        parts_f.append(
            (
                sent.at[:, x0 - 2 : x0 - 2 + xn, 8 * y0 : 8 * (y0 + yn), :],
                received.at[:, dst_x[a] : dst_x[a] + xn, 8 * y1 : 8 * (y1 + yn), :],
                a,
                b,
            )
        )
    fields = [
        (remote(src, dst, field_send.at[i], field_recv.at[i], a, b), a, b) for i, (src, dst, a, b) in enumerate(parts_f)
    ]

    for _, dst, a, b in parts + parts_f:

        @pl.when(jnp.logical_not(exists(gx, gy, -a, -b)))
        def _(dst=dst):
            dst[...] = jnp.zeros(dst.shape, dst.dtype)

    def each(copies, step, sign):
        for direction in far:
            mine = [copy for copy, a, b in copies if (a, b) == direction]
            if not mine:
                continue

            @pl.when(exists(gx, gy, sign * direction[0], sign * direction[1]))
            def _(mine=mine):
                for copy in mine:
                    step(copy)

    def start(copies):
        each(copies, lambda copy: copy.start(), 1)

    def arrive(copies):
        each(copies, lambda copy: copy.wait_recv(), -1)

    def leave(copies):
        each(copies, lambda copy: copy.wait_send(), 1)

    def pack(c, _):
        for x in range(X):
            row0[pl.ds(x * CH + c, 1), :] = nodes[x, c].astype(F32)[0:1, :]
        return 0

    lax.fori_loop(0, CH, pack, 0)
    first_row[...] = row0[...].astype(BF16)

    along = lambda i, n: 1 + (i > 0).astype(jnp.int32) + (i < n - 1).astype(jnp.int32)
    pl.semaphore_wait(barrier, along(gx, NX) * along(gy, NY) - 1 + len(NEAR_A) + len(NEAR_B))

    start(halos)
    for tokens, member in ((TOKENS_A, member_a), (TOKENS_B, member_b)):
        for o in tokens:
            back = (8 - o[0], (4 if member is member_a else 2) - o[1])
            pl.semaphore_signal(token, inc=1, device_id=member(gx, gy, back), device_id_type=MESH)

    for h in (0, 1):
        for x in range(X + 4):
            ix = gx * X + (x - 2)
            inside_x = jnp.where((ix >= 0) & (ix < NX * X), 1.0, 0.0)
            iy = gy * Y - 8 + lax.broadcasted_iota(jnp.int32, (32, L), 0)
            wext[h, x] = jnp.where((iy >= 0) & (iy < NY * Y), inside_x, 0.0)

    def weights(x, _):
        for g in (0, 1):
            at = pl.ds(pl.multiple_of(x * Y + 8 * g, 8), 8)
            for h, s in enumerate(filter_density(wext, x, g, lane)):
                coef[0, h, at, :] = 1.0 / s
        return 0

    lax.fori_loop(0, X, weights, 0)

    row = lax.broadcasted_iota(jnp.int32, (Z, Z), 0)
    col = lax.broadcasted_iota(jnp.int32, (Z, Z), 1)
    here = jnp.where(row == col, 1.0, 0.0)
    there = jnp.where(row == col + 1, 1.0, 0.0)
    zmat[:, 0:Z] = (here + there).astype(BF16)
    zmat[:, Z : 2 * Z] = (there - here).astype(BF16)

    def depth(x, _):
        t = jnp.dot(nodes[x].reshape(CH * Y, Z), zmat[...], preferred_element_type=F32)
        at = pl.ds(pl.multiple_of(x * ZROWS, 8), Y)
        for c in range(CH):
            for q in range(4):
                zs[c, q, at, :] = t[c * Y : (c + 1) * Y, q * L : (q + 1) * L]
        return 0

    lax.fori_loop(0, X, depth, 0)

    def elements(x0, x1):
        def body(i, _):
            m, h = i // 2, lax.rem(i, 2)
            for g in (0, 1):
                low = layer_of(zs, m, h, x0, g)
                for x in range(x0, x1):
                    high = layer_of(zs, m, h, x + 1, g)
                    kq, mq = energies(across(low, high))
                    at = slice(x * Y + 8 * g, x * Y + 8 * g + 8)
                    forms[m, h, at, :] = kq
                    forms[MODES + m, h, at, :] = mq
                    low = high
            return 0

        lax.fori_loop(0, 2 * MODES, body, 0, unroll=2 if x1 - x0 == 1 else 1)

    elements(0, X - 1)

    arrive(halos[10:])
    depth(X, 0)
    elements(X - 1, X)

    def unpack(b):
        s = (b + 1) // 2
        to = {-1: slice(24, 26), 1: slice(6, 8)}[b]
        for h in (0, 1):
            for x in range(X):
                dext[h, x + 2, to, :] = side_in[s, h, 2 * x : 2 * x + 2, :]
            for k, (a, _) in enumerate(corners):
                if k % 2 == s:
                    for i in (0, 1):
                        dext[h, dst_x[a] + i, to, :] = corner_in[k, 4 * h + 2 * i : 4 * h + 2 * i + 2, :]

    top = math.tanh(BETA_SHARP * ETA_MID)
    denom = top + math.tanh(BETA_SHARP * (1.0 - ETA_MID))

    def project(g, x):
        at = slice(x * Y + 8 * g, x * Y + 8 * g + 8)
        for h, s in enumerate(filter_density(dext, x, g, lane)):
            share = coef[0, h, at, :]
            sharp = jnp.tanh(BETA_SHARP * (s * share - ETA_MID))
            projected = (top + sharp) * (1.0 / denom)
            slope = (BETA_SHARP / denom) * (1.0 - sharp * sharp) * share
            square = projected * projected
            coef[1, h, at, :] = YOUNG_MIN + square * projected * (1.0 - YOUNG_MIN)
            coef[2, h, at, :] = projected
            coef[3, h, at, :] = slope * (square * (3.0 * (1.0 - YOUNG_MIN)))
            coef[4, h, at, :] = slope

    arrive(halos[8:10] + halos[6:7] + halos[2:5:2])
    unpack(1)
    for x in range(X):
        project(0, x)

    def scale(g, i, sums):
        h, x = i // X, lax.rem(i, X)
        sums = list(sums)
        at = pl.ds(pl.multiple_of(x * Y + 8 * g, 8), 8)
        young, projected, a, b = (coef[n, h, at, :] for n in range(1, 5))
        for f in range(2 * MODES):
            q = forms[f, h, at, :]
            sums[f] = sums[f] + q * (young if f < MODES else projected)
            ext[h, x + 2, pl.ds((2 + 8 * g) * 8 + f, 8, stride=8), :] = q * (a if f < MODES else b)
        return tuple(sums)

    zeros = tuple(jnp.zeros((8, L), F32) for _ in range(2 * MODES))
    sums = lax.fori_loop(0, 2 * X, functools.partial(scale, 0), zeros, unroll=2)

    arrive(halos[5:6] + halos[1:4:2])
    unpack(-1)
    for x in range(X):
        project(1, x)

    arrive(halos[0:1] + halos[7:8])
    t = jnp.dot(next_row[...], zmat[...], preferred_element_type=F32)
    for q in range(4):
        yz[q, 0 : CH * X + 16, :] = t[:, q * L : (q + 1) * L]

    def last_row(i, _):
        m, h = i // 2, lax.rem(i, 2)
        kq, mq = energies(across(last_row_of(zs, yz, m, h, 0), last_row_of(zs, yz, m, h, 1)))
        forms[m, h, pl.ds(Y - 1, X, stride=Y), :] = kq[0:X]
        forms[MODES + m, h, pl.ds(Y - 1, X, stride=Y), :] = mq[0:X]
        return 0

    lax.fori_loop(0, 2 * MODES, last_row, 0, unroll=4)

    sums = lax.fori_loop(0, 2 * X, functools.partial(scale, 1), sums, unroll=2)

    part = list(sums)
    for k in (64, 32, 16):
        half = len(part) // 2
        upper = lane & k != 0
        part = [
            jnp.where(upper, q + pltpu.roll(q, k, 1), p + pltpu.roll(p, L - k, 1))
            for p, q in zip(part[:half], part[half:])
        ]
    part = jnp.sum(part[0], axis=0, keepdims=True)
    own = lane // 16 == lax.broadcasted_iota(jnp.int32, (8, L), 0)

    def group(slots, offsets, member, n, value):
        slots[0] = value
        for k, o in enumerate(offsets):
            pltpu.make_async_remote_copy(
                src_ref=slots.at[0],
                dst_ref=slots.at[k + 1],
                send_sem=sum_send.at[n],
                recv_sem=sum_recv.at[n],
                device_id=member(gx, gy, o),
                device_id_type=MESH,
            ).start()

    def group_wait(slots, sem):
        others = slots.at[pl.ds(1, slots.shape[0] - 1)]
        pltpu.make_async_copy(others, others, sem).wait()

    def group_sum(slots, n):
        group_wait(slots, sum_recv.at[n])
        return jnp.sum(slots[...], axis=0)

    pl.semaphore_wait(token, len(TOKENS_A) + len(TOKENS_B))
    group(slots_a, GROUP_A, member_a, 0, part)

    def shorten(x, _):
        for h in (0, 1):
            sent[h, x] = ext[h, x + 2, 16:144, :].astype(BF16)
        return 0

    lax.fori_loop(0, X, shorten, 0)
    start(fields)

    group(slots_b, GROUP_B, member_b, 1, group_sum(slots_a, 0))

    arrive(fields)

    for h in (0, 1):
        for x in range(X + 4):
            if 2 <= x < X + 2:
                for at in (slice(0, 16), slice(144, 160)):
                    ext[h, x, at, :] = received[h, x, at, :].astype(F32)
            else:
                ext[h, x] = received[h, x].astype(F32)

    def filter_fields(x, _):
        f, x1, x2 = [[], []], [[], []], [[], []]
        for y in range(Y + 4):
            for h in (0, 1):
                at = lambda a: ext[h, x + 2 + a, 8 * y : 8 * y + 8, :]
                f[h].append(at(0))
                x1[h].append(at(-1) + at(1))
                x2[h].append(at(-2) + at(2))
        for y in range(Y):
            planes = [plane_sums(f[h][y : y + 5], x1[h][y : y + 5], x2[h][y : y + 5]) for h in (0, 1)]
            g0, g1, g2 = zip(*planes)
            for h, s in enumerate(fold_depth(g0, g1, g2, lane)):
                cone[h, x, 8 * y : 8 * y + 8, :] = s
        return 0

    lax.fori_loop(0, X, filter_fields, 0)

    leave(halos + fields)
    group_wait(slots_a, sum_send.at[0])
    group_wait(slots_b, sum_send.at[1])
    total = jnp.broadcast_to(group_sum(slots_b, 1), (8, L))
    total = jnp.sum(jnp.where(own, total, 0.0), axis=1, keepdims=True)
    elements_total = float(NX * X * NY * Y * Z)
    first, second = [], []
    for m in range(MODES):
        stiff_norm = jnp.broadcast_to(total[m : m + 1, :], (8, L))
        mass_norm = jnp.broadcast_to(total[MODES + m : MODES + m + 1, :], (8, L))
        first.append(elements_total / mass_norm)
        second.append(first[m] * (stiff_norm / mass_norm))

    def combine(x, _):
        for m in range(MODES):
            for g in (0, 1):
                for h in (0, 1):
                    stiff = cone[h, x, pl.ds(64 * g + m, 8, stride=8), :]
                    mass = cone[h, x, pl.ds(64 * g + MODES + m, 8, stride=8), :]
                    out_ref[m, x, 8 * g : 8 * g + 8, L * h : L * (h + 1)] = first[m] * stiff - second[m] * mass
        return 0

    lax.fori_loop(0, X, combine, 0)


def local(density, modes):
    return pl.pallas_call(
        kernel,
        out_shape=jax.ShapeDtypeStruct((MODES, X, Y, Z), F32),
        in_specs=[pl.BlockSpec(memory_space=pl.ANY)] * 2,
        out_specs=pl.BlockSpec(memory_space=pltpu.VMEM),
        scratch_shapes=[
            pltpu.VMEM((2, X + 4, 32, L), F32),
            pltpu.VMEM((2, X + 4, 32, L), F32),
            pltpu.VMEM((X + 1, CH, Y, Z), BF16),
            pltpu.VMEM((2, 2, 8, L), F32),
            pltpu.VMEM((2, 2, 8, L), F32),
            pltpu.VMEM((4, 8, L), F32),
            pltpu.VMEM((4, 8, L), F32),
            pltpu.VMEM((CH * X, Z), F32),
            pltpu.VMEM((CH * X, Z), BF16),
            pltpu.VMEM((CH * X + 16, Z), BF16),
            pltpu.VMEM((Z, 2 * Z), BF16),
            pltpu.VMEM((CH, 4, 9 * ZROWS, L), F32),
            pltpu.VMEM((4, 112, L), F32),
            pltpu.VMEM((2 * MODES, 2, X * Y, L), F32),
            pltpu.VMEM((5, 2, X * Y, L), F32),
            pltpu.VMEM((2, X + 4, 8 * (Y + 4), L), F32),
            pltpu.VMEM((2, X, 8 * Y, L), BF16),
            pltpu.VMEM((2, X + 4, 8 * (Y + 4), L), BF16),
            pltpu.VMEM((2, X, 8 * Y, L), F32),
            pltpu.VMEM((len(GROUP_A) + 1, 1, L), F32),
            pltpu.VMEM((len(GROUP_B) + 1, 1, L), F32),
            pltpu.SemaphoreType.DMA((2 + X,)),
            pltpu.SemaphoreType.DMA((11,)),
            pltpu.SemaphoreType.DMA((11,)),
            pltpu.SemaphoreType.DMA((8,)),
            pltpu.SemaphoreType.DMA((8,)),
            pltpu.SemaphoreType.DMA((2,)),
            pltpu.SemaphoreType.DMA((2,)),
            pltpu.SemaphoreType.REGULAR,
        ],
        compiler_params=pltpu.CompilerParams(
            collective_id=0, has_side_effects=True, vmem_limit_bytes=40 * 1024 * 1024
        ),
    )(*(pltpu.with_memory_space_constraint(a, pltpu.HBM) for a in (density, modes)))


def solution(mesh):
    return jax.shard_map(
        local,
        mesh=mesh,
        in_specs=(P("gx", "gy", None), P(None, "gx", "gy", None)),
        out_specs=P(None, "gx", "gy", None),
        check_vma=False,
    )
```

```python
import functools
import math

import jax
import jax.numpy as jnp
import numpy as np
from jax import lax
from jax.experimental import pallas as pl
from jax.experimental.pallas import tpu as pltpu
from jax.sharding import PartitionSpec as P

RADIUS = 3
BETA_SHARP = 16.0
ETA_MID = 0.5
YOUNG_MIN = 0.001
POISSON = 0.3
MESH = pl.DeviceIdType.MESH

NX, NY = 32, 16
X, Y, Z = 4, 16, 256
L = 128
MODES = 4
CH = 3 * MODES
ZROWS = 24
F32 = jnp.float32
BF16 = jnp.bfloat16

NEIGHBOURS = [(a, b) for a in (-1, 0, 1) for b in (-1, 0, 1) if (a, b) != (0, 0)]


def weight(n):
    return max(0.0, RADIUS - math.sqrt(n))


def position():
    gx, gy = lax.axis_index("gx"), lax.axis_index("gy")
    return gx, gy


def exists(gx, gy, a, b):
    inside = {-1: lambda i, n: [i > 0], 0: lambda i, n: [], 1: lambda i, n: [i < n - 1]}
    return functools.reduce(jnp.logical_and, inside[a](gx, NX) + inside[b](gy, NY))


def neighbour(gx, gy, a, b):
    return (lax.rem(gx + a + NX, NX), lax.rem(gy + b + NY, NY))


def ring(v, n):
    v %= n
    return min(v, n - v)


def hops_a(o):
    return ring(o[0], 8) + ring(o[1], 4)


def hops_b(o):
    return ring(o[0], 8)


GROUP_A = [(y, x, c) for y in range(8) for x in range(4) for c in range(2) if (y, x, c) != (0, 0, 0)]
GROUP_A.sort(key=lambda o: -hops_a(o))
GROUP_B = sorted(((z,) for z in range(1, 8)), key=lambda o: -hops_b(o))
NEAR_A = [o for o in GROUP_A if hops_a(o) <= 3]
NEAR_B = [o for o in GROUP_B if hops_b(o) <= 2]
TOKENS_A = [(2, 1, 0), (6, 1, 0), (2, 3, 0)]
TOKENS_B = [(2,), (6,)]
for group, near, tokens, hops, limit in (
    (GROUP_A, NEAR_A, TOKENS_A, hops_a, 3),
    (GROUP_B, NEAR_B, TOKENS_B, hops_b, 2),
):
    assert all(t in near for t in tokens)
    assert all(o in near or any(hops([p - q for p, q in zip(o, t)]) <= limit for t in tokens) for o in group)


def member_a(gx, gy, o):
    y, low, core = gx // 4, lax.rem(gx // 2, 2), lax.rem(gx, 2)
    high, x = gy // 4, lax.rem(gy, 4)
    return (lax.rem(y + o[0], 8) * 4 + 2 * low + lax.rem(core + o[2], 2), high * 4 + lax.rem(x + o[1], 4))


def member_b(gx, gy, o):
    y, core = gx // 4, lax.rem(gx, 2)
    z = lax.rem(2 * (gy // 4) + lax.rem(gx // 2, 2) + o[0], 8)
    return (y * 4 + 2 * lax.rem(z, 2) + core, (z // 2) * 4 + lax.rem(gy, 4))


def fold_depth(g0, g1, g2, lane):
    lo, hi = g0
    for k, (p, q) in ((1, g1), (2, g2)):
        p_up, q_up = pltpu.roll(p, k, 1), pltpu.roll(q, k, 1)
        p_dn, q_dn = pltpu.roll(p, L - k, 1), pltpu.roll(q, L - k, 1)
        first, last = lane < k, lane >= L - k
        lo = lo + (jnp.where(first, 0.0, p_up) + jnp.where(last, q_dn, p_dn))
        hi = hi + (jnp.where(first, p_up, q_up) + jnp.where(last, 0.0, q_dn))
    return lo, hi


def plane_sums(f, x1, x2):
    s0 = f[2]
    s1 = x1[2] + (f[1] + f[3])
    s2 = x1[1] + x1[3]
    s4 = x2[2] + (f[0] + f[4])
    s5 = (x1[0] + x1[4]) + (x2[1] + x2[3])
    s8 = x2[0] + x2[4]
    sums = ((0, s0), (1, s1), (2, s2), (4, s4), (5, s5), (8, s8))
    out = []
    for c in (0, 1, 4):
        total = None
        for n, s in sums:
            w = weight(n + c)
            if w > 0:
                total = w * s if total is None else total + w * s
        out.append(total)
    return out


def filter_density(ext, x, g, lane):
    planes = []
    for h in (0, 1):
        rows = lambda a, b: ext[h, x + 2 + a, 8 + 8 * g + b : 16 + 8 * g + b, :]
        f = [rows(0, b) for b in range(-2, 3)]
        x1 = [rows(-1, b) + rows(1, b) for b in range(-2, 3)]
        x2 = [rows(-2, b) + rows(2, b) for b in range(-2, 3)]
        planes.append(plane_sums(f, x1, x2))
    g0, g1, g2 = zip(*planes)
    return fold_depth(g0, g1, g2, lane)


def energies(t):
    lame = POISSON / ((1.0 + POISSON) * (1.0 - 2.0 * POISSON))
    shear = 1.0 / (2.0 * (1.0 + POISSON))
    sq = lambda v: v * v
    u, v, w = t
    total = lambda terms: functools.reduce(lambda p, q: p + q, terms)
    rigid = total([sq(c[0][0][0]) for c in t])
    diag = sq(u[1][0][0]) + sq(v[0][1][0]) + sq(w[0][0][1])
    first = total([sq(u[0][1][0]), sq(u[0][0][1]), sq(v[1][0][0]), sq(v[0][0][1]), sq(w[1][0][0]), sq(w[0][1][0])])
    second = total([sq(u[1][1][0]), sq(u[1][0][1]), sq(v[1][1][0]), sq(v[0][1][1]), sq(w[1][0][1]), sq(w[0][1][1])])
    other = total([sq(u[0][1][1]), sq(v[1][0][1]), sq(w[1][1][0])])
    third = total([sq(c[1][1][1]) for c in t])
    mass = rigid * (1 / 64) + (diag + first) * (1 / 192) + (second + other) * (1 / 576) + third * (1 / 1728)
    div = sq(u[1][0][0] + v[0][1][0] + w[0][0][1])
    div1 = total([sq(v[1][1][0] + w[1][0][1]), sq(u[1][1][0] + w[0][1][1]), sq(u[1][0][1] + v[0][1][1])])
    slide = total([sq(u[0][1][0] + v[1][0][0]), sq(u[0][0][1] + w[1][0][0]), sq(v[0][0][1] + w[0][1][0])])
    slide1 = total([sq(u[0][1][1] + v[1][0][1]), sq(u[0][1][1] + w[1][1][0]), sq(v[1][0][1] + w[1][1][0])])
    stiff = (
        (lame / 16) * div
        + (lame / 48) * div1
        + (shear / 8) * diag
        + (shear / 16) * slide
        + (shear / 48) * slide1
        + (shear / 16) * second
        + ((lame + 4 * shear) / 144) * third
    )
    return stiff, mass


def across(low, high):
    return [
        [
            [[low[c][j][k] + high[c][j][k] for k in (0, 1)] for j in (0, 1)],
            [[high[c][j][k] - low[c][j][k] for k in (0, 1)] for j in (0, 1)],
        ]
        for c in range(3)
    ]


def layer_of(zs, m, h, x, g):
    out = []
    for c in range(3):
        both = []
        for k in (0, 1):
            at = x * ZROWS + 8 * g
            here = zs[3 * m + c, 2 * k + h, at : at + 8, :]
            there = zs[3 * m + c, 2 * k + h, at + 1 : at + 9, :]
            both.append((here + there, there - here))
        out.append([[both[k][j] for k in (0, 1)] for j in (0, 1)])
    return out


def last_row_of(zs, yz, m, h, x):
    out = []
    for c in range(3):
        both = []
        for k in (0, 1):
            here = zs[3 * m + c, 2 * k + h, pl.ds(x * ZROWS + Y - 1, 8, stride=ZROWS), :]
            there = yz[2 * k + h, pl.ds(x * CH + 3 * m + c, 8, stride=CH), :]
            both.append((here + there, there - here))
        out.append([[both[k][j] for k in (0, 1)] for j in (0, 1)])
    return out


def kernel(
    dens_ref,
    modes_ref,
    out_ref,
    dext,
    wext,
    nodes,
    side_out,
    side_in,
    corner_out,
    corner_in,
    row0,
    first_row,
    next_row,
    zmat,
    zs,
    yz,
    forms,
    coef,
    ext,
    sent,
    received,
    cone,
    slots_a,
    slots_b,
    in_sem,
    halo_send,
    halo_recv,
    field_send,
    field_recv,
    sum_send,
    sum_recv,
    token,
):
    gx, gy = position()
    lane = lax.broadcasted_iota(jnp.int32, (8, L), 1)

    barrier = pltpu.get_barrier_semaphore()
    for a, b in NEIGHBOURS:

        @pl.when(exists(gx, gy, a, b))
        def _(a=a, b=b):
            pl.semaphore_signal(barrier, inc=1, device_id=neighbour(gx, gy, a, b), device_id_type=MESH)

    loads = [
        pltpu.make_async_copy(dens_ref.at[:, :, L * h : L * (h + 1)], dext.at[h, 2:6, 8:24, :], in_sem.at[h])
        for h in (0, 1)
    ] + [pltpu.make_async_copy(modes_ref.at[:, x], nodes.at[x], in_sem.at[2 + x]) for x in range(X)]
    for load in loads:
        load.start()

    for o in NEAR_A:
        pl.semaphore_signal(barrier, inc=1, device_id=member_a(gx, gy, o), device_id_type=MESH)
    for o in NEAR_B:
        pl.semaphore_signal(barrier, inc=1, device_id=member_b(gx, gy, o), device_id_type=MESH)

    for load in loads:
        load.wait()

    corners = [(a, b) for a in (-1, 1) for b in (-1, 1)]
    rows_from = {-1: slice(8, 10), 1: slice(22, 24)}
    for h in (0, 1):
        for s, b in enumerate((-1, 1)):
            for x in range(X):
                side_out[s, h, 2 * x : 2 * x + 2, :] = dext[h, x + 2, rows_from[b], :]
        for k, (a, b) in enumerate(corners):
            for i in (0, 1):
                x = i if a == -1 else X - 2 + i
                corner_out[k, 4 * h + 2 * i : 4 * h + 2 * i + 2, :] = dext[h, x + 2, rows_from[b], :]

    def remote(src, dst, send, recv, a, b):
        return pltpu.make_async_remote_copy(
            src_ref=src,
            dst_ref=dst,
            send_sem=send,
            recv_sem=recv,
            device_id=neighbour(gx, gy, a, b),
            device_id_type=MESH,
        )

    src_x, dst_x = {-1: (2, 2), 0: (2, 4), 1: (4, 2)}, {-1: 6, 0: 2, 1: 0}
    far = sorted(NEIGHBOURS, key=lambda o: (-abs(o[0]) - abs(o[1]), abs(o[0]), -o[0]))
    parts = [(first_row.at[0:16], next_row.at[CH * X : CH * X + 16], -1, -1)]
    parts += [(corner_out.at[k], corner_in.at[k], a, b) for k, (a, b) in enumerate(corners)]
    parts += [(side_out.at[s], side_in.at[s], 0, b) for s, b in enumerate((-1, 1))]
    parts.append((first_row, next_row.at[0 : CH * X], 0, -1))
    for a in (-1, 1):
        x0 = src_x[a][0]
        parts.append((dext.at[:, x0 : x0 + 2, 8:24, :], dext.at[:, dst_x[a] : dst_x[a] + 2, 8:24, :], a, 0))
    parts.append((nodes.at[0], nodes.at[X], -1, 0))
    halos = [(remote(src, dst, halo_send.at[i], halo_recv.at[i], a, b), a, b) for i, (src, dst, a, b) in enumerate(parts)]
    parts_f = []
    for a, b in far:
        x0, xn = src_x[a]
        y0, yn = {-1: (0, 2), 0: (0, 16), 1: (14, 2)}[b]
        y1 = {-1: 18, 0: 2, 1: 0}[b]
        parts_f.append(
            (
                sent.at[:, x0 - 2 : x0 - 2 + xn, 8 * y0 : 8 * (y0 + yn), :],
                received.at[:, dst_x[a] : dst_x[a] + xn, 8 * y1 : 8 * (y1 + yn), :],
                a,
                b,
            )
        )
    fields = [
        (remote(src, dst, field_send.at[i], field_recv.at[i], a, b), a, b) for i, (src, dst, a, b) in enumerate(parts_f)
    ]

    for _, dst, a, b in parts + parts_f:

        @pl.when(jnp.logical_not(exists(gx, gy, -a, -b)))
        def _(dst=dst):
            dst[...] = jnp.zeros(dst.shape, dst.dtype)

    def each(copies, step, sign):
        for direction in far:
            mine = [copy for copy, a, b in copies if (a, b) == direction]
            if not mine:
                continue

            @pl.when(exists(gx, gy, sign * direction[0], sign * direction[1]))
            def _(mine=mine):
                for copy in mine:
                    step(copy)

    def start(copies):
        each(copies, lambda copy: copy.start(), 1)

    def arrive(copies):
        each(copies, lambda copy: copy.wait_recv(), -1)

    def leave(copies):
        each(copies, lambda copy: copy.wait_send(), 1)

    def pack(c, _):
        for x in range(X):
            row0[pl.ds(x * CH + c, 1), :] = nodes[x, c].astype(F32)[0:1, :]
        return 0

    lax.fori_loop(0, CH, pack, 0)
    first_row[...] = row0[...].astype(BF16)

    along = lambda i, n: 1 + (i > 0).astype(jnp.int32) + (i < n - 1).astype(jnp.int32)
    pl.semaphore_wait(barrier, along(gx, NX) * along(gy, NY) - 1 + len(NEAR_A) + len(NEAR_B))

    start(halos)
    for tokens, member in ((TOKENS_A, member_a), (TOKENS_B, member_b)):
        for o in tokens:
            back = [n - v for n, v in zip((8, 4, 2), o)]
            pl.semaphore_signal(token, inc=1, device_id=member(gx, gy, back), device_id_type=MESH)

    for h in (0, 1):
        for x in range(X + 4):
            ix = gx * X + (x - 2)
            inside_x = jnp.where((ix >= 0) & (ix < NX * X), 1.0, 0.0)
            iy = gy * Y - 8 + lax.broadcasted_iota(jnp.int32, (32, L), 0)
            wext[h, x] = jnp.where((iy >= 0) & (iy < NY * Y), inside_x, 0.0)

    def weights(x, _):
        for g in (0, 1):
            at = pl.ds(pl.multiple_of(x * Y + 8 * g, 8), 8)
            for h, s in enumerate(filter_density(wext, x, g, lane)):
                coef[0, h, at, :] = 1.0 / s
        return 0

    lax.fori_loop(0, X, weights, 0)

    row = lax.broadcasted_iota(jnp.int32, (Z, Z), 0)
    col = lax.broadcasted_iota(jnp.int32, (Z, Z), 1)
    here = jnp.where(row == col, 1.0, 0.0)
    there = jnp.where(row == col + 1, 1.0, 0.0)
    zmat[:, 0:Z] = (here + there).astype(BF16)
    zmat[:, Z : 2 * Z] = (there - here).astype(BF16)

    def depth(x, _):
        t = jnp.dot(nodes[x].reshape(CH * Y, Z), zmat[...], preferred_element_type=F32)
        at = pl.ds(pl.multiple_of(x * ZROWS, 8), Y)
        for c in range(CH):
            for q in range(4):
                zs[c, q, at, :] = t[c * Y : (c + 1) * Y, q * L : (q + 1) * L]
        return 0

    lax.fori_loop(0, X, depth, 0)

    def elements(x0, x1):
        def body(i, _):
            m, h = i // 2, lax.rem(i, 2)
            for g in (0, 1):
                low = layer_of(zs, m, h, x0, g)
                for x in range(x0, x1):
                    high = layer_of(zs, m, h, x + 1, g)
                    kq, mq = energies(across(low, high))
                    at = slice(x * Y + 8 * g, x * Y + 8 * g + 8)
                    forms[m, h, at, :] = kq
                    forms[MODES + m, h, at, :] = mq
                    low = high
            return 0

        lax.fori_loop(0, 2 * MODES, body, 0, unroll=2 if x1 - x0 == 1 else 1)

    elements(0, X - 1)

    arrive(halos[10:])
    depth(X, 0)
    elements(X - 1, X)

    def unpack(b):
        s = (b + 1) // 2
        to = {-1: slice(24, 26), 1: slice(6, 8)}[b]
        for h in (0, 1):
            for x in range(X):
                dext[h, x + 2, to, :] = side_in[s, h, 2 * x : 2 * x + 2, :]
            for k, (a, _) in enumerate(corners):
                if k % 2 == s:
                    for i in (0, 1):
                        dext[h, dst_x[a] + i, to, :] = corner_in[k, 4 * h + 2 * i : 4 * h + 2 * i + 2, :]

    top = math.tanh(BETA_SHARP * ETA_MID)
    denom = top + math.tanh(BETA_SHARP * (1.0 - ETA_MID))

    def project(g, x):
        at = slice(x * Y + 8 * g, x * Y + 8 * g + 8)
        for h, s in enumerate(filter_density(dext, x, g, lane)):
            share = coef[0, h, at, :]
            sharp = jnp.tanh(BETA_SHARP * (s * share - ETA_MID))
            projected = (top + sharp) * (1.0 / denom)
            slope = (BETA_SHARP / denom) * (1.0 - sharp * sharp) * share
            square = projected * projected
            coef[1, h, at, :] = YOUNG_MIN + square * projected * (1.0 - YOUNG_MIN)
            coef[2, h, at, :] = projected
            coef[3, h, at, :] = slope * (square * (3.0 * (1.0 - YOUNG_MIN)))
            coef[4, h, at, :] = slope

    arrive(halos[8:10] + halos[6:7] + halos[2:5:2])
    unpack(1)
    for x in range(X):
        project(0, x)

    def scale(g, i, sums):
        h, x = i // X, lax.rem(i, X)
        sums = list(sums)
        at = pl.ds(pl.multiple_of(x * Y + 8 * g, 8), 8)
        young, projected, a, b = (coef[n, h, at, :] for n in range(1, 5))
        for f in range(2 * MODES):
            q = forms[f, h, at, :]
            sums[f] = sums[f] + q * (young if f < MODES else projected)
            ext[h, x + 2, pl.ds((2 + 8 * g) * 8 + f, 8, stride=8), :] = q * (a if f < MODES else b)
        return tuple(sums)

    zeros = tuple(jnp.zeros((8, L), F32) for _ in range(2 * MODES))
    sums = lax.fori_loop(0, 2 * X, functools.partial(scale, 0), zeros, unroll=2)

    arrive(halos[5:6] + halos[1:4:2])
    unpack(-1)
    for x in range(X):
        project(1, x)

    arrive(halos[0:1] + halos[7:8])
    after = next_row[...].astype(F32)
    end = lax.broadcasted_iota(jnp.int32, (CH * X + 16, L), 1) == L - 1
    moved = [pltpu.roll(after[:, h * L : (h + 1) * L], L - 1, 1) for h in (0, 1)]
    moved = [jnp.where(end, moved[1], moved[0]), jnp.where(end, 0.0, moved[1])]
    for h in (0, 1):
        yz[h, 0 : CH * X + 16, :] = after[:, h * L : (h + 1) * L] + moved[h]
        yz[2 + h, 0 : CH * X + 16, :] = moved[h] - after[:, h * L : (h + 1) * L]

    def last_row(i, _):
        m, h = i // 2, lax.rem(i, 2)
        kq, mq = energies(across(last_row_of(zs, yz, m, h, 0), last_row_of(zs, yz, m, h, 1)))
        forms[m, h, pl.ds(Y - 1, X, stride=Y), :] = kq[0:X]
        forms[MODES + m, h, pl.ds(Y - 1, X, stride=Y), :] = mq[0:X]
        return 0

    lax.fori_loop(0, 2 * MODES, last_row, 0, unroll=4)

    sums = lax.fori_loop(0, 2 * X, functools.partial(scale, 1), sums, unroll=2)

    part = list(sums)
    for k in (64, 32, 16):
        half = len(part) // 2
        upper = lane & k != 0
        part = [
            jnp.where(upper, q + pltpu.roll(q, k, 1), p + pltpu.roll(p, L - k, 1))
            for p, q in zip(part[:half], part[half:])
        ]
    part = jnp.sum(part[0], axis=0, keepdims=True)
    own = lane // 16 == lax.broadcasted_iota(jnp.int32, (8, L), 0)

    def group(slots, offsets, member, n, value):
        slots[0] = value
        for k, o in enumerate(offsets):
            pltpu.make_async_remote_copy(
                src_ref=slots.at[0],
                dst_ref=slots.at[k + 1],
                send_sem=sum_send.at[n],
                recv_sem=sum_recv.at[n],
                device_id=member(gx, gy, o),
                device_id_type=MESH,
            ).start()

    def group_wait(slots, sem):
        others = slots.at[pl.ds(1, slots.shape[0] - 1)]
        pltpu.make_async_copy(others, others, sem).wait()

    def group_sum(slots, n):
        group_wait(slots, sum_recv.at[n])
        return jnp.sum(slots[...], axis=0)

    pl.semaphore_wait(token, len(TOKENS_A) + len(TOKENS_B))
    group(slots_a, GROUP_A, member_a, 0, part)

    def shorten(x, _):
        for h in (0, 1):
            sent[h, x] = ext[h, x + 2, 16:144, :].astype(BF16)
        return 0

    lax.fori_loop(0, X, shorten, 0)
    start(fields)

    group(slots_b, GROUP_B, member_b, 1, group_sum(slots_a, 0))

    arrive(fields)

    for h in (0, 1):
        for x in range(X + 4):
            if 2 <= x < X + 2:
                for at in (slice(0, 16), slice(144, 160)):
                    ext[h, x, at, :] = received[h, x, at, :].astype(F32)
            else:
                ext[h, x] = received[h, x].astype(F32)

    def filter_fields(x, _):
        f, x1, x2 = [[], []], [[], []], [[], []]
        for y in range(Y + 4):
            for h in (0, 1):
                at = lambda a: ext[h, x + 2 + a, 8 * y : 8 * y + 8, :]
                f[h].append(at(0))
                x1[h].append(at(-1) + at(1))
                x2[h].append(at(-2) + at(2))
        for y in range(Y):
            planes = [plane_sums(f[h][y : y + 5], x1[h][y : y + 5], x2[h][y : y + 5]) for h in (0, 1)]
            g0, g1, g2 = zip(*planes)
            for h, s in enumerate(fold_depth(g0, g1, g2, lane)):
                cone[h, x, 8 * y : 8 * y + 8, :] = s
        return 0

    lax.fori_loop(0, X, filter_fields, 0)

    leave(halos + fields)
    group_wait(slots_a, sum_send.at[0])
    group_wait(slots_b, sum_send.at[1])
    total = jnp.broadcast_to(group_sum(slots_b, 1), (8, L))
    total = jnp.sum(jnp.where(own, total, 0.0), axis=1, keepdims=True)
    elements_total = float(NX * X * NY * Y * Z)
    first, second = [], []
    for m in range(MODES):
        stiff_norm = jnp.broadcast_to(total[m : m + 1, :], (8, L))
        mass_norm = jnp.broadcast_to(total[MODES + m : MODES + m + 1, :], (8, L))
        first.append(elements_total / mass_norm)
        second.append(first[m] * (stiff_norm / mass_norm))

    def combine(x, _):
        for m in range(MODES):
            for g in (0, 1):
                for h in (0, 1):
                    stiff = cone[h, x, pl.ds(64 * g + m, 8, stride=8), :]
                    mass = cone[h, x, pl.ds(64 * g + MODES + m, 8, stride=8), :]
                    out_ref[m, x, 8 * g : 8 * g + 8, L * h : L * (h + 1)] = first[m] * stiff - second[m] * mass
        return 0

    lax.fori_loop(0, X, combine, 0, unroll=2)


def local(density, modes):
    return pl.pallas_call(
        kernel,
        out_shape=jax.ShapeDtypeStruct((MODES, X, Y, Z), F32),
        in_specs=[pl.BlockSpec(memory_space=pl.ANY)] * 2,
        out_specs=pl.BlockSpec(memory_space=pltpu.VMEM),
        scratch_shapes=[
            pltpu.VMEM((2, X + 4, 32, L), F32),
            pltpu.VMEM((2, X + 4, 32, L), F32),
            pltpu.VMEM((X + 1, CH, Y, Z), BF16),
            pltpu.VMEM((2, 2, 8, L), F32),
            pltpu.VMEM((2, 2, 8, L), F32),
            pltpu.VMEM((4, 8, L), F32),
            pltpu.VMEM((4, 8, L), F32),
            pltpu.VMEM((CH * X, Z), F32),
            pltpu.VMEM((CH * X, Z), BF16),
            pltpu.VMEM((CH * X + 16, Z), BF16),
            pltpu.VMEM((Z, 2 * Z), BF16),
            pltpu.VMEM((CH, 4, 9 * ZROWS, L), F32),
            pltpu.VMEM((4, 112, L), F32),
            pltpu.VMEM((2 * MODES, 2, X * Y, L), F32),
            pltpu.VMEM((5, 2, X * Y, L), F32),
            pltpu.VMEM((2, X + 4, 8 * (Y + 4), L), F32),
            pltpu.VMEM((2, X, 8 * Y, L), BF16),
            pltpu.VMEM((2, X + 4, 8 * (Y + 4), L), BF16),
            pltpu.VMEM((2, X, 8 * Y, L), F32),
            pltpu.VMEM((len(GROUP_A) + 1, 1, L), F32),
            pltpu.VMEM((len(GROUP_B) + 1, 1, L), F32),
            pltpu.SemaphoreType.DMA((2 + X,)),
            pltpu.SemaphoreType.DMA((11,)),
            pltpu.SemaphoreType.DMA((11,)),
            pltpu.SemaphoreType.DMA((8,)),
            pltpu.SemaphoreType.DMA((8,)),
            pltpu.SemaphoreType.DMA((2,)),
            pltpu.SemaphoreType.DMA((2,)),
            pltpu.SemaphoreType.REGULAR,
        ],
        compiler_params=pltpu.CompilerParams(
            collective_id=0, has_side_effects=True, vmem_limit_bytes=40 * 1024 * 1024
        ),
    )(*(pltpu.with_memory_space_constraint(a, pltpu.HBM) for a in (density, modes)))


def solution(mesh):
    return jax.shard_map(
        local,
        mesh=mesh,
        in_specs=(P("gx", "gy", None), P(None, "gx", "gy", None)),
        out_specs=P(None, "gx", "gy", None),
        check_vma=False,
    )
```

```python
import functools
import math

import jax
import jax.numpy as jnp
import numpy as np
from jax import lax
from jax.experimental import pallas as pl
from jax.experimental.pallas import tpu as pltpu
from jax.sharding import PartitionSpec as P

RADIUS = 3
BETA_SHARP = 16.0
ETA_MID = 0.5
YOUNG_MIN = 0.001
POISSON = 0.3
MESH = pl.DeviceIdType.MESH

NX, NY = 32, 16
X, Y, Z = 4, 16, 256
L = 128
MODES = 4
CH = 3 * MODES
ZROWS = 24
F32 = jnp.float32
BF16 = jnp.bfloat16

NEIGHBOURS = [(a, b) for a in (-1, 0, 1) for b in (-1, 0, 1) if (a, b) != (0, 0)]


def weight(n):
    return max(0.0, RADIUS - math.sqrt(n))


def position():
    gx, gy = lax.axis_index("gx"), lax.axis_index("gy")
    return gx, gy


def exists(gx, gy, a, b):
    inside = {-1: lambda i, n: [i > 0], 0: lambda i, n: [], 1: lambda i, n: [i < n - 1]}
    return functools.reduce(jnp.logical_and, inside[a](gx, NX) + inside[b](gy, NY))


def neighbour(gx, gy, a, b):
    return (lax.rem(gx + a + NX, NX), lax.rem(gy + b + NY, NY))


def ring(v, n):
    v %= n
    return min(v, n - v)


def hops_a(o):
    return ring(o[0], 8) + ring(o[1], 4)


def hops_b(o):
    return ring(o[0], 8)


GROUP_A = [(y, x, c) for y in range(8) for x in range(4) for c in range(2) if (y, x, c) != (0, 0, 0)]
GROUP_A.sort(key=lambda o: -hops_a(o))
GROUP_B = sorted(((z,) for z in range(1, 8)), key=lambda o: -hops_b(o))
NEAR_A = [o for o in GROUP_A if hops_a(o) <= 3]
NEAR_B = [o for o in GROUP_B if hops_b(o) <= 2]
TOKENS_A = [(2, 1, 0), (6, 1, 0), (2, 3, 0)]
TOKENS_B = [(2,), (6,)]
for group, near, tokens, hops, limit in (
    (GROUP_A, NEAR_A, TOKENS_A, hops_a, 3),
    (GROUP_B, NEAR_B, TOKENS_B, hops_b, 2),
):
    assert all(t in near for t in tokens)
    assert all(o in near or any(hops([p - q for p, q in zip(o, t)]) <= limit for t in tokens) for o in group)


def member_a(gx, gy, o):
    y, low, core = gx // 4, lax.rem(gx // 2, 2), lax.rem(gx, 2)
    high, x = gy // 4, lax.rem(gy, 4)
    return (lax.rem(y + o[0], 8) * 4 + 2 * low + lax.rem(core + o[2], 2), high * 4 + lax.rem(x + o[1], 4))


def member_b(gx, gy, o):
    y, core = gx // 4, lax.rem(gx, 2)
    z = lax.rem(2 * (gy // 4) + lax.rem(gx // 2, 2) + o[0], 8)
    return (y * 4 + 2 * lax.rem(z, 2) + core, (z // 2) * 4 + lax.rem(gy, 4))


def fold_depth(g0, g1, g2, lane):
    lo, hi = g0
    for k, (p, q) in ((1, g1), (2, g2)):
        p_up, q_up = pltpu.roll(p, k, 1), pltpu.roll(q, k, 1)
        p_dn, q_dn = pltpu.roll(p, L - k, 1), pltpu.roll(q, L - k, 1)
        first, last = lane < k, lane >= L - k
        lo = lo + (jnp.where(first, 0.0, p_up) + jnp.where(last, q_dn, p_dn))
        hi = hi + (jnp.where(first, p_up, q_up) + jnp.where(last, 0.0, q_dn))
    return lo, hi


def plane_sums(f, x1, x2):
    s0 = f[2]
    s1 = x1[2] + (f[1] + f[3])
    s2 = x1[1] + x1[3]
    s4 = x2[2] + (f[0] + f[4])
    s5 = (x1[0] + x1[4]) + (x2[1] + x2[3])
    s8 = x2[0] + x2[4]
    sums = ((0, s0), (1, s1), (2, s2), (4, s4), (5, s5), (8, s8))
    out = []
    for c in (0, 1, 4):
        total = None
        for n, s in sums:
            w = weight(n + c)
            if w > 0:
                total = w * s if total is None else total + w * s
        out.append(total)
    return out


def filter_density(ext, x, g, lane):
    planes = []
    for h in (0, 1):
        rows = lambda a, b: ext[h, x + 2 + a, 8 + 8 * g + b : 16 + 8 * g + b, :]
        f = [rows(0, b) for b in range(-2, 3)]
        x1 = [rows(-1, b) + rows(1, b) for b in range(-2, 3)]
        x2 = [rows(-2, b) + rows(2, b) for b in range(-2, 3)]
        planes.append(plane_sums(f, x1, x2))
    g0, g1, g2 = zip(*planes)
    return fold_depth(g0, g1, g2, lane)


def energies(t):
    lame = POISSON / ((1.0 + POISSON) * (1.0 - 2.0 * POISSON))
    shear = 1.0 / (2.0 * (1.0 + POISSON))
    sq = lambda v: v * v
    u, v, w = t
    total = lambda terms: functools.reduce(lambda p, q: p + q, terms)
    rigid = total([sq(c[0][0][0]) for c in t])
    diag = sq(u[1][0][0]) + sq(v[0][1][0]) + sq(w[0][0][1])
    first = total([sq(u[0][1][0]), sq(u[0][0][1]), sq(v[1][0][0]), sq(v[0][0][1]), sq(w[1][0][0]), sq(w[0][1][0])])
    second = total([sq(u[1][1][0]), sq(u[1][0][1]), sq(v[1][1][0]), sq(v[0][1][1]), sq(w[1][0][1]), sq(w[0][1][1])])
    other = total([sq(u[0][1][1]), sq(v[1][0][1]), sq(w[1][1][0])])
    third = total([sq(c[1][1][1]) for c in t])
    mass = rigid * (1 / 64) + (diag + first) * (1 / 192) + (second + other) * (1 / 576) + third * (1 / 1728)
    div = sq(u[1][0][0] + v[0][1][0] + w[0][0][1])
    div1 = total([sq(v[1][1][0] + w[1][0][1]), sq(u[1][1][0] + w[0][1][1]), sq(u[1][0][1] + v[0][1][1])])
    slide = total([sq(u[0][1][0] + v[1][0][0]), sq(u[0][0][1] + w[1][0][0]), sq(v[0][0][1] + w[0][1][0])])
    slide1 = total([sq(u[0][1][1] + v[1][0][1]), sq(u[0][1][1] + w[1][1][0]), sq(v[1][0][1] + w[1][1][0])])
    stiff = (
        (lame / 16) * div
        + (lame / 48) * div1
        + (shear / 8) * diag
        + (shear / 16) * slide
        + (shear / 48) * slide1
        + (shear / 16) * second
        + ((lame + 4 * shear) / 144) * third
    )
    return stiff, mass


def across(low, high):
    return [
        [
            [[low[c][j][k] + high[c][j][k] for k in (0, 1)] for j in (0, 1)],
            [[high[c][j][k] - low[c][j][k] for k in (0, 1)] for j in (0, 1)],
        ]
        for c in range(3)
    ]


def layer_of(zs, m, h, x, g):
    out = []
    for c in range(3):
        both = []
        for k in (0, 1):
            at = x * ZROWS + 8 * g
            here = zs[3 * m + c, 2 * k + h, at : at + 8, :]
            there = zs[3 * m + c, 2 * k + h, at + 1 : at + 9, :]
            both.append((here + there, there - here))
        out.append([[both[k][j] for k in (0, 1)] for j in (0, 1)])
    return out


def last_row_of(zs, yz, m, h, x):
    out = []
    for c in range(3):
        both = []
        for k in (0, 1):
            here = zs[3 * m + c, 2 * k + h, pl.ds(x * ZROWS + Y - 1, 8, stride=ZROWS), :]
            there = yz[2 * k + h, pl.ds(x * CH + 3 * m + c, 8, stride=CH), :]
            both.append((here + there, there - here))
        out.append([[both[k][j] for k in (0, 1)] for j in (0, 1)])
    return out


def kernel(
    dens_ref,
    modes_ref,
    out_ref,
    dext,
    wext,
    nodes,
    side_out,
    side_in,
    corner_out,
    corner_in,
    row0,
    first_row,
    next_row,
    zmat,
    zs,
    yz,
    forms,
    coef,
    ext,
    sent,
    received,
    cone,
    slots_a,
    slots_b,
    in_sem,
    halo_send,
    halo_recv,
    field_send,
    field_recv,
    sum_send,
    sum_recv,
    token,
):
    gx, gy = position()
    lane = lax.broadcasted_iota(jnp.int32, (8, L), 1)

    barrier = pltpu.get_barrier_semaphore()
    for a, b in NEIGHBOURS:

        @pl.when(exists(gx, gy, a, b))
        def _(a=a, b=b):
            pl.semaphore_signal(barrier, inc=1, device_id=neighbour(gx, gy, a, b), device_id_type=MESH)

    loads = [
        pltpu.make_async_copy(dens_ref.at[:, :, L * h : L * (h + 1)], dext.at[h, 2:6, 8:24, :], in_sem.at[h])
        for h in (0, 1)
    ] + [pltpu.make_async_copy(modes_ref.at[:, x], nodes.at[x], in_sem.at[2 + x]) for x in range(X)]
    for load in loads:
        load.start()

    for o in NEAR_A:
        pl.semaphore_signal(barrier, inc=1, device_id=member_a(gx, gy, o), device_id_type=MESH)
    for o in NEAR_B:
        pl.semaphore_signal(barrier, inc=1, device_id=member_b(gx, gy, o), device_id_type=MESH)

    for load in loads:
        load.wait()

    corners = [(a, b) for a in (-1, 1) for b in (-1, 1)]
    rows_from = {-1: slice(8, 10), 1: slice(22, 24)}
    for h in (0, 1):
        for s, b in enumerate((-1, 1)):
            for x in range(X):
                side_out[s, h, 2 * x : 2 * x + 2, :] = dext[h, x + 2, rows_from[b], :]
        for k, (a, b) in enumerate(corners):
            for i in (0, 1):
                x = i if a == -1 else X - 2 + i
                corner_out[k, 4 * h + 2 * i : 4 * h + 2 * i + 2, :] = dext[h, x + 2, rows_from[b], :]

    def remote(src, dst, send, recv, a, b):
        return pltpu.make_async_remote_copy(
            src_ref=src,
            dst_ref=dst,
            send_sem=send,
            recv_sem=recv,
            device_id=neighbour(gx, gy, a, b),
            device_id_type=MESH,
        )

    src_x, dst_x = {-1: (2, 2), 0: (2, 4), 1: (4, 2)}, {-1: 6, 0: 2, 1: 0}
    far = sorted(NEIGHBOURS, key=lambda o: (-abs(o[0]) - abs(o[1]), abs(o[0]), -o[0]))
    parts = [(first_row.at[0:16], next_row.at[CH * X : CH * X + 16], -1, -1)]
    parts += [(corner_out.at[k], corner_in.at[k], a, b) for k, (a, b) in enumerate(corners)]
    parts += [(side_out.at[s], side_in.at[s], 0, b) for s, b in enumerate((-1, 1))]
    parts.append((first_row, next_row.at[0 : CH * X], 0, -1))
    for a in (-1, 1):
        x0 = src_x[a][0]
        parts.append((dext.at[:, x0 : x0 + 2, 8:24, :], dext.at[:, dst_x[a] : dst_x[a] + 2, 8:24, :], a, 0))
    parts.append((nodes.at[0], nodes.at[X], -1, 0))
    halos = [(remote(src, dst, halo_send.at[i], halo_recv.at[i], a, b), a, b) for i, (src, dst, a, b) in enumerate(parts)]
    parts_f = []
    for a, b in far:
        x0, xn = src_x[a]
        y0, yn = {-1: (0, 2), 0: (0, 16), 1: (14, 2)}[b]
        y1 = {-1: 18, 0: 2, 1: 0}[b]
        parts_f.append(
            (
                sent.at[:, x0 - 2 : x0 - 2 + xn, 8 * y0 : 8 * (y0 + yn), :],
                received.at[:, dst_x[a] : dst_x[a] + xn, 8 * y1 : 8 * (y1 + yn), :],
                a,
                b,
            )
        )
    fields = [
        (remote(src, dst, field_send.at[i], field_recv.at[i], a, b), a, b) for i, (src, dst, a, b) in enumerate(parts_f)
    ]

    for _, dst, a, b in parts + parts_f:

        @pl.when(jnp.logical_not(exists(gx, gy, -a, -b)))
        def _(dst=dst):
            dst[...] = jnp.zeros(dst.shape, dst.dtype)

    def each(copies, step, sign):
        for direction in far:
            mine = [copy for copy, a, b in copies if (a, b) == direction]
            if not mine:
                continue

            @pl.when(exists(gx, gy, sign * direction[0], sign * direction[1]))
            def _(mine=mine):
                for copy in mine:
                    step(copy)

    def start(copies):
        each(copies, lambda copy: copy.start(), 1)

    def arrive(copies):
        each(copies, lambda copy: copy.wait_recv(), -1)

    def leave(copies):
        each(copies, lambda copy: copy.wait_send(), 1)

    def pack(c, _):
        for x in range(X):
            row0[pl.ds(x * CH + c, 1), :] = nodes[x, c].astype(F32)[0:1, :]
        return 0

    lax.fori_loop(0, CH, pack, 0)
    first_row[...] = row0[...].astype(BF16)

    along = lambda i, n: 1 + (i > 0).astype(jnp.int32) + (i < n - 1).astype(jnp.int32)
    pl.semaphore_wait(barrier, along(gx, NX) * along(gy, NY) - 1 + len(NEAR_A) + len(NEAR_B))

    start(halos)
    for tokens, member in ((TOKENS_A, member_a), (TOKENS_B, member_b)):
        for o in tokens:
            back = [n - v for n, v in zip((8, 4, 2), o)]
            pl.semaphore_signal(token, inc=1, device_id=member(gx, gy, back), device_id_type=MESH)

    for h in (0, 1):
        for x in range(X + 4):
            ix = gx * X + (x - 2)
            inside_x = jnp.where((ix >= 0) & (ix < NX * X), 1.0, 0.0)
            iy = gy * Y - 8 + lax.broadcasted_iota(jnp.int32, (32, L), 0)
            wext[h, x] = jnp.where((iy >= 0) & (iy < NY * Y), inside_x, 0.0)

    def weights(x, _):
        for g in (0, 1):
            at = pl.ds(pl.multiple_of(x * Y + 8 * g, 8), 8)
            for h, s in enumerate(filter_density(wext, x, g, lane)):
                coef[0, h, at, :] = 1.0 / s
        return 0

    lax.fori_loop(0, X, weights, 0)

    row = lax.broadcasted_iota(jnp.int32, (Z, Z), 0)
    col = lax.broadcasted_iota(jnp.int32, (Z, Z), 1)
    here = jnp.where(row == col, 1.0, 0.0)
    there = jnp.where(row == col + 1, 1.0, 0.0)
    zmat[:, 0:Z] = (here + there).astype(BF16)
    zmat[:, Z : 2 * Z] = (there - here).astype(BF16)

    def depth(x, _):
        t = jnp.dot(nodes[x].reshape(CH * Y, Z), zmat[...], preferred_element_type=F32)
        at = pl.ds(pl.multiple_of(x * ZROWS, 8), Y)
        for c in range(CH):
            for q in range(4):
                zs[c, q, at, :] = t[c * Y : (c + 1) * Y, q * L : (q + 1) * L]
        return 0

    lax.fori_loop(0, X, depth, 0)

    def elements(x0, x1):
        def body(i, _):
            m, h = i // 2, lax.rem(i, 2)
            for g in (0, 1):
                low = layer_of(zs, m, h, x0, g)
                for x in range(x0, x1):
                    high = layer_of(zs, m, h, x + 1, g)
                    kq, mq = energies(across(low, high))
                    at = slice(x * Y + 8 * g, x * Y + 8 * g + 8)
                    forms[m, h, at, :] = kq
                    forms[MODES + m, h, at, :] = mq
                    low = high
            return 0

        lax.fori_loop(0, 2 * MODES, body, 0, unroll=4 if x1 - x0 == 1 else 1)

    elements(0, X - 1)

    arrive(halos[10:])
    depth(X, 0)
    elements(X - 1, X)

    def unpack(b):
        s = (b + 1) // 2
        to = {-1: slice(24, 26), 1: slice(6, 8)}[b]
        for h in (0, 1):
            for x in range(X):
                dext[h, x + 2, to, :] = side_in[s, h, 2 * x : 2 * x + 2, :]
            for k, (a, _) in enumerate(corners):
                if k % 2 == s:
                    for i in (0, 1):
                        dext[h, dst_x[a] + i, to, :] = corner_in[k, 4 * h + 2 * i : 4 * h + 2 * i + 2, :]

    top = math.tanh(BETA_SHARP * ETA_MID)
    denom = top + math.tanh(BETA_SHARP * (1.0 - ETA_MID))

    def project(g, x):
        at = slice(x * Y + 8 * g, x * Y + 8 * g + 8)
        for h, s in enumerate(filter_density(dext, x, g, lane)):
            share = coef[0, h, at, :]
            sharp = jnp.tanh(BETA_SHARP * (s * share - ETA_MID))
            projected = (top + sharp) * (1.0 / denom)
            slope = (BETA_SHARP / denom) * (1.0 - sharp * sharp) * share
            square = projected * projected
            coef[1, h, at, :] = YOUNG_MIN + square * projected * (1.0 - YOUNG_MIN)
            coef[2, h, at, :] = projected
            coef[3, h, at, :] = slope * (square * (3.0 * (1.0 - YOUNG_MIN)))
            coef[4, h, at, :] = slope

    arrive(halos[8:10] + halos[6:7] + halos[2:5:2])
    unpack(1)
    for x in range(X):
        project(0, x)

    def scale(g, i, sums):
        h, x = i // X, lax.rem(i, X)
        sums = list(sums)
        at = pl.ds(pl.multiple_of(x * Y + 8 * g, 8), 8)
        young, projected, a, b = (coef[n, h, at, :] for n in range(1, 5))
        for f in range(2 * MODES):
            q = forms[f, h, at, :]
            sums[f] = sums[f] + q * (young if f < MODES else projected)
            ext[h, x + 2, pl.ds((2 + 8 * g) * 8 + f, 8, stride=8), :] = q * (a if f < MODES else b)
        return tuple(sums)

    zeros = tuple(jnp.zeros((8, L), F32) for _ in range(2 * MODES))
    sums = lax.fori_loop(0, 2 * X, functools.partial(scale, 0), zeros, unroll=4)

    arrive(halos[5:6] + halos[1:4:2])
    unpack(-1)
    for x in range(X):
        project(1, x)

    arrive(halos[0:1] + halos[7:8])
    after = next_row[...].astype(F32)
    end = lax.broadcasted_iota(jnp.int32, (CH * X + 16, L), 1) == L - 1
    moved = [pltpu.roll(after[:, h * L : (h + 1) * L], L - 1, 1) for h in (0, 1)]
    moved = [jnp.where(end, moved[1], moved[0]), jnp.where(end, 0.0, moved[1])]
    for h in (0, 1):
        yz[h, 0 : CH * X + 16, :] = after[:, h * L : (h + 1) * L] + moved[h]
        yz[2 + h, 0 : CH * X + 16, :] = moved[h] - after[:, h * L : (h + 1) * L]

    def last_row(i, _):
        m, h = i // 2, lax.rem(i, 2)
        kq, mq = energies(across(last_row_of(zs, yz, m, h, 0), last_row_of(zs, yz, m, h, 1)))
        forms[m, h, pl.ds(Y - 1, X, stride=Y), :] = kq[0:X]
        forms[MODES + m, h, pl.ds(Y - 1, X, stride=Y), :] = mq[0:X]
        return 0

    lax.fori_loop(0, 2 * MODES, last_row, 0, unroll=8)

    sums = lax.fori_loop(0, 2 * X, functools.partial(scale, 1), sums, unroll=4)

    part = list(sums)
    for k in (64, 32, 16):
        half = len(part) // 2
        upper = lane & k != 0
        part = [
            jnp.where(upper, q + pltpu.roll(q, k, 1), p + pltpu.roll(p, L - k, 1))
            for p, q in zip(part[:half], part[half:])
        ]
    part = jnp.sum(part[0], axis=0, keepdims=True)
    own = lane // 16 == lax.broadcasted_iota(jnp.int32, (8, L), 0)

    def group(slots, offsets, member, n, value):
        slots[0] = value
        for k, o in enumerate(offsets):
            pltpu.make_async_remote_copy(
                src_ref=slots.at[0],
                dst_ref=slots.at[k + 1],
                send_sem=sum_send.at[n],
                recv_sem=sum_recv.at[n],
                device_id=member(gx, gy, o),
                device_id_type=MESH,
            ).start()

    def group_wait(slots, sem):
        others = slots.at[pl.ds(1, slots.shape[0] - 1)]
        pltpu.make_async_copy(others, others, sem).wait()

    def group_sum(slots, n):
        group_wait(slots, sum_recv.at[n])
        return jnp.sum(slots[...], axis=0)

    pl.semaphore_wait(token, len(TOKENS_A) + len(TOKENS_B))
    group(slots_a, GROUP_A, member_a, 0, part)

    def shorten(x, _):
        for h in (0, 1):
            sent[h, x] = ext[h, x + 2, 16:144, :].astype(BF16)
        return 0

    lax.fori_loop(0, X, shorten, 0)
    start(fields)

    group(slots_b, GROUP_B, member_b, 1, group_sum(slots_a, 0))

    arrive(fields)

    for h in (0, 1):
        for x in range(X + 4):
            if 2 <= x < X + 2:
                for at in (slice(0, 16), slice(144, 160)):
                    ext[h, x, at, :] = received[h, x, at, :].astype(F32)
            else:
                ext[h, x] = received[h, x].astype(F32)

    def filter_fields(x, _):
        f, x1, x2 = [[], []], [[], []], [[], []]
        for y in range(Y + 4):
            for h in (0, 1):
                at = lambda a: ext[h, x + 2 + a, 8 * y : 8 * y + 8, :]
                f[h].append(at(0))
                x1[h].append(at(-1) + at(1))
                x2[h].append(at(-2) + at(2))
        for y in range(Y):
            planes = [plane_sums(f[h][y : y + 5], x1[h][y : y + 5], x2[h][y : y + 5]) for h in (0, 1)]
            g0, g1, g2 = zip(*planes)
            for h, s in enumerate(fold_depth(g0, g1, g2, lane)):
                cone[h, x, 8 * y : 8 * y + 8, :] = s
        return 0

    lax.fori_loop(0, X, filter_fields, 0)

    leave(halos + fields)
    group_wait(slots_a, sum_send.at[0])
    group_wait(slots_b, sum_send.at[1])
    total = jnp.broadcast_to(group_sum(slots_b, 1), (8, L))
    total = jnp.sum(jnp.where(own, total, 0.0), axis=1, keepdims=True)
    elements_total = float(NX * X * NY * Y * Z)
    first, second = [], []
    for m in range(MODES):
        stiff_norm = jnp.broadcast_to(total[m : m + 1, :], (8, L))
        mass_norm = jnp.broadcast_to(total[MODES + m : MODES + m + 1, :], (8, L))
        first.append(elements_total / mass_norm)
        second.append(first[m] * (stiff_norm / mass_norm))

    def combine(x, _):
        for m in range(MODES):
            for g in (0, 1):
                for h in (0, 1):
                    stiff = cone[h, x, pl.ds(64 * g + m, 8, stride=8), :]
                    mass = cone[h, x, pl.ds(64 * g + MODES + m, 8, stride=8), :]
                    out_ref[m, x, 8 * g : 8 * g + 8, L * h : L * (h + 1)] = first[m] * stiff - second[m] * mass
        return 0

    lax.fori_loop(0, X, combine, 0, unroll=4)


def local(density, modes):
    return pl.pallas_call(
        kernel,
        out_shape=jax.ShapeDtypeStruct((MODES, X, Y, Z), F32),
        in_specs=[pl.BlockSpec(memory_space=pl.ANY)] * 2,
        out_specs=pl.BlockSpec(memory_space=pltpu.VMEM),
        scratch_shapes=[
            pltpu.VMEM((2, X + 4, 32, L), F32),
            pltpu.VMEM((2, X + 4, 32, L), F32),
            pltpu.VMEM((X + 1, CH, Y, Z), BF16),
            pltpu.VMEM((2, 2, 8, L), F32),
            pltpu.VMEM((2, 2, 8, L), F32),
            pltpu.VMEM((4, 8, L), F32),
            pltpu.VMEM((4, 8, L), F32),
            pltpu.VMEM((CH * X, Z), F32),
            pltpu.VMEM((CH * X, Z), BF16),
            pltpu.VMEM((CH * X + 16, Z), BF16),
            pltpu.VMEM((Z, 2 * Z), BF16),
            pltpu.VMEM((CH, 4, 9 * ZROWS, L), F32),
            pltpu.VMEM((4, 112, L), F32),
            pltpu.VMEM((2 * MODES, 2, X * Y, L), F32),
            pltpu.VMEM((5, 2, X * Y, L), F32),
            pltpu.VMEM((2, X + 4, 8 * (Y + 4), L), F32),
            pltpu.VMEM((2, X, 8 * Y, L), BF16),
            pltpu.VMEM((2, X + 4, 8 * (Y + 4), L), BF16),
            pltpu.VMEM((2, X, 8 * Y, L), F32),
            pltpu.VMEM((len(GROUP_A) + 1, 1, L), F32),
            pltpu.VMEM((len(GROUP_B) + 1, 1, L), F32),
            pltpu.SemaphoreType.DMA((2 + X,)),
            pltpu.SemaphoreType.DMA((11,)),
            pltpu.SemaphoreType.DMA((11,)),
            pltpu.SemaphoreType.DMA((8,)),
            pltpu.SemaphoreType.DMA((8,)),
            pltpu.SemaphoreType.DMA((2,)),
            pltpu.SemaphoreType.DMA((2,)),
            pltpu.SemaphoreType.REGULAR,
        ],
        compiler_params=pltpu.CompilerParams(
            collective_id=0, has_side_effects=True, vmem_limit_bytes=40 * 1024 * 1024
        ),
    )(*(pltpu.with_memory_space_constraint(a, pltpu.HBM) for a in (density, modes)))


def solution(mesh):
    return jax.shard_map(
        local,
        mesh=mesh,
        in_specs=(P("gx", "gy", None), P(None, "gx", "gy", None)),
        out_specs=P(None, "gx", "gy", None),
        check_vma=False,
    )
```
